128 devices in a mesh: band: 4 (over y), row: 32 (over x, z, core).
Axes of the slice: x: 4, y: 4, z: 4, core: 2. Of those that a mesh axis runs over, the one named last changes fastest.
Arguments:
- amplitude: bfloat16 [2048, 8192], P('row'), may hold values from 0.5 to 1.5
- seg_map: int32 [2048, 8192], P('row'), may hold values from 0 to 1199, as said below
- seg_box: int32 [4, 1200], replicated, may hold values from 0 to 8191, as said below
- seg_coeffs: float32 [3, 1200], replicated, may hold values from -1 to 1
- probe_freq: int32 [2, 2], replicated, may hold values from 3 to 23
- probe_amp: float32 [2], replicated, may hold values from 0.3 to 0.8
- measured: float32 [8, 256, 4, 2, 256], P('band', 'row'), may hold values from -6 to 6
Outputs:
- gradient: float32 [3, 1200], replicated
The draws below stay inside these ranges and needn't reach their ends.
Inputs may be any that keep to these rules, and one draw needn't show every extreme that they name: `seg_map`: segments lie in 16 rows of rectangular tiles of whole pupil rows, 75 tiles side by side in each, alternate rows offset by half a tile; segment numbers rise by tile row, then by column; every segment has samples. `seg_box`: the bounds of each segment's samples in seg_map, rows first.
All inputs are finite; a program needn't handle non-finite values.
Results may differ from the reference program's by a relative error of at most 0.0015.
Values may be sent and summed in bfloat16 or wider, within the bound.
A program may use at most 192 MiB of HBM per device.

```python
import math
import jax
import jax.numpy as jnp
from jax import lax

NC = 8192
NR = 2048
M = 256
BANDS = 8
PAIRS = 2
PROBES = 4
SEG = 1200
SROWS = 16


def segment_layout(key):
    key = jax.random.fold_in(key, 11)
    key_rows, key_cols = jax.random.split(key)
    per_row = SEG // SROWS
    step_rows = NR // SROWS
    jitter_rows = step_rows // 4
    inner_rows = jnp.arange(1, SROWS, dtype=jnp.int32) * step_rows + jax.random.randint(key_rows, (SROWS - 1,), -jitter_rows, jitter_rows + 1, dtype=jnp.int32)
    row_edges = jnp.concatenate([jnp.zeros((1,), jnp.int32), inner_rows, jnp.full((1,), NR, jnp.int32)])
    width = NC // per_row
    jitter_cols = width // 4
    offset = jnp.arange(SROWS, dtype=jnp.int32) % 2 * (width // 2)
    inner_cols = jnp.arange(1, per_row, dtype=jnp.int32)[None, :] * width + offset[:, None] + jax.random.randint(key_cols, (SROWS, per_row - 1), -jitter_cols, jitter_cols + 1, dtype=jnp.int32)
    col_edges = jnp.concatenate([jnp.zeros((SROWS, 1), jnp.int32), inner_cols, jnp.full((SROWS, 1), NC, jnp.int32)], axis=1)
    rows_all = jnp.arange(NR, dtype=jnp.int32)
    tile_row = jnp.sum((rows_all[:, None] >= inner_rows[None, :]).astype(jnp.int32), axis=1)
    cols_all = jnp.arange(NC, dtype=jnp.int32)
    count_table = jnp.sum((cols_all[None, :, None] >= inner_cols[:, None, :]).astype(jnp.int32), axis=2)
    seg_map = tile_row[:, None] * per_row + jnp.take(count_table, tile_row, axis=0)
    box = jnp.stack([jnp.repeat(row_edges[:-1], per_row), jnp.repeat(row_edges[1:] - 1, per_row), col_edges[:, :-1].reshape(-1), (col_edges[:, 1:] - 1).reshape(-1)])
    return (seg_map.astype(jnp.int32), box.astype(jnp.int32))


def draw_seg_map(key, part):
    return segment_layout(key)[0]


def draw_seg_box(key, part):
    return segment_layout(key)[1]


def place_ends(array, rng, low, top_value):
    spot = [jax.random.randint(jax.random.fold_in(rng, axis), (), 0, length) for axis, length in enumerate(array.shape)]
    widest = array.shape.index(max(array.shape))
    neighbour = spot[:widest] + [(spot[widest] + 1) % array.shape[widest]] + spot[widest + 1:]
    return array.at[tuple(spot)].set(low).at[tuple(neighbour)].set(top_value)


def steps_of(own_key, dims, cuts, least, top_value):
    gain = 1.0
    for position, parts in cuts:
        heights = jax.random.uniform(jax.random.fold_in(jax.random.fold_in(own_key, 6), position), (parts,), jnp.float32, least / len(cuts), top_value / len(cuts))
        gain = gain * jnp.repeat(jnp.exp(heights), dims[position] // parts).reshape((-1,) + (1,) * (len(dims) - 1 - position))
    return gain


def bell_draw(own_key, shape, scale, reach, cuts=(), kind=jnp.bfloat16):
    values = jax.random.normal(own_key, shape, jnp.float32) * scale
    if len(cuts) > 0:
        values = steps_of(own_key, shape, cuts, -0.22, 0.18) * values
    return jnp.clip(values, min=-reach, max=reach).astype(kind)


def setup_inputs(seed: int = 0) -> dict:
    key_of = jax.random.split(jax.random.key(seed), 8)
    amplitude = jnp.clip(0.5 + 1.0 * jax.random.uniform(key_of[0], (NR, NC), jnp.float32) ** steps_of(key_of[0], (NR, NC), ((0, 32),), -0.2, 0.2), 0.5, 1.5).astype(jnp.bfloat16)
    seg_map = draw_seg_map(jax.random.fold_in(key_of[7], 71), 0)
    seg_box = draw_seg_box(jax.random.fold_in(key_of[7], 71), 0)
    seg_coeffs = jnp.clip(jax.random.uniform(key_of[3], (3, SEG), jnp.float32, -1.0, 1.0), -1.0, 1.0)
    probe_freq = place_ends(jax.random.randint(key_of[4], (PAIRS, 2), 3, 24), jax.random.fold_in(key_of[4], 1), 3, 23).astype(jnp.int32)
    probe_amp = jnp.clip(jax.random.uniform(key_of[5], (PAIRS,), jnp.float32, 0.3, 0.8), 0.3, 0.8)
    measured = bell_draw(key_of[6], (BANDS, M, PROBES, 2, M), 1.0, 6.0, ((0, 4), (1, 32)), jnp.float32)
    return dict(amplitude=amplitude, seg_map=seg_map, seg_box=seg_box, seg_coeffs=seg_coeffs, probe_freq=probe_freq, probe_amp=probe_amp, measured=measured)


TWO_PI = 2.0 * math.pi
SAMPLING = 0.5
SPREAD = 0.2

def wave_tables(coords, band, count):
    ratio = 1.0 + SPREAD * ((band + 0.5) / BANDS - 0.5)
    focal = (jnp.arange(count, dtype=jnp.float32) - count / 2 + 0.5) * SAMPLING
    angle = TWO_PI * focal[:, None] * coords[None, :] / ratio
    return jnp.stack([jnp.cos(angle), jnp.sin(angle)]).astype(jnp.bfloat16)

def column_coords():
    return (jnp.arange(NC, dtype=jnp.float32) + 0.5) / NC - 0.5

def row_coords(rows_global, total_rows):
    return (rows_global.astype(jnp.float32) + 0.5) / NC - total_rows / (2.0 * NC)

def segment_basis(seg_map, seg_box, seg_coeffs, rows_global):
    bounds = seg_box.astype(jnp.float32)
    middle_row = 0.5 * (bounds[0] + bounds[1])
    half_row = 0.5 * (bounds[1] - bounds[0] + 1.0)
    middle_col = 0.5 * (bounds[2] + bounds[3])
    half_col = 0.5 * (bounds[3] - bounds[2] + 1.0)
    columns = jnp.arange(NC, dtype=jnp.float32)
    across = (columns[None, :] - jnp.take(middle_col, seg_map)) / jnp.take(half_col, seg_map)
    down = (rows_global.astype(jnp.float32)[:, None] - jnp.take(middle_row, seg_map)) / jnp.take(half_row, seg_map)
    phase = jnp.take(seg_coeffs[0], seg_map) + jnp.take(seg_coeffs[1], seg_map) * across + jnp.take(seg_coeffs[2], seg_map) * down
    return (phase, across, down)

def probe_waves(probe_freq, probe_amp, rows_global, total_rows):
    freq = probe_freq.astype(jnp.float32)
    columns = column_coords()
    rows_here = row_coords(rows_global, total_rows)
    angle = TWO_PI * (freq[:, 0, None, None] * columns[None, None, :] + freq[:, 1, None, None] * rows_here[None, :, None])
    waves = probe_amp[:, None, None] * jnp.sin(angle)
    return jnp.stack([waves, -waves], axis=1).reshape(2 * PAIRS, rows_here.shape[0], NC)

def reference(amplitude, seg_map, seg_box, seg_coeffs, probe_freq, probe_amp, measured):
    rows_global = jnp.arange(NR, dtype=jnp.int32)
    normf = 1.0 / math.sqrt(NR * NC)
    phase, across, down = segment_basis(seg_map, seg_box, seg_coeffs, rows_global)
    waves = probe_waves(probe_freq, probe_amp, rows_global, NR)
    magnitude = amplitude.astype(jnp.float32)
    row_values = row_coords(rows_global, NR)

    def band_step(accum, inputs):
        band_index, measured_band = inputs
        band = band_index.astype(jnp.float32)
        pupil_table = wave_tables(column_coords(), band, M)
        row_table = wave_tables(row_values, band, M)

        def probe_step(inner, probe_inputs):
            wave, measured_probe = probe_inputs
            total_phase = phase + wave
            field_real = magnitude * jnp.cos(total_phase)
            field_imag = magnitude * jnp.sin(total_phase)
            field_low = jnp.stack([field_real, field_imag]).astype(jnp.bfloat16).reshape(2 * NR, NC)
            section_one = jnp.dot(field_low, pupil_table.reshape(2 * M, NC).T, preferred_element_type=jnp.float32).reshape(2, NR, 2, M)
            y_real = section_one[0, :, 0] + section_one[1, :, 1]
            y_imag = section_one[1, :, 0] - section_one[0, :, 1]
            half_way = jnp.stack([y_real, y_imag]).astype(jnp.bfloat16)
            section_two = jnp.dot(half_way.transpose(2, 0, 1).reshape(2 * M, NR), row_table.reshape(2 * M, NR).T, preferred_element_type=jnp.float32).reshape(M, 2, 2, M)
            f_real = section_two[:, 0, 0] + section_two[:, 1, 1]
            f_imag = section_two[:, 1, 0] - section_two[:, 0, 1]
            focal = jnp.stack([f_real, f_imag], axis=1) * normf
            residual = (focal - measured_probe).astype(jnp.bfloat16)
            back_two = jnp.dot(residual.reshape(2 * M, M), row_table.transpose(1, 0, 2).reshape(M, 2 * NR), preferred_element_type=jnp.float32).reshape(M, 2, 2, NR)
            h_real = back_two[:, 0, 0] - back_two[:, 1, 1]
            h_imag = back_two[:, 1, 0] + back_two[:, 0, 1]
            hidden_side = jnp.stack([h_real, h_imag], axis=1).astype(jnp.bfloat16)
            back_one = jnp.dot(hidden_side.reshape(M, 2 * NR).T, pupil_table.transpose(1, 0, 2).reshape(M, 2 * NC), preferred_element_type=jnp.float32).reshape(2, NR, 2, NC)
            g_real = back_one[0, :, 0] - back_one[1, :, 1]
            g_imag = back_one[1, :, 0] + back_one[0, :, 1]
            return (inner + (g_imag * field_real - g_real * field_imag), None)
        result, unused = lax.scan(probe_step, accum, (waves, measured_band.transpose(1, 0, 2, 3)))
        return (result, None)
    start = jnp.zeros((NR, NC), jnp.float32)
    weight, unused = lax.scan(band_step, start, (jnp.arange(BANDS, dtype=jnp.int32), measured))
    weight = weight * (2.0 * normf / (BANDS * PROBES))
    flat_ids = seg_map.reshape(-1)
    sums = [jax.ops.segment_sum(term.reshape(-1), flat_ids, num_segments=SEG) for term in (weight, weight * across, weight * down)]
    return jnp.stack(sums)
```

```python
import functools
import math

import jax
import jax.numpy as jnp
import ml_dtypes
import numpy as np
from jax import lax
from jax.experimental import pallas as pl
from jax.experimental.pallas import tpu as pltpu
from jax.sharding import PartitionSpec as P

NC = 8192
NR = 2048
M = 256
BANDS = 8
PROBES = 4
SEG = 1200
SROWS = 16
PER_ROW = SEG // SROWS
HALF = M // 2
ROWS = 64
PEERS = 32
OWN = 8
SPREAD = 0.2
SAMPLING = 0.5
MESH = pl.DeviceIdType.MESH
F32 = jnp.float32
BF16 = jnp.bfloat16
CB = 1024
NT = (((1,), (1,)), ((), ()))


def series(fn, top, count):
    cheb = np.polynomial.chebyshev.Chebyshev.interpolate(
        lambda s: fn(np.sqrt(s)), count - 1, domain=[0.0, top * top]
    )
    return [float(v) for v in cheb.convert(kind=np.polynomial.Polynomial).coef]


def sinc(x):
    return np.sinc(x / np.pi)


SIN_PHASE = series(sinc, 3.02, 6)
COS_PHASE = series(np.cos, 3.02, 7)
SIN_WAVE = series(sinc, 0.81, 4)
COS_WAVE = series(np.cos, 0.81, 4)
SIN_TURN = series(lambda x: 2 * np.pi * np.sinc(2 * x), 0.5, 8)
COS_TURN = series(lambda x: np.cos(2 * np.pi * x), 0.5, 8)


def poly(coefs, s):
    total = jnp.full_like(s, coefs[-1])
    for value in coefs[-2::-1]:
        total = total * s + value
    return total


def turn_sincos(turns):
    part = turns - jnp.floor(turns + 0.5)
    square = part * part
    return part * poly(SIN_TURN, square), poly(COS_TURN, square)


def half_tables(coords, order):
    focal = (np.arange(HALF, dtype=np.float32) - np.float32(M / 2) + np.float32(0.5)) * np.float32(SAMPLING)
    base = (np.float32(2.0 * math.pi) * focal)[:, None] * coords[None, :]
    out = []
    for band in range(BANDS):
        ratio = np.float32(1.0) + np.float32(SPREAD) * (
            (np.float32(band) + np.float32(0.5)) / np.float32(BANDS) - np.float32(0.5)
        )
        angle = (base / ratio).astype(np.float64)
        out.append(np.stack([np.cos(angle), np.sin(angle)]).astype(np.float32).astype(ml_dtypes.bfloat16))
    return np.stack(out)


def column_table():
    coords = (np.arange(NC, dtype=np.float32) + np.float32(0.5)) / np.float32(NC) - np.float32(0.5)
    return half_tables(coords, 0).reshape(4, 4 * HALF, NC)


def row_table():
    coords = (np.arange(NR, dtype=np.float32) + np.float32(0.5)) / np.float32(NC) - np.float32(NR / (2.0 * NC))
    return half_tables(coords, 0).reshape(4, 4 * HALF, NR)


def lane_sign(first, second):
    lane = lax.broadcasted_iota(jnp.int32, (1, 128), 1)
    return jnp.where(lane < 64, F32(first), F32(second))


def iota(shape, dim):
    return lax.broadcasted_iota(jnp.int32, shape, dim)


def tile_row_of(column):
    total = jnp.zeros((ROWS, 1), jnp.int32)
    for m in range(1, SROWS):
        total = total + (column >= PER_ROW * m).astype(jnp.int32)
    return total


def pick_rows(trow, tab_ref, which):
    value = jnp.zeros((ROWS, 128), F32)
    for t in range(SROWS):
        value = jnp.where(trow == t, tab_ref[which, t : t + 1, :], value)
    return value


def wave_setup(where_ref, freq_ref, amp_ref, roww, colw):
    row0 = where_ref[1] * ROWS
    rows = (iota((ROWS, 128), 0) + row0).astype(F32)
    place = (rows + 0.5) / NC - NR / (2.0 * NC)
    cols = (iota((NC // 128, 128), 0) * 128 + iota((NC // 128, 128), 1)).astype(F32)
    across = (cols + 0.5) / NC - 0.5
    for j in range(2):
        s, c = turn_sincos(place * freq_ref[j, 1].astype(F32))
        roww[2 * j] = s * amp_ref[j]
        roww[2 * j + 1] = c * amp_ref[j]
        s, c = turn_sincos(across * freq_ref[j, 0].astype(F32))
        colw[2 * j] = s
        colw[2 * j + 1] = c


def wave_sincos(j, rows, tile, roww, colw):
    col_sin = colw[2 * j, pl.ds(tile, 1), :]
    col_cos = colw[2 * j + 1, pl.ds(tile, 1), :]
    wave = roww[2 * j + 1, rows, :] * col_sin + roww[2 * j, rows, :] * col_cos
    square = wave * wave
    return wave * poly(SIN_WAVE, square), poly(COS_WAVE, square)


def forward_kernel(where_ref, amp_ref, seg_ref, tab_ref, freq_ref, pamp_ref, table_ref,
                   pay_ref, p_ref, acc, rowt, base, roww, colw, ebuf, ysc):
    step = pl.program_id(0)

    @pl.when(step == 0)
    def _():
        trow = tile_row_of(seg_ref[:, 0:1])
        trow = jnp.broadcast_to(trow, (ROWS, 128))
        base[...] = trow * PER_ROW
        r0 = pick_rows(trow, tab_ref, 0)
        r1 = pick_rows(trow, tab_ref, 1)
        c0 = pick_rows(trow, tab_ref, 2)
        c1 = pick_rows(trow, tab_ref, 3)
        rows = (iota((ROWS, 128), 0) + where_ref[1] * ROWS).astype(F32)
        down = (rows - 0.5 * (r0 + r1)) / (0.5 * (r1 - r0 + 1.0))
        rowt[0] = pick_rows(trow, tab_ref, 4) + pick_rows(trow, tab_ref, 6) * down
        rowt[1] = pick_rows(trow, tab_ref, 5) / (0.5 * (c1 - c0 + 1.0))
        rowt[2] = 0.5 * (c0 + c1)
        wave_setup(where_ref, freq_ref, pamp_ref, roww, colw)
        acc[...] = jnp.zeros_like(acc)

    lane = iota((32, 128), 1)
    for lt in range(CB // 128):
        tile = step * (CB // 128) + lt
        cols = slice(128 * lt, 128 * lt + 128)
        cf = (lane + tile * 128).astype(F32)
        for rh in range(2):
            rows = slice(32 * rh, 32 * rh + 32)
            idx = seg_ref[rows, cols] - base[rows, :]
            a = jnp.take_along_axis(rowt[0, rows, :], idx, axis=1)
            b = jnp.take_along_axis(rowt[1, rows, :], idx, axis=1)
            m = jnp.take_along_axis(rowt[2, rows, :], idx, axis=1)
            phase = a + b * (cf - m)
            square = phase * phase
            mag = amp_ref[rows, cols].astype(F32)
            pr = mag * poly(COS_PHASE, square)
            pi = mag * (phase * poly(SIN_PHASE, square))
            p_ref[0, rows, cols] = pr
            p_ref[1, rows, cols] = pi
            for j in range(2):
                sw, cw = wave_sincos(j, rows, tile, roww, colw)
                for t, f in ((0, cw), (1, sw)):
                    at = 256 * j + 128 * t + 32 * rh
                    ebuf[at : at + 32, cols] = (pr * f).astype(BF16)
                    ebuf[at + 64 : at + 96, cols] = (pi * f).astype(BF16)
    acc[...] += lax.dot_general(table_ref[0], ebuf[...], NT, preferred_element_type=F32)

    @pl.when(step == pl.num_programs(0) - 1)
    def _():
        plus = lane_sign(1.0, -1.0)
        for b in range(2):
            for j in range(2):
                parts = []
                for t in range(2):
                    cols = slice(256 * j + 128 * t, 256 * j + 128 * t + 128)
                    c = acc[256 * b : 256 * b + 128, cols]
                    s = plus * pltpu.roll(acc[256 * b + 128 : 256 * b + 256, cols], 64, 1)
                    parts.append((c + s, c - s))
                for side in range(2):
                    even = parts[0][side]
                    odd = plus * pltpu.roll(parts[1][side], 64, 1)
                    ysc[side, b, :, 256 * j : 256 * j + 128] = even - odd
                    ysc[side, b, :, 256 * j + 128 : 256 * j + 256] = even + odd
        for d in range(PEERS // 2):
            for side in range(2):
                to = d if side == 0 else PEERS - 1 - d
                pay_ref[to] = jnp.concatenate(
                    [ysc[side, b, OWN * d : OWN * d + OWN, :] for b in range(2)], axis=0
                ).astype(BF16)


def exchange(count, send, dst, me, band, ssem, rsem):
    def one(o, carry):
        peer = lax.rem(me + o, count)
        pltpu.make_async_remote_copy(
            src_ref=send.at[peer], dst_ref=dst.at[me], send_sem=ssem.at[peer], recv_sem=rsem.at[me],
            device_id=(band, peer), device_id_type=MESH).start()
        return carry
    lax.fori_loop(1, count, one, 0)


def exchange_wait(count, send, dst, me, band, ssem, rsem):
    def one(o, carry):
        peer = lax.rem(me + o, count)
        pltpu.make_async_remote_copy(
            src_ref=send.at[peer], dst_ref=dst.at[peer], send_sem=ssem.at[peer], recv_sem=rsem.at[peer],
            device_id=(band, peer), device_id_type=MESH).wait()
        return carry
    lax.fori_loop(1, count, one, 0)


def focal_kernel(normf, pay_ref, meas_ref, table_hbm, out_ref, table, recv, hpay, lhs, hs, ms, tsem, osem,
                 ssem, rsem, ssem2, rsem2):
    band = lax.axis_index("band")
    me = lax.axis_index("row")
    fetch = pltpu.make_async_copy(table_hbm.at[band], table, tsem)
    fetch.start()
    barrier = pltpu.get_barrier_semaphore()

    def greet(o, carry):
        pl.semaphore_signal(barrier, inc=1, device_id=(band, lax.rem(me + o, PEERS)), device_id_type=MESH)
        return carry
    lax.fori_loop(1, PEERS, greet, 0)
    pl.semaphore_wait(barrier, PEERS - 1)

    exchange(PEERS, pay_ref, recv, me, band, ssem, rsem)
    own = pltpu.make_async_copy(pay_ref.at[me], recv.at[me], osem.at[0])
    own.start()

    flip = (iota((128, 128), 0) + iota((128, 128), 1) == 127).astype(F32)
    for b in range(2):
        for v in range(OWN):
            source = jnp.where(me < PEERS // 2, v, OWN - 1 - v)
            at = b * 64 + 8 * v
            from_rows = pl.ds(pl.multiple_of(b * 64 + 8 * source, 8), 8)
            ms[0, at : at + 8, :] = meas_ref[from_rows, :HALF]
            ms[1, at : at + 8, :] = meas_ref[from_rows, HALF:]
    ms[1] = jnp.dot(ms[1], flip, precision=lax.Precision.HIGHEST, preferred_element_type=F32)

    own.wait()
    exchange_wait(PEERS, pay_ref, recv, me, band, ssem, rsem)
    fetch.wait()

    low = iota((16, 128), 1) < 64

    def gather(s, carry):
        cols = pl.ds(pl.multiple_of(s * 128, 128), 128)
        for q in range(4):
            one = recv[2 * s, :, 128 * q : 128 * q + 128].astype(F32)
            two = recv[2 * s + 1, :, 128 * q : 128 * q + 128].astype(F32)
            re = jnp.where(low, one, pltpu.roll(two, 64, 1))
            im = jnp.where(low, pltpu.roll(one, 64, 1), two)
            for b in range(2):
                lhs[b, 16 * q : 16 * q + 8, cols] = re[8 * b : 8 * b + 8]
                lhs[b, 16 * q + 8 : 16 * q + 16, cols] = im[8 * b : 8 * b + 8]
        return carry
    lax.fori_loop(0, PEERS // 2, gather, 0)

    for b in range(2):
        here = table[256 * b : 256 * b + 256, :]
        parts = lax.dot_general(lhs[b].astype(BF16), here, NT, preferred_element_type=F32)
        rows = []
        for q in range(4):
            re, im = parts[16 * q : 16 * q + 8], parts[16 * q + 8 : 16 * q + 16]
            pieces = []
            for o, (c, s) in enumerate(((re[:, :HALF], im[:, HALF:]), (im[:, :HALF], -re[:, HALF:]))):
                want = pl.ds(b * 64 + 2 * q + o, 8, stride=8)
                one = (c + s) * normf - ms[0, want, :]
                two = (c - s) * normf - ms[1, want, :]
                pieces.append((one + two, one - two))
            (re_e, re_o), (im_e, im_o) = pieces
            rows.append(jnp.concatenate([re_e, -im_o], axis=1))
            rows.append(jnp.concatenate([im_e, re_o], axis=1))
        left = jnp.concatenate(rows, axis=0).astype(BF16)
        hs[b] = jnp.dot(left, here, preferred_element_type=F32)

    low8 = iota((8, 128), 1) < 64

    def spread(s, carry):
        cols = pl.ds(pl.multiple_of(s * 128, 128), 128)
        for q in range(4):
            first, second = [], []
            for b in range(2):
                re = hs[b, 16 * q : 16 * q + 8, cols]
                im = hs[b, 16 * q + 8 : 16 * q + 16, cols]
                first.append(jnp.where(low8, re, pltpu.roll(im, 64, 1)))
                second.append(jnp.where(low8, pltpu.roll(re, 64, 1), im))
            hpay[2 * s, :, 128 * q : 128 * q + 128] = jnp.concatenate(first, axis=0).astype(BF16)
            hpay[2 * s + 1, :, 128 * q : 128 * q + 128] = jnp.concatenate(second, axis=0).astype(BF16)
        return carry
    lax.fori_loop(0, PEERS // 2, spread, 0)

    exchange(PEERS, hpay, out_ref, me, band, ssem2, rsem2)
    back = pltpu.make_async_copy(hpay.at[me], out_ref.at[me], osem.at[1])
    back.start()
    back.wait()
    exchange_wait(PEERS, hpay, out_ref, me, band, ssem2, rsem2)


def backward_kernel(where_ref, seg_ref, hid_ref, tab_ref, box_ref, freq_ref, pamp_ref, p_ref, table_ref,
                    out_ref, left, leftt, gbuf, wbuf, downs, segc, roww, colw):
    step = pl.program_id(0)

    @pl.when(step == 0)
    def _():
        wave_setup(where_ref, freq_ref, pamp_ref, roww, colw)
        trow = jnp.broadcast_to(tile_row_of(seg_ref[:, 0:1]), (ROWS, 128))
        downs[0] = trow.astype(F32)
        r0 = pick_rows(trow, tab_ref, 0)
        r1 = pick_rows(trow, tab_ref, 1)
        rows = (iota((ROWS, 128), 0) + where_ref[1] * ROWS).astype(F32)
        downs[1] = jnp.broadcast_to(((rows - 0.5 * (r0 + r1)) / (0.5 * (r1 - r0 + 1.0)))[:, 0:1], (ROWS, 128))
        minus = lane_sign(-1.0, 1.0)
        for d in range(PEERS // 2):
            here = hid_ref[d].astype(F32)
            there = hid_ref[PEERS - 1 - d].astype(F32)
            even, odd = here + there, here - there
            for j in range(2):
                e = [even[:, 256 * j + 128 * t : 256 * j + 128 * t + 128] for t in range(2)]
                o = [odd[:, 256 * j + 128 * t : 256 * j + 128 * t + 128] for t in range(2)]
                for t in range(2):
                    cols = slice(256 * j + 128 * t, 256 * j + 128 * t + 128)
                    es = e[0] + e[1] if t == 0 else e[0] - e[1]
                    os = o[0] + o[1] if t == 0 else o[0] - o[1]
                    os = minus * pltpu.roll(os, 64, 1)
                    for b in range(2):
                        left[256 * b + 8 * d : 256 * b + 8 * d + 8, cols] = es[8 * b : 8 * b + 8]
                        left[256 * b + 128 + 8 * d : 256 * b + 136 + 8 * d, cols] = os[8 * b : 8 * b + 8]
        leftt[...] = left[...].T.astype(BF16)

    for lt in range(CB // 256):
        gbuf[...] = jnp.dot(leftt[...], table_ref[0, :, 256 * lt : 256 * lt + 256], preferred_element_type=F32)
        for lh in range(2):
            tile = step * (CB // 128) + 2 * lt + lh
            gc = slice(128 * lh, 128 * lh + 128)
            cols = slice(256 * lt + 128 * lh, 256 * lt + 128 * lh + 128)
            for rh in range(2):
                rows = slice(32 * rh, 32 * rh + 32)
                zr, zi = 0.0, 0.0
                for j in range(2):
                    sw, cw = wave_sincos(j, rows, tile, roww, colw)
                    g = [gbuf[256 * j + 64 * n + 32 * rh : 256 * j + 64 * n + 32 * rh + 32, gc] for n in range(4)]
                    zr = zr + cw * g[0] + sw * g[3]
                    zi = zi + cw * g[1] - sw * g[2]
                wbuf[tile, rows, :] = p_ref[0, rows, cols] * zi - p_ref[1, rows, cols] * zr

    @pl.when(step == pl.num_programs(0) - 1)
    def _():
        out_ref[...] = jnp.zeros_like(out_ref)
        first, last = where_ref[2], where_ref[3]
        seg_iota = iota((128, 128), 0)
        lane = iota((64, 128), 1) + iota((64, 128), 0) * 128

        def slot(t, carry):
            here = (downs[0] == t.astype(F32)).astype(F32)
            down = here * downs[1]

            def count(j, idx):
                return idx + (lane >= box_ref[2, t * PER_ROW + j]).astype(jnp.int32)
            idx = lax.fori_loop(1, PER_ROW, count, jnp.zeros((64, 128), jnp.int32))
            c0 = jnp.broadcast_to(tab_ref[2, pl.ds(t, 1), :], (64, 128))
            c1 = jnp.broadcast_to(tab_ref[3, pl.ds(t, 1), :], (64, 128))
            lo = jnp.take_along_axis(c0, idx, axis=1)
            hi = jnp.take_along_axis(c1, idx, axis=1)
            segc[0] = (lane.astype(F32) - 0.5 * (lo + hi)) / (0.5 * (hi - lo + 1.0))
            segc[1] = idx.astype(F32)

            def tile(i, total):
                w = wbuf[i]
                ws = jnp.sum(w * here, axis=0, keepdims=True)
                wd = jnp.sum(w * down, axis=0, keepdims=True)
                three = jnp.concatenate([ws, ws * segc[0, pl.ds(i, 1), :], wd, jnp.zeros((5, 128), F32)], axis=0)
                hi1 = three.astype(BF16)
                rest = three - hi1.astype(F32)
                hi2 = rest.astype(BF16)
                hi3 = (rest - hi2.astype(F32)).astype(BF16)
                hot = (seg_iota.astype(F32) == segc[1, pl.ds(i, 1), :]).astype(F32).astype(BF16)
                for part in (hi1, hi2, hi3):
                    total = total + lax.dot_general(part, hot, NT, preferred_element_type=F32)
                return total
            total = lax.fori_loop(0, NC // 128, tile, jnp.zeros((8, 128), F32))
            for q in range(3):
                out_ref[q, pl.ds(t, 1), :] = total[q : q + 1, :]
            return carry
        lax.fori_loop(first, last + 1, slot, 0)


def sum_kernel(scale, in_ref, out_ref, mine, got1, got2, ssem, rsem, ssem2, rsem2):
    band = lax.axis_index("band")
    me = lax.axis_index("row")
    core = lax.rem(me, 2)
    chip = me // 2
    near = band * 2 + core
    barrier = pltpu.get_barrier_semaphore()

    def near_id(o):
        peer = lax.rem(near + o, 8)
        return peer, (peer // 2, chip * 2 + lax.rem(peer, 2))

    def far_id(o):
        peer = lax.rem(chip + o, 16)
        return peer, (band, peer * 2 + core)

    def greet1(o, carry):
        pl.semaphore_signal(barrier, inc=1, device_id=near_id(o)[1], device_id_type=MESH)
        return carry

    def greet2(o, carry):
        pl.semaphore_signal(barrier, inc=1, device_id=far_id(o)[1], device_id_type=MESH)
        return carry
    lax.fori_loop(1, 8, greet1, 0)
    lax.fori_loop(1, 16, greet2, 0)
    pl.semaphore_wait(barrier, 22)

    def send1(o, carry):
        peer, where = near_id(o)
        pltpu.make_async_remote_copy(src_ref=in_ref, dst_ref=got1.at[near], send_sem=ssem.at[peer],
                                     recv_sem=rsem.at[near], device_id=where, device_id_type=MESH).start()
        return carry

    def wait1(o, carry):
        peer, where = near_id(o)
        pltpu.make_async_remote_copy(src_ref=in_ref, dst_ref=got1.at[peer], send_sem=ssem.at[peer],
                                     recv_sem=rsem.at[peer], device_id=where, device_id_type=MESH).wait()
        return carry
    lax.fori_loop(1, 8, send1, 0)
    got1[near] = in_ref[...]
    lax.fori_loop(1, 8, wait1, 0)
    total = got1[0]
    for i in range(1, 8):
        total = total + got1[i]
    mine[...] = total

    def send2(o, carry):
        peer, where = far_id(o)
        pltpu.make_async_remote_copy(src_ref=mine, dst_ref=got2.at[chip], send_sem=ssem2.at[peer],
                                     recv_sem=rsem2.at[chip], device_id=where, device_id_type=MESH).start()
        return carry

    def wait2(o, carry):
        peer, where = far_id(o)
        pltpu.make_async_remote_copy(src_ref=mine, dst_ref=got2.at[peer], send_sem=ssem2.at[peer],
                                     recv_sem=rsem2.at[peer], device_id=where, device_id_type=MESH).wait()
        return carry
    lax.fori_loop(1, 16, send2, 0)
    got2[chip] = mine[...]
    lax.fori_loop(1, 16, wait2, 0)
    total = got2[0]
    for i in range(1, 16):
        total = total + got2[i]
    out_ref[...] = total * scale


VM = pl.BlockSpec(memory_space=pltpu.VMEM)
SM = pl.BlockSpec(memory_space=pltpu.SMEM)
LIMIT = 60 * 1024 * 1024


def prelude(seg_map, seg_box, seg_coeffs):
    tabs = jnp.concatenate([seg_box.astype(F32), seg_coeffs], axis=0).reshape(7, SROWS, PER_ROW)
    tabs = jnp.pad(tabs, ((0, 0), (0, 0), (0, 128 - PER_ROW)))
    where = jnp.stack([lax.axis_index("band").astype(jnp.int32), lax.axis_index("row").astype(jnp.int32),
                       seg_map[0, 0] // PER_ROW, seg_map[ROWS - 1, 0] // PER_ROW])
    return tabs, where


def run_forward(where, amplitude, seg_map, tabs, probe_freq, probe_amp, ctable):
    return pl.pallas_call(
        forward_kernel,
        grid_spec=pltpu.PrefetchScalarGridSpec(
            num_scalar_prefetch=1,
            grid=(NC // CB,),
            in_specs=[
                pl.BlockSpec((ROWS, CB), lambda i, w: (0, i)),
                pl.BlockSpec((ROWS, CB), lambda i, w: (0, i)),
                VM, SM, SM,
                pl.BlockSpec((1, 512, CB), lambda i, w: (w[0], 0, i)),
            ],
            out_specs=[
                pl.BlockSpec((PEERS, 16, 512), lambda i, w: (0, 0, 0)),
                pl.BlockSpec((2, ROWS, CB), lambda i, w: (0, 0, i)),
            ],
            scratch_shapes=[
                pltpu.VMEM((512, 512), F32),
                pltpu.VMEM((3, ROWS, 128), F32),
                pltpu.VMEM((ROWS, 128), jnp.int32),
                pltpu.VMEM((4, ROWS, 128), F32),
                pltpu.VMEM((4, NC // 128, 128), F32),
                pltpu.VMEM((512, CB), BF16),
                pltpu.VMEM((2, 2, HALF, 512), F32),
            ],
        ),
        out_shape=[
            jax.ShapeDtypeStruct((PEERS, 16, 512), BF16),
            jax.ShapeDtypeStruct((2, ROWS, NC), F32),
        ],
        compiler_params=pltpu.CompilerParams(vmem_limit_bytes=LIMIT),
        name="fields_forward",
    )(where, amplitude, seg_map, tabs, probe_freq, probe_amp, ctable)


def run_focal(pay, meas, rtable):
    return pl.pallas_call(
        functools.partial(focal_kernel, 1.0 / math.sqrt(NR * NC)),
        in_specs=[VM, VM, pl.BlockSpec(memory_space=pl.ANY)],
        out_specs=VM,
        out_shape=jax.ShapeDtypeStruct((PEERS, 16, 512), BF16),
        scratch_shapes=[
            pltpu.VMEM((512, NR), BF16),
            pltpu.VMEM((PEERS, 16, 512), BF16),
            pltpu.VMEM((PEERS, 16, 512), BF16),
            pltpu.VMEM((2, 64, NR), F32),
            pltpu.VMEM((2, 64, NR), F32),
            pltpu.VMEM((2, 128, HALF), F32),
            pltpu.SemaphoreType.DMA,
            pltpu.SemaphoreType.DMA((2,)),
            pltpu.SemaphoreType.DMA((PEERS,)),
            pltpu.SemaphoreType.DMA((PEERS,)),
            pltpu.SemaphoreType.DMA((PEERS,)),
            pltpu.SemaphoreType.DMA((PEERS,)),
        ],
        compiler_params=pltpu.CompilerParams(collective_id=0, has_side_effects=True, vmem_limit_bytes=LIMIT),
        name="focal_exchange",
    )(pay, meas, rtable)


def run_backward(where, seg_map, hid, tabs, seg_box, probe_freq, probe_amp, pfield, ctable):
    return pl.pallas_call(
        backward_kernel,
        grid_spec=pltpu.PrefetchScalarGridSpec(
            num_scalar_prefetch=1,
            grid=(NC // CB,),
            in_specs=[
                pl.BlockSpec((ROWS, 128), lambda i, w: (0, 0)),
                VM, VM, SM, SM, SM,
                pl.BlockSpec((2, ROWS, CB), lambda i, w: (0, 0, i)),
                pl.BlockSpec((1, 512, CB), lambda i, w: (w[0], 0, i)),
            ],
            out_specs=pl.BlockSpec((3, SROWS, 128), lambda i, w: (0, 0, 0)),
            scratch_shapes=[
                pltpu.VMEM((512, 512), F32),
                pltpu.VMEM((512, 512), BF16),
                pltpu.VMEM((512, 256), F32),
                pltpu.VMEM((NC // 128, ROWS, 128), F32),
                pltpu.VMEM((2, ROWS, 128), F32),
                pltpu.VMEM((2, NC // 128, 128), F32),
                pltpu.VMEM((4, ROWS, 128), F32),
                pltpu.VMEM((4, NC // 128, 128), F32),
            ],
        ),
        out_shape=jax.ShapeDtypeStruct((3, SROWS, 128), F32),
        compiler_params=pltpu.CompilerParams(vmem_limit_bytes=LIMIT),
        name="backward_sums",
    )(where, seg_map, hid, tabs, seg_box, probe_freq, probe_amp, pfield, ctable)


def run_sum(sums):
    scale = 2.0 / math.sqrt(NR * NC) / (BANDS * PROBES)
    return pl.pallas_call(
        functools.partial(sum_kernel, scale),
        in_specs=[VM],
        out_specs=VM,
        out_shape=jax.ShapeDtypeStruct((3, SROWS, 128), F32),
        scratch_shapes=[
            pltpu.VMEM((3, SROWS, 128), F32),
            pltpu.VMEM((8, 3, SROWS, 128), F32),
            pltpu.VMEM((16, 3, SROWS, 128), F32),
            pltpu.SemaphoreType.DMA((8,)),
            pltpu.SemaphoreType.DMA((8,)),
            pltpu.SemaphoreType.DMA((16,)),
            pltpu.SemaphoreType.DMA((16,)),
        ],
        compiler_params=pltpu.CompilerParams(collective_id=1, has_side_effects=True),
        name="sum_all",
    )(sums)


def solution(mesh):
    ctable = jnp.asarray(column_table())
    rtable = jnp.asarray(row_table())

    def body(amplitude, seg_map, seg_box, seg_coeffs, probe_freq, probe_amp, measured):
        tabs, where = prelude(seg_map, seg_box, seg_coeffs)
        pay, pfield = run_forward(where, amplitude, seg_map, tabs, probe_freq, probe_amp, ctable)
        hid = run_focal(pay, measured.reshape(128, M), rtable)
        sums = run_backward(where, seg_map, hid, tabs, seg_box, probe_freq, probe_amp, pfield, ctable)
        return run_sum(sums)[:, :, :PER_ROW].reshape(3, SEG)

    in_specs = (P("row", None), P("row", None), P(), P(), P(), P(), P("band", "row", None, None, None))
    return jax.shard_map(body, mesh=mesh, in_specs=in_specs, out_specs=P(), check_vma=False)
```

```python
import functools
import math

import jax
import jax.numpy as jnp
import ml_dtypes
import numpy as np
from jax import lax
from jax.experimental import pallas as pl
from jax.experimental.pallas import tpu as pltpu
from jax.sharding import PartitionSpec as P

NC = 8192
NR = 2048
M = 256
BANDS = 8
PROBES = 4
SEG = 1200
SROWS = 16
PER_ROW = SEG // SROWS
HALF = M // 2
ROWS = 64
PEERS = 32
OWN = 8
SPREAD = 0.2
SAMPLING = 0.5
MESH = pl.DeviceIdType.MESH
F32 = jnp.float32
BF16 = jnp.bfloat16
SUB = 512
CHUNK = 1024
CHUNKS = NC // CHUNK
TILES = NC // 128
CHIPS = 16
YS = 4
NT = (((1,), (1,)), ((), ()))


def series(fn, top, count):
    cheb = np.polynomial.chebyshev.Chebyshev.interpolate(
        lambda s: fn(np.sqrt(s)), count - 1, domain=[0.0, top * top]
    )
    return [float(v) for v in cheb.convert(kind=np.polynomial.Polynomial).coef]


def sinc(x):
    return np.sinc(x / np.pi)


SIN_PHASE = series(sinc, 3.02, 6)
COS_PHASE = series(np.cos, 3.02, 7)
SIN_WAVE = series(sinc, 0.81, 4)
COS_WAVE = series(np.cos, 0.81, 4)
SIN_TURN = series(lambda x: 2 * np.pi * np.sinc(2 * x), 0.5, 8)
COS_TURN = series(lambda x: np.cos(2 * np.pi * x), 0.5, 8)


def poly(coefs, s):
    total = jnp.full_like(s, coefs[-1])
    for value in coefs[-2::-1]:
        total = total * s + value
    return total


def turn_sincos(turns):
    part = turns - jnp.floor(turns + 0.5)
    square = part * part
    return part * poly(SIN_TURN, square), poly(COS_TURN, square)


def half_tables(coords, order):
    focal = (np.arange(HALF, dtype=np.float32) - np.float32(M / 2) + np.float32(0.5)) * np.float32(SAMPLING)
    base = (np.float32(2.0 * math.pi) * focal)[:, None] * coords[None, :]
    out = []
    for band in range(BANDS):
        ratio = np.float32(1.0) + np.float32(SPREAD) * (
            (np.float32(band) + np.float32(0.5)) / np.float32(BANDS) - np.float32(0.5)
        )
        angle = (base / ratio).astype(np.float64)
        out.append(np.stack([np.cos(angle), np.sin(angle)]).astype(np.float32).astype(ml_dtypes.bfloat16))
    return np.stack(out)


def column_table():
    coords = (np.arange(NC, dtype=np.float32) + np.float32(0.5)) / np.float32(NC) - np.float32(0.5)
    return half_tables(coords, 0).reshape(4, 4 * HALF, NC)


def row_table():
    coords = (np.arange(NR, dtype=np.float32) + np.float32(0.5)) / np.float32(NC) - np.float32(NR / (2.0 * NC))
    return half_tables(coords, 0).reshape(4, 4 * HALF, NR)


def lane_sign(first, second):
    lane = lax.broadcasted_iota(jnp.int32, (1, 128), 1)
    return jnp.where(lane < 64, F32(first), F32(second))


def iota(shape, dim):
    return lax.broadcasted_iota(jnp.int32, shape, dim)


def wave_setup(row0, freq_ref, amp_ref, roww, colw):
    rows = (iota((ROWS, 128), 0) + row0).astype(F32)
    place = (rows + 0.5) / NC - NR / (2.0 * NC)
    cols = (iota((TILES, 128), 0) * 128 + iota((TILES, 128), 1)).astype(F32)
    across = (cols + 0.5) / NC - 0.5
    for j in range(2):
        s, c = turn_sincos(place * freq_ref[j, 1].astype(F32))
        roww[2 * j] = s * amp_ref[j]
        roww[2 * j + 1] = c * amp_ref[j]
        s, c = turn_sincos(across * freq_ref[j, 0].astype(F32))
        colw[2 * j] = s
        colw[2 * j + 1] = c


def wave_sincos(j, rows, tile, roww, colw):
    col_sin = colw[2 * j, pl.ds(tile, 1), :]
    col_cos = colw[2 * j + 1, pl.ds(tile, 1), :]
    wave = roww[2 * j + 1, rows, :] * col_sin + roww[2 * j, rows, :] * col_cos
    square = wave * wave
    return wave * poly(SIN_WAVE, square), poly(COS_WAVE, square)


def lanes(index, width):
    return pl.ds(pl.multiple_of(index * width, width), width)


def segment_setup(row0, box_ref, coef_ref, seg, flat, tabs, rowt, base, pick):
    flat[...] = jnp.zeros_like(flat)
    flat[0:4, 0:SEG] = box_ref[...].astype(F32)
    flat[4:7, 0:SEG] = coef_ref[...]
    lane = iota((8, 128), 1)
    for t in range(SROWS):
        first, off = divmod(PER_ROW * t, 128)
        one = flat[:, 128 * first : 128 * first + 128]
        if off:
            two = flat[:, 128 * first + 128 : 128 * first + 256]
            one = jnp.where(lane < 128 - off, pltpu.roll(one, 128 - off, 1), pltpu.roll(two, 128 - off, 1))
        tabs[t] = one
    column = seg[:, 0:1]
    trow = jnp.zeros((ROWS, 1), jnp.int32)
    for m in range(1, SROWS):
        trow = trow + (column >= PER_ROW * m).astype(jnp.int32)
    trow = jnp.broadcast_to(trow, (ROWS, 128))
    base[...] = trow * PER_ROW
    rows = (iota((ROWS, 128), 0) + row0).astype(F32)
    alpha, beta, middle, down_all = [jnp.zeros((ROWS, 128), F32) for _ in range(4)]
    for t in range(SROWS):
        r0, r1, c0, c1 = [tabs[t, q : q + 1, :] for q in range(4)]
        piston, tip, tilt = [tabs[t, q : q + 1, :] for q in range(4, 7)]
        here = trow == t
        down = (rows - 0.5 * (r0 + r1)) / (0.5 * (r1 - r0 + 1.0))
        alpha = jnp.where(here, piston + tilt * down, alpha)
        beta = jnp.where(here, tip / (0.5 * (c1 - c0 + 1.0)), beta)
        middle = jnp.where(here, 0.5 * (c0 + c1), middle)
        down_all = jnp.where(here, down, down_all)
    rowt[0] = alpha
    rowt[1] = beta
    rowt[2] = middle
    lane = iota((ROWS, 128), 1)
    down_all = jnp.broadcast_to(down_all[:, 0:1], (ROWS, 128))
    high = down_all.astype(BF16).astype(F32)
    which = jnp.where(lane < 16, 1.0, jnp.where(lane < 32, high, jnp.where(lane < 48, down_all - high, 0.0)))
    chosen = jnp.where(lax.rem(lane, 16) == trow, which, 0.0)
    pick[...] = jnp.concatenate([chosen, chosen], axis=0).T.astype(BF16)


def fields(j, chunk, ebuf, amp, seg, rowt, base, roww, colw, pbuf):
    for lt in range(SUB // 128):
        tile = chunk * (SUB // 128) + lt
        wide = lanes(tile, 128)
        cols = slice(128 * lt, 128 * lt + 128)
        cf = (iota((32, 128), 1) + tile * 128).astype(F32)
        for rh in range(2):
            rows = slice(32 * rh, 32 * rh + 32)
            if j == 0:
                idx = seg[rows, wide] - base[rows, :]
                a = jnp.take_along_axis(rowt[0, rows, :], idx, axis=1)
                b = jnp.take_along_axis(rowt[1, rows, :], idx, axis=1)
                m = jnp.take_along_axis(rowt[2, rows, :], idx, axis=1)
                phase = a + b * (cf - m)
                square = phase * phase
                mag = amp[rows, wide].astype(F32)
                pr = mag * poly(COS_PHASE, square)
                pi = mag * (phase * poly(SIN_PHASE, square))
                pbuf[0, rows, wide] = pr
                pbuf[1, rows, wide] = pi
            else:
                pr = pbuf[0, rows, wide]
                pi = pbuf[1, rows, wide]
            sw, cw = wave_sincos(j, rows, tile, roww, colw)
            for t, f in ((0, cw), (1, sw)):
                at = 128 * t + 32 * rh
                ebuf[at : at + 32, cols] = (pr * f).astype(BF16)
                ebuf[at + 64 : at + 96, cols] = (pi * f).astype(BF16)


def column_sums(acc, pay, ysc):
    plus = lane_sign(1.0, -1.0)
    for b in range(2):
        parts = []
        for t in range(2):
            cols = slice(128 * t, 128 * t + 128)
            c = acc[256 * b : 256 * b + 128, cols]
            s = plus * pltpu.roll(acc[256 * b + 128 : 256 * b + 256, cols], 64, 1)
            parts.append((c + s, c - s))
        for side in range(2):
            even = parts[0][side]
            odd = plus * pltpu.roll(parts[1][side], 64, 1)
            ysc[side, b, :, 0:128] = even - odd
            ysc[side, b, :, 128:256] = even + odd
    for d in range(PEERS // 2):
        for side in range(2):
            to = d if side == 0 else PEERS - 1 - d
            pay[to] = jnp.concatenate(
                [ysc[side, b, OWN * d : OWN * d + OWN, :] for b in range(2)], axis=0
            ).astype(BF16)


def focal_part(j, normf, recv, hpay, lhs, hs, ms, table):
    low = iota((16, 128), 1) < 64

    def gather(s4, carry):
        for k in range(4):
            s = s4 * 4 + k
            cols = lanes(s, 128)
            for q in range(2):
                one = recv[2 * s, :, 128 * q : 128 * q + 128].astype(F32)
                two = recv[2 * s + 1, :, 128 * q : 128 * q + 128].astype(F32)
                re = jnp.where(low, one, pltpu.roll(two, 64, 1))
                im = jnp.where(low, pltpu.roll(one, 64, 1), two)
                for b in range(2):
                    lhs[b, 16 * q : 16 * q + 8, cols] = re[8 * b : 8 * b + 8]
                    lhs[b, 16 * q + 8 : 16 * q + 16, cols] = im[8 * b : 8 * b + 8]
        return carry
    lax.fori_loop(0, PEERS // 8, gather, 0)

    for b in range(2):
        here = table[256 * b : 256 * b + 256, :]
        parts = lax.dot_general(lhs[b].astype(BF16), here, NT, preferred_element_type=F32)
        rows = []
        for q in range(2):
            re, im = parts[16 * q : 16 * q + 8], parts[16 * q + 8 : 16 * q + 16]
            pieces = []
            for o, (c, s) in enumerate(((re[:, :HALF], im[:, HALF:]), (im[:, :HALF], -re[:, HALF:]))):
                want = pl.ds(b * 64 + 4 * j + 2 * q + o, 8, stride=8)
                one = (c + s) * normf - ms[0, want, :]
                two = (c - s) * normf - ms[1, want, :]
                pieces.append((one + two, one - two))
            (re_e, re_o), (im_e, im_o) = pieces
            rows.append(jnp.concatenate([re_e, -im_o], axis=1))
            rows.append(jnp.concatenate([im_e, re_o], axis=1))
        left = jnp.concatenate(rows, axis=0).astype(BF16)
        hs[b] = jnp.dot(left, here, preferred_element_type=F32)

    low8 = iota((8, 128), 1) < 64

    def spread(s4, carry):
        for k in range(4):
            s = s4 * 4 + k
            cols = lanes(s, 128)
            for q in range(2):
                first, second = [], []
                for b in range(2):
                    re = hs[b, 16 * q : 16 * q + 8, cols]
                    im = hs[b, 16 * q + 8 : 16 * q + 16, cols]
                    first.append(jnp.where(low8, re, pltpu.roll(im, 64, 1)))
                    second.append(jnp.where(low8, pltpu.roll(re, 64, 1), im))
                hpay[2 * s, :, 128 * q : 128 * q + 128] = jnp.concatenate(first, axis=0).astype(BF16)
                hpay[2 * s + 1, :, 128 * q : 128 * q + 128] = jnp.concatenate(second, axis=0).astype(BF16)
        return carry
    lax.fori_loop(0, PEERS // 8, spread, 0)


def hidden_left(hid, left, leftt):
    minus = lane_sign(-1.0, 1.0)
    for d in range(PEERS // 2):
        here = hid[d].astype(F32)
        there = hid[PEERS - 1 - d].astype(F32)
        even, odd = here + there, here - there
        e = [even[:, 128 * t : 128 * t + 128] for t in range(2)]
        o = [odd[:, 128 * t : 128 * t + 128] for t in range(2)]
        for t in range(2):
            cols = slice(128 * t, 128 * t + 128)
            es = e[0] + e[1] if t == 0 else e[0] - e[1]
            os = o[0] + o[1] if t == 0 else o[0] - o[1]
            os = minus * pltpu.roll(os, 64, 1)
            for b in range(2):
                left[256 * b + 8 * d : 256 * b + 8 * d + 8, cols] = es[8 * b : 8 * b + 8]
                left[256 * b + 128 + 8 * d : 256 * b + 136 + 8 * d, cols] = os[8 * b : 8 * b + 8]
    leftt[...] = left[...].T.astype(BF16)


def backward(j, chunk, leftt, table, gbuf, roww, colw, pbuf, zbuf, wst, pick, ubuf):
    for lt in range(CHUNK // 256):
        piece = chunk * (CHUNK // 256) + lt
        gbuf[lt] = jnp.dot(leftt[...], table[:, lanes(piece, 256)], preferred_element_type=F32)
        for lh in range(2):
            tile = piece * 2 + lh
            wide = lanes(tile, 128)
            gc = slice(128 * lh, 128 * lh + 128)
            for rh in range(2):
                rows = slice(32 * rh, 32 * rh + 32)
                sw, cw = wave_sincos(j, rows, tile, roww, colw)
                g = [gbuf[lt, 64 * n + 32 * rh : 64 * n + 32 * rh + 32, gc] for n in range(4)]
                zr = cw * g[0] + sw * g[3]
                zi = cw * g[1] - sw * g[2]
                if j == 0:
                    zbuf[0, rows, wide] = zr
                    zbuf[1, rows, wide] = zi
                else:
                    zr = zr + zbuf[0, rows, wide]
                    zi = zi + zbuf[1, rows, wide]
                    w = pbuf[0, rows, wide] * zi - pbuf[1, rows, wide] * zr
                    high = w.astype(BF16)
                    wst[lt, 32 * rh : 32 * rh + 32, gc] = high
                    wst[lt, 64 + 32 * rh : 96 + 32 * rh, gc] = (w - high.astype(F32)).astype(BF16)
        if j == 1:
            u = jnp.dot(pick[0:48, :], wst[lt], preferred_element_type=F32)
            for lh in range(2):
                gc = slice(128 * lh, 128 * lh + 128)
                at = pl.ds(pl.multiple_of((piece * 2 + lh) * 32, 32), 32)
                ubuf[at, :] = jnp.concatenate([u[0:16, gc], u[16:32, gc] + u[32:48, gc]], axis=0)


def segment_sums(tabs, ubuf, pre, sbuf, pack):
    row, col = iota((256, 256), 0), iota((256, 256), 1)
    at = jnp.where(row < 128, row, row - 128)
    to = jnp.where(col < 128, col, col - 128)
    weight = jnp.where(col < 128, 1.0, at.astype(F32))
    tri = jnp.where(at <= to, weight, 0.0).astype(BF16)

    def prefix(k, carry):
        rows = pl.ds(pl.multiple_of(k * 256, 256), 256)
        u = ubuf[rows, :]
        high = u.astype(BF16)
        low = (u - high.astype(F32)).astype(BF16)
        both = jnp.dot(jnp.concatenate([high, low], axis=1), tri, preferred_element_type=F32)
        pre[0, rows, :] = both[:, :128]
        pre[1, rows, :] = both[:, 128:]
        return carry
    lax.fori_loop(0, TILES * 32 // 256, prefix, 0)

    tile = iota((TILES, 128), 0).astype(F32)
    last = jnp.full((TILES, 128), 127, jnp.int32)
    lane = iota((1, 128), 1)

    def slot(t, carry):
        c0 = tabs[t, 2:3, :]
        c1 = tabs[t, 3:4, :]
        tile0 = jnp.floor(c0 * (1.0 / 128.0))
        tile1 = jnp.floor(c1 * (1.0 / 128.0))
        in0 = c0 - 128.0 * tile0 - 1.0
        in1 = c1 - 128.0 * tile1
        idx0 = jnp.broadcast_to(jnp.maximum(in0, 0.0).astype(jnp.int32), (TILES, 128))
        idx1 = jnp.broadcast_to(in1.astype(jnp.int32), (TILES, 128))
        some = in0 >= 0.0
        diffs = []
        for half, at in ((0, t), (1, t), (0, t + 16)):
            a = pre[half, pl.ds(at, TILES, stride=32), :]
            whole = jnp.take_along_axis(a, last, axis=1)
            g1 = jnp.take_along_axis(a, idx1, axis=1)
            g0 = jnp.where(some, jnp.take_along_axis(a, idx0, axis=1), 0.0)
            upto1 = jnp.where(tile == tile1, g1, jnp.where(tile < tile1, whole, 0.0))
            upto0 = jnp.where(tile == tile0, g0, jnp.where(tile < tile0, whole, 0.0))
            diffs.append(upto1 - upto0)
        middle = 0.5 * (c0 + c1)
        half_width = 0.5 * (c1 - c0 + 1.0)
        slope = diffs[1] + (128.0 * tile - middle) * diffs[0]
        sums = [jnp.sum(diffs[0], axis=0, keepdims=True),
                jnp.sum(slope, axis=0, keepdims=True) / half_width,
                jnp.sum(diffs[2], axis=0, keepdims=True)]
        sbuf[t] = jnp.where(lane < PER_ROW, jnp.concatenate(sums + [jnp.zeros((5, 128), F32)], axis=0), 0.0)
        return carry
    lax.fori_loop(0, SROWS, slot, 0)

    packed = [jnp.zeros((8, 128), F32) for _ in range(10)]
    lane = iota((8, 128), 1)
    for t in range(SROWS):
        first, off = divmod(PER_ROW * t, 128)
        turned = pltpu.roll(sbuf[t], off, 1) if off else sbuf[t]
        packed[first] = packed[first] + jnp.where(lane >= off, turned, 0.0)
        if off + PER_ROW > 128:
            packed[first + 1] = packed[first + 1] + jnp.where(lane < off, turned, 0.0)
    for q in range(3):
        for k in range(10):
            p, r = divmod(q * 10 + k, 8)
            pack[p, r : r + 1, :] = packed[k][q : q + 1, :]
    pack[3, 6:8, :] = jnp.zeros((2, 128), F32)


def remote(src, dst, ssem, rsem, where):
    return pltpu.make_async_remote_copy(src_ref=src, dst_ref=dst, send_sem=ssem, recv_sem=rsem,
                                        device_id=where, device_id_type=MESH)


def each(count, fn):
    def step(o, carry):
        fn(o)
        return carry
    lax.fori_loop(1, count, step, 0)


def kernel(normf, scale, amp_hbm, seg_hbm, box_ref, coef_ref, freq_ref, pamp_ref, meas_ref, ctab_hbm, rtab_hbm,
           out_ref, amp, seg, ctab, rtab, flat, tabs, rowt, base, pick, roww, colw, pbuf, eb0, eb1, acc, ysc,
           pay, recv, lhs, hs, ms, hpay, hid, left, leftt, gbuf, zbuf, wst, ubuf, pre, sbuf, pack,
           got_a, mine_b, got_b, mine_c, got_c, lsem, tsem, osem, ssem, rsem, asem, bsem, csem):
    band = lax.axis_index("band")
    me = lax.axis_index("row")
    core = lax.rem(me, 2)
    chip = me // 2
    row0 = me * ROWS

    def loads(i):
        cols = lanes(i, CHUNK)
        return [pltpu.make_async_copy(seg_hbm.at[:, cols], seg.at[:, cols], lsem.at[0, i]),
                pltpu.make_async_copy(amp_hbm.at[:, cols], amp.at[:, cols], lsem.at[1, i]),
                pltpu.make_async_copy(ctab_hbm.at[band, :, cols], ctab.at[:, cols], lsem.at[2, i])]

    def start_loads(i, carry):
        for copy in loads(i):
            copy.start()
        return carry
    lax.fori_loop(0, CHUNKS, start_loads, 0)
    table_copy = pltpu.make_async_copy(rtab_hbm.at[band], rtab, tsem)
    table_copy.start()

    barrier = pltpu.get_barrier_semaphore()

    def greet(where):
        pl.semaphore_signal(barrier, inc=1, device_id=where, device_id_type=MESH)
    each(PEERS, lambda o: greet((band, lax.rem(me + o, PEERS))))
    for o in range(1, YS):
        for c in range(2):
            greet((lax.rem(band + o, YS), chip * 2 + c))

    wave_setup(row0, freq_ref, pamp_ref, roww, colw)
    for b in range(2):
        for v in range(OWN):
            source = jnp.where(me < PEERS // 2, v, OWN - 1 - v)
            for k in range(PROBES):
                at = b * 64 + 8 * v + 2 * k
                ms[0, at : at + 2, :] = meas_ref[b, source, k, :, :HALF]
                ms[1, at : at + 2, :] = meas_ref[b, source, k, :, HALF:]
    flip = (iota((128, 128), 0) + iota((128, 128), 1) == 127).astype(F32)
    ms[1] = jnp.dot(ms[1], flip, precision=lax.Precision.HIGHEST, preferred_element_type=F32)

    def send(j, source, target):
        def one(o):
            peer = lax.rem(me + o, PEERS)
            remote(source.at[j, peer], target.at[j, me], ssem.at[j, peer], rsem.at[j, me], (band, peer)).start()
        each(PEERS, one)

    def await_all(j, source, target):
        def one(o):
            peer = lax.rem(me + o, PEERS)
            remote(source.at[j, peer], target.at[j, peer], ssem.at[j, peer], rsem.at[j, peer], (band, peer)).wait()
        each(PEERS, one)

    for j in range(2):
        acc[...] = jnp.zeros_like(acc)
        eb1[...] = jnp.zeros_like(eb1)

        def forward(i, carry):
            if j == 0:
                for copy in loads(i):
                    copy.wait()

                @pl.when(i == 0)
                def _():
                    segment_setup(row0, box_ref, coef_ref, seg, flat, tabs, rowt, base, pick)
            before = jnp.maximum(2 * i - 1, 0)
            fields(j, 2 * i, eb0, amp, seg, rowt, base, roww, colw, pbuf)
            acc[...] += lax.dot_general(ctab[:, lanes(before, SUB)], eb1[...], NT, preferred_element_type=F32)
            fields(j, 2 * i + 1, eb1, amp, seg, rowt, base, roww, colw, pbuf)
            acc[...] += lax.dot_general(ctab[:, lanes(2 * i, SUB)], eb0[...], NT, preferred_element_type=F32)
            return carry
        lax.fori_loop(0, CHUNKS, forward, 0)
        acc[...] += lax.dot_general(ctab[:, NC - SUB : NC], eb1[...], NT, preferred_element_type=F32)
        column_sums(acc, pay.at[j], ysc)
        if j == 0:
            pl.semaphore_wait(barrier, PEERS - 1 + 2 * (YS - 1))
        send(j, pay, recv)
        recv[j, me] = pay[j, me]

    table_copy.wait()
    for j in range(2):
        await_all(j, pay, recv)
        focal_part(j, normf, recv.at[j], hpay.at[j], lhs, hs, ms, rtab)
        def one(o):
            peer = lax.rem(me + o, PEERS)
            remote(hpay.at[j, peer], hid.at[j, me], ssem.at[2 + j, peer], rsem.at[2 + j, me], (band, peer)).start()
        each(PEERS, one)
        hid[j, me] = hpay[j, me]

    for j in range(2):
        def done(o):
            peer = lax.rem(me + o, PEERS)
            remote(hpay.at[j, peer], hid.at[j, peer], ssem.at[2 + j, peer], rsem.at[2 + j, peer],
                   (band, peer)).wait()
        each(PEERS, done)
        hidden_left(hid.at[j], left, leftt)

        def back(i, carry):
            backward(j, i, leftt, ctab, gbuf, roww, colw, pbuf, zbuf, wst, pick, ubuf)
            return carry
        lax.fori_loop(0, CHUNKS, back, 0)

    segment_sums(tabs, ubuf, pre, sbuf, pack)

    near = band * 2 + core

    def near_copy(o, slot):
        peer = lax.rem(near + o, 2 * YS)
        to = peer // 2
        at = near if slot == "mine" else peer
        return remote(pack.at[to], got_a.at[at], asem.at[0, peer], asem.at[1, at],
                      (to, chip * 2 + lax.rem(peer, 2)))
    each(2 * YS, lambda o: near_copy(o, "mine").start())
    got_a[near] = pack[band]
    each(2 * YS, lambda o: near_copy(o, "peer").wait())
    total = got_a[0]
    for k in range(1, 2 * YS):
        total = total + got_a[k]
    mine_b[...] = total

    def far_copy(o, slot):
        peer = lax.rem(chip + o, CHIPS)
        at = chip if slot == "mine" else peer
        return remote(mine_b, got_b.at[at], bsem.at[0, peer], bsem.at[1, at], (band, peer * 2 + core))
    each(CHIPS, lambda o: far_copy(o, "mine").start())
    got_b[chip] = mine_b[...]
    each(CHIPS, lambda o: far_copy(o, "peer").wait())
    total = got_b[0]
    for k in range(1, CHIPS):
        total = total + got_b[k]
    mine_c[...] = total * scale

    def share_copy(o, slot):
        peer = lax.rem(band + o, YS)
        at = band if slot == "mine" else peer
        return remote(mine_c, got_c.at[at], csem.at[0, peer], csem.at[1, at], (peer, me))
    each(YS, lambda o: share_copy(o, "mine").start())
    got_c[band] = mine_c[...]
    each(YS, lambda o: share_copy(o, "peer").wait())
    for q in range(3):
        for k in range(10):
            p, r = divmod(q * 10 + k, 8)
            width = min(128, SEG - 128 * k)
            out_ref[q : q + 1, 128 * k : 128 * k + width] = got_c[p, r : r + 1, :width]


VM = pl.BlockSpec(memory_space=pltpu.VMEM)
SM = pl.BlockSpec(memory_space=pltpu.SMEM)
HBM = pl.BlockSpec(memory_space=pl.ANY)
LIMIT = 60 * 1024 * 1024


def solution(mesh):
    ctable = jnp.asarray(column_table())
    rtable = jnp.asarray(row_table())
    root = math.sqrt(NR * NC)

    def body(amplitude, seg_map, seg_box, seg_coeffs, probe_freq, probe_amp, measured):
        dma = pltpu.SemaphoreType.DMA
        return pl.pallas_call(
            functools.partial(kernel, 1.0 / root, 2.0 / root / (BANDS * PROBES)),
            in_specs=[HBM, HBM, VM, VM, SM, SM, VM, HBM, HBM],
            out_specs=VM,
            out_shape=jax.ShapeDtypeStruct((3, SEG), F32),
            scratch_shapes=[
                pltpu.VMEM((ROWS, NC), BF16),
                pltpu.VMEM((ROWS, NC), jnp.int32),
                pltpu.VMEM((4 * HALF, NC), BF16),
                pltpu.VMEM((4 * HALF, NR), BF16),
                pltpu.VMEM((8, 1280), F32),
                pltpu.VMEM((SROWS, 8, 128), F32),
                pltpu.VMEM((3, ROWS, 128), F32),
                pltpu.VMEM((ROWS, 128), jnp.int32),
                pltpu.VMEM((128, 128), BF16),
                pltpu.VMEM((4, ROWS, 128), F32),
                pltpu.VMEM((4, TILES, 128), F32),
                pltpu.VMEM((2, ROWS, NC), F32),
                pltpu.VMEM((256, SUB), BF16),
                pltpu.VMEM((256, SUB), BF16),
                pltpu.VMEM((4 * HALF, 256), F32),
                pltpu.VMEM((2, 2, HALF, 256), F32),
                pltpu.VMEM((2, PEERS, 16, 256), BF16),
                pltpu.VMEM((2, PEERS, 16, 256), BF16),
                pltpu.VMEM((2, 32, NR), F32),
                pltpu.VMEM((2, 32, NR), F32),
                pltpu.VMEM((2, 128, HALF), F32),
                pltpu.VMEM((2, PEERS, 16, 256), BF16),
                pltpu.VMEM((2, PEERS, 16, 256), BF16),
                pltpu.VMEM((4 * HALF, 256), F32),
                pltpu.VMEM((256, 4 * HALF), BF16),
                pltpu.VMEM((CHUNK // 256, 256, 256), F32),
                pltpu.VMEM((2, ROWS, NC), F32),
                pltpu.VMEM((CHUNK // 256, 128, 256), BF16),
                pltpu.VMEM((TILES * 32, 128), F32),
                pltpu.VMEM((2, TILES * 32, 128), F32),
                pltpu.VMEM((SROWS, 8, 128), F32),
                pltpu.VMEM((4, 8, 128), F32),
                pltpu.VMEM((2 * YS, 8, 128), F32),
                pltpu.VMEM((8, 128), F32),
                pltpu.VMEM((CHIPS, 8, 128), F32),
                pltpu.VMEM((8, 128), F32),
                pltpu.VMEM((YS, 8, 128), F32),
                dma((3, CHUNKS)),
                dma,
                dma((2,)),
                dma((4, PEERS)),
                dma((4, PEERS)),
                dma((2, 2 * YS)),
                dma((2, CHIPS)),
                dma((2, YS)),
            ],
            compiler_params=pltpu.CompilerParams(collective_id=0, has_side_effects=True, vmem_limit_bytes=LIMIT),
            name="gradient",
        )(amplitude, seg_map, seg_box, seg_coeffs, probe_freq, probe_amp, measured, ctable, rtable)

    in_specs = (P("row", None), P("row", None), P(), P(), P(), P(), P("band", "row", None, None, None))
    return jax.shard_map(body, mesh=mesh, in_specs=in_specs, out_specs=P(), check_vma=False)
```

```python
import functools
import math

import jax
import jax.numpy as jnp
import ml_dtypes
import numpy as np
from jax import lax
from jax.experimental import pallas as pl
from jax.experimental.pallas import tpu as pltpu
from jax.sharding import PartitionSpec as P

NC = 8192
NR = 2048
M = 256
BANDS = 8
PROBES = 4
SEG = 1200
SROWS = 16
PER_ROW = SEG // SROWS
HALF = M // 2
ROWS = 64
PEERS = 32
OWN = 8
SPREAD = 0.2
SAMPLING = 0.5
MESH = pl.DeviceIdType.MESH
F32 = jnp.float32
BF16 = jnp.bfloat16
SUB = 512
CHUNK = 1024
CHUNKS = NC // CHUNK
BCHUNK = 1024
TILES = NC // 128
CHIPS = 16
YS = 4
NT = (((1,), (1,)), ((), ()))


def series(fn, top, count):
    cheb = np.polynomial.chebyshev.Chebyshev.interpolate(
        lambda s: fn(np.sqrt(s)), count - 1, domain=[0.0, top * top]
    )
    return [float(v) for v in cheb.convert(kind=np.polynomial.Polynomial).coef]


def sinc(x):
    return np.sinc(x / np.pi)


SIN_PHASE = series(sinc, 3.02, 6)
COS_PHASE = series(np.cos, 3.02, 7)
SIN_WAVE = series(sinc, 0.81, 4)
COS_WAVE = series(np.cos, 0.81, 4)
SIN_TURN = series(lambda x: 2 * np.pi * np.sinc(2 * x), 0.5, 8)
COS_TURN = series(lambda x: np.cos(2 * np.pi * x), 0.5, 8)


def poly(coefs, s):
    total = jnp.full_like(s, coefs[-1])
    for value in coefs[-2::-1]:
        total = total * s + value
    return total


def turn_sincos(turns):
    part = turns - jnp.floor(turns + 0.5)
    square = part * part
    return part * poly(SIN_TURN, square), poly(COS_TURN, square)


def half_tables(coords, order):
    focal = (np.arange(HALF, dtype=np.float32) - np.float32(M / 2) + np.float32(0.5)) * np.float32(SAMPLING)
    base = (np.float32(2.0 * math.pi) * focal)[:, None] * coords[None, :]
    out = []
    for band in range(BANDS):
        ratio = np.float32(1.0) + np.float32(SPREAD) * (
            (np.float32(band) + np.float32(0.5)) / np.float32(BANDS) - np.float32(0.5)
        )
        angle = (base / ratio).astype(np.float64)
        out.append(np.stack([np.cos(angle), np.sin(angle)]).astype(np.float32).astype(ml_dtypes.bfloat16))
    return np.stack(out)


def column_table():
    coords = (np.arange(NC, dtype=np.float32) + np.float32(0.5)) / np.float32(NC) - np.float32(0.5)
    return half_tables(coords, 0).reshape(4, 4 * HALF, NC)


def row_table():
    coords = (np.arange(NR, dtype=np.float32) + np.float32(0.5)) / np.float32(NC) - np.float32(NR / (2.0 * NC))
    return half_tables(coords, 0).reshape(4, 4 * HALF, NR)


def lane_sign(first, second):
    lane = lax.broadcasted_iota(jnp.int32, (1, 128), 1)
    return jnp.where(lane < 64, F32(first), F32(second))


def iota(shape, dim):
    return lax.broadcasted_iota(jnp.int32, shape, dim)


def wave_setup(row0, freq_ref, amp_ref, roww, colw):
    rows = (iota((ROWS, 128), 0) + row0).astype(F32)
    place = (rows + 0.5) / NC - NR / (2.0 * NC)
    cols = (iota((TILES, 128), 0) * 128 + iota((TILES, 128), 1)).astype(F32)
    across = (cols + 0.5) / NC - 0.5
    for j in range(2):
        s, c = turn_sincos(place * freq_ref[j, 1].astype(F32))
        roww[2 * j] = s * amp_ref[j]
        roww[2 * j + 1] = c * amp_ref[j]
        s, c = turn_sincos(across * freq_ref[j, 0].astype(F32))
        colw[2 * j] = s
        colw[2 * j + 1] = c


def wave_sincos(j, rows, tile, roww, colw):
    col_sin = colw[2 * j, pl.ds(tile, 1), :]
    col_cos = colw[2 * j + 1, pl.ds(tile, 1), :]
    wave = roww[2 * j + 1, rows, :] * col_sin + roww[2 * j, rows, :] * col_cos
    square = wave * wave
    return wave * poly(SIN_WAVE, square), poly(COS_WAVE, square)


def lanes(index, width):
    return pl.ds(pl.multiple_of(index * width, width), width)


def segment_setup(row0, box_ref, coef_ref, seg, flat, tabs, rowt, base, pick):
    flat[...] = jnp.zeros_like(flat)
    flat[0:4, 0:SEG] = box_ref[...].astype(F32)
    flat[4:7, 0:SEG] = coef_ref[...]
    lane = iota((8, 128), 1)
    for t in range(SROWS):
        first, off = divmod(PER_ROW * t, 128)
        one = flat[:, 128 * first : 128 * first + 128]
        if off:
            two = flat[:, 128 * first + 128 : 128 * first + 256]
            one = jnp.where(lane < 128 - off, pltpu.roll(one, 128 - off, 1), pltpu.roll(two, 128 - off, 1))
        tabs[t] = one
    column = seg[:, 0:1]
    trow = jnp.zeros((ROWS, 1), jnp.int32)
    for m in range(1, SROWS):
        trow = trow + (column >= PER_ROW * m).astype(jnp.int32)
    trow = jnp.broadcast_to(trow, (ROWS, 128))
    base[...] = trow * PER_ROW
    rows = (iota((ROWS, 128), 0) + row0).astype(F32)
    alpha, beta, middle, down_all = [jnp.zeros((ROWS, 128), F32) for _ in range(4)]
    for t in range(SROWS):
        r0, r1, c0, c1 = [tabs[t, q : q + 1, :] for q in range(4)]
        piston, tip, tilt = [tabs[t, q : q + 1, :] for q in range(4, 7)]
        here = trow == t
        down = (rows - 0.5 * (r0 + r1)) / (0.5 * (r1 - r0 + 1.0))
        alpha = jnp.where(here, piston + tilt * down, alpha)
        beta = jnp.where(here, tip / (0.5 * (c1 - c0 + 1.0)), beta)
        middle = jnp.where(here, 0.5 * (c0 + c1), middle)
        down_all = jnp.where(here, down, down_all)
    rowt[0] = alpha
    rowt[1] = beta
    rowt[2] = middle
    lane = iota((ROWS, 128), 1)
    down_all = jnp.broadcast_to(down_all[:, 0:1], (ROWS, 128))
    high = down_all.astype(BF16).astype(F32)
    which = jnp.where(lane < 16, 1.0, jnp.where(lane < 32, high, jnp.where(lane < 48, down_all - high, 0.0)))
    chosen = jnp.where(lax.rem(lane, 16) == trow, which, 0.0)
    pick[...] = jnp.concatenate([chosen, chosen], axis=0).T.astype(BF16)


def fields(j, chunk, ebuf, amp, seg, rowt, base, roww, colw, pbuf):
    for lt in range(SUB // 128):
        tile = chunk * (SUB // 128) + lt
        wide = lanes(tile, 128)
        cols = slice(128 * lt, 128 * lt + 128)
        cf = (iota((32, 128), 1) + tile * 128).astype(F32)
        for rh in range(2):
            rows = slice(32 * rh, 32 * rh + 32)
            if j == 0:
                idx = seg[rows, wide] - base[rows, :]
                a = jnp.take_along_axis(rowt[0, rows, :], idx, axis=1)
                b = jnp.take_along_axis(rowt[1, rows, :], idx, axis=1)
                m = jnp.take_along_axis(rowt[2, rows, :], idx, axis=1)
                phase = a + b * (cf - m)
                square = phase * phase
                mag = amp[rows, wide].astype(F32)
                pr = mag * poly(COS_PHASE, square)
                pi = mag * (phase * poly(SIN_PHASE, square))
                pbuf[0, rows, wide] = pr
                pbuf[1, rows, wide] = pi
            else:
                pr = pbuf[0, rows, wide]
                pi = pbuf[1, rows, wide]
            sw, cw = wave_sincos(j, rows, tile, roww, colw)
            for t, f in ((0, cw), (1, sw)):
                at = 128 * t + 32 * rh
                ebuf[at : at + 32, cols] = (pr * f).astype(BF16)
                ebuf[at + 64 : at + 96, cols] = (pi * f).astype(BF16)


def column_sums(acc, pay, ysc):
    plus = lane_sign(1.0, -1.0)
    for b in range(2):
        parts = []
        for t in range(2):
            cols = slice(128 * t, 128 * t + 128)
            c = acc[256 * b : 256 * b + 128, cols]
            s = plus * pltpu.roll(acc[256 * b + 128 : 256 * b + 256, cols], 64, 1)
            parts.append((c + s, c - s))
        for side in range(2):
            even = parts[0][side]
            odd = plus * pltpu.roll(parts[1][side], 64, 1)
            ysc[side, b, :, 0:128] = even - odd
            ysc[side, b, :, 128:256] = even + odd
    for d in range(PEERS // 2):
        for side in range(2):
            to = d if side == 0 else PEERS - 1 - d
            pay[to] = jnp.concatenate(
                [ysc[side, b, OWN * d : OWN * d + OWN, :] for b in range(2)], axis=0
            ).astype(BF16)


def focal_part(j, normf, recv, hpay, lhs, hs, ms, table):
    low = iota((16, 128), 1) < 64

    def gather(s4, carry):
        for k in range(4):
            s = s4 * 4 + k
            cols = lanes(s, 128)
            for q in range(2):
                one = recv[2 * s, :, 128 * q : 128 * q + 128].astype(F32)
                two = recv[2 * s + 1, :, 128 * q : 128 * q + 128].astype(F32)
                re = jnp.where(low, one, pltpu.roll(two, 64, 1))
                im = jnp.where(low, pltpu.roll(one, 64, 1), two)
                for b in range(2):
                    lhs[b, 16 * q : 16 * q + 8, cols] = re[8 * b : 8 * b + 8]
                    lhs[b, 16 * q + 8 : 16 * q + 16, cols] = im[8 * b : 8 * b + 8]
        return carry
    lax.fori_loop(0, PEERS // 8, gather, 0)

    for b in range(2):
        here = table[256 * b : 256 * b + 256, :]
        parts = lax.dot_general(lhs[b].astype(BF16), here, NT, preferred_element_type=F32)
        rows = []
        for q in range(2):
            re, im = parts[16 * q : 16 * q + 8], parts[16 * q + 8 : 16 * q + 16]
            pieces = []
            for o, (c, s) in enumerate(((re[:, :HALF], im[:, HALF:]), (im[:, :HALF], -re[:, HALF:]))):
                want = pl.ds(b * 64 + 4 * j + 2 * q + o, 8, stride=8)
                one = (c + s) * normf - ms[0, want, :]
                two = (c - s) * normf - ms[1, want, :]
                pieces.append((one + two, one - two))
            (re_e, re_o), (im_e, im_o) = pieces
            rows.append(jnp.concatenate([re_e, -im_o], axis=1))
            rows.append(jnp.concatenate([im_e, re_o], axis=1))
        left = jnp.concatenate(rows, axis=0).astype(BF16)
        hs[b] = jnp.dot(left, here, preferred_element_type=F32)

    low8 = iota((8, 128), 1) < 64

    def spread(s4, carry):
        for k in range(4):
            s = s4 * 4 + k
            cols = lanes(s, 128)
            for q in range(2):
                first, second = [], []
                for b in range(2):
                    re = hs[b, 16 * q : 16 * q + 8, cols]
                    im = hs[b, 16 * q + 8 : 16 * q + 16, cols]
                    first.append(jnp.where(low8, re, pltpu.roll(im, 64, 1)))
                    second.append(jnp.where(low8, pltpu.roll(re, 64, 1), im))
                hpay[2 * s, :, 128 * q : 128 * q + 128] = jnp.concatenate(first, axis=0).astype(BF16)
                hpay[2 * s + 1, :, 128 * q : 128 * q + 128] = jnp.concatenate(second, axis=0).astype(BF16)
        return carry
    lax.fori_loop(0, PEERS // 8, spread, 0)


def hidden_left(j, hid, left, leftt):
    minus = lane_sign(-1.0, 1.0)
    for d in range(PEERS // 2):
        here = hid[d].astype(F32)
        there = hid[PEERS - 1 - d].astype(F32)
        even, odd = here + there, here - there
        e = [even[:, 128 * t : 128 * t + 128] for t in range(2)]
        o = [odd[:, 128 * t : 128 * t + 128] for t in range(2)]
        for t in range(2):
            cols = slice(128 * t, 128 * t + 128)
            es = e[0] + e[1] if t == 0 else e[0] - e[1]
            os = o[0] + o[1] if t == 0 else o[0] - o[1]
            os = minus * pltpu.roll(os, 64, 1)
            for b in range(2):
                left[256 * b + 8 * d : 256 * b + 8 * d + 8, cols] = es[8 * b : 8 * b + 8]
                left[256 * b + 128 + 8 * d : 256 * b + 136 + 8 * d, cols] = os[8 * b : 8 * b + 8]
    leftt[256 * j : 256 * j + 256, :] = left[...].T.astype(BF16)


def weights(lt, piece, gbuf, roww, colw, pbuf, wst):
    for lh in range(2):
        tile = piece * 2 + lh
        wide = lanes(tile, 128)
        gc = slice(128 * lh, 128 * lh + 128)
        for rh in range(2):
            rows = slice(32 * rh, 32 * rh + 32)
            zr, zi = 0.0, 0.0
            for j in range(2):
                sw, cw = wave_sincos(j, rows, tile, roww, colw)
                at = [256 * j + 64 * n + 32 * rh for n in range(4)]
                g = [gbuf[lt, x : x + 32, gc] for x in at]
                zr = zr + (cw * g[0] + sw * g[3])
                zi = zi + (cw * g[1] - sw * g[2])
            w = pbuf[0, rows, wide] * zi - pbuf[1, rows, wide] * zr
            high = w.astype(BF16)
            wst[32 * rh : 32 * rh + 32, wide] = high
            wst[64 + 32 * rh : 96 + 32 * rh, wide] = (w - high.astype(F32)).astype(BF16)


def backward(chunk, leftt, table, gbuf, roww, colw, pbuf, wst):
    count = BCHUNK // 256
    for lt in range(count + 1):
        piece = chunk * count + lt
        if lt < count:
            gbuf[lt] = jnp.dot(leftt[...], table[:, lanes(piece, 256)], preferred_element_type=F32)
        if lt > 0:
            weights(lt - 1, piece - 1, gbuf, roww, colw, pbuf, wst)


def segment_sums(tabs, wst, pick, pre, sbuf, pack):
    row, col = iota((256, 512), 0), iota((256, 512), 1)
    at = lax.rem(row, 128)
    to = jnp.where(col < 256, lax.rem(col, 128), 127)
    weight = jnp.where(lax.rem(col, 256) < 128, 1.0, at.astype(F32))
    tri = jnp.where(at <= to, weight, 0.0).astype(BF16)

    def prefix(k, carry):
        rows = pl.ds(pl.multiple_of(k * 256, 256), 256)
        u = jnp.dot(pick[0:48, :], wst[:, lanes(k, 1024)], preferred_element_type=F32)
        parts = []
        for lt in range(8):
            gc = slice(128 * lt, 128 * lt + 128)
            parts += [u[0:16, gc], u[16:32, gc] + u[32:48, gc]]
        u = jnp.concatenate(parts, axis=0)
        high = u.astype(BF16)
        low = (u - high.astype(F32)).astype(BF16)
        both = jnp.dot(jnp.concatenate([high, low], axis=1), tri, preferred_element_type=F32)
        for q in range(4):
            pre[q, rows, :] = both[:, 128 * q : 128 * q + 128]
        return carry
    lax.fori_loop(0, TILES * 32 // 256, prefix, 0)

    tile = iota((TILES, 128), 0).astype(F32)
    lane = iota((1, 128), 1)

    def slot(t, carry):
        c0 = tabs[t, 2:3, :]
        c1 = tabs[t, 3:4, :]
        tile0 = jnp.floor(c0 * (1.0 / 128.0))
        tile1 = jnp.floor(c1 * (1.0 / 128.0))
        in0 = c0 - 128.0 * tile0 - 1.0
        in1 = c1 - 128.0 * tile1
        idx0 = jnp.broadcast_to(jnp.maximum(in0, 0.0).astype(jnp.int32), (TILES, 128))
        idx1 = jnp.broadcast_to(in1.astype(jnp.int32), (TILES, 128))
        some = in0 >= 0.0
        diffs = []
        for half, at in ((0, t), (1, t), (0, t + 16)):
            a = pre[half, pl.ds(at, TILES, stride=32), :]
            whole = pre[half + 2, pl.ds(at, TILES, stride=32), :]
            g1 = jnp.take_along_axis(a, idx1, axis=1)
            g0 = jnp.where(some, jnp.take_along_axis(a, idx0, axis=1), 0.0)
            upto1 = jnp.where(tile == tile1, g1, jnp.where(tile < tile1, whole, 0.0))
            upto0 = jnp.where(tile == tile0, g0, jnp.where(tile < tile0, whole, 0.0))
            diffs.append(upto1 - upto0)
        middle = 0.5 * (c0 + c1)
        half_width = 0.5 * (c1 - c0 + 1.0)
        slope = diffs[1] + (128.0 * tile - middle) * diffs[0]
        sums = [jnp.sum(diffs[0], axis=0, keepdims=True),
                jnp.sum(slope, axis=0, keepdims=True) / half_width,
                jnp.sum(diffs[2], axis=0, keepdims=True)]
        sbuf[t] = jnp.where(lane < PER_ROW, jnp.concatenate(sums + [jnp.zeros((5, 128), F32)], axis=0), 0.0)
        return carry
    lax.fori_loop(0, SROWS, slot, 0, unroll=4)

    packed = [jnp.zeros((8, 128), F32) for _ in range(10)]
    lane = iota((8, 128), 1)
    for t in range(SROWS):
        first, off = divmod(PER_ROW * t, 128)
        turned = pltpu.roll(sbuf[t], off, 1) if off else sbuf[t]
        packed[first] = packed[first] + jnp.where(lane >= off, turned, 0.0)
        if off + PER_ROW > 128:
            packed[first + 1] = packed[first + 1] + jnp.where(lane < off, turned, 0.0)
    for q in range(3):
        for k in range(10):
            p, r = divmod(q * 10 + k, 8)
            pack[p, r : r + 1, :] = packed[k][q : q + 1, :]
    pack[3, 6:8, :] = jnp.zeros((2, 128), F32)


def remote(src, dst, ssem, rsem, where):
    return pltpu.make_async_remote_copy(src_ref=src, dst_ref=dst, send_sem=ssem, recv_sem=rsem,
                                        device_id=where, device_id_type=MESH)


def each(count, fn):
    def step(o, carry):
        fn(o)
        return carry
    lax.fori_loop(1, count, step, 0)


def kernel(normf, scale, amp_hbm, seg_hbm, box_hbm, coef_hbm, freq_ref, pamp_ref, meas_hbm, ctab_hbm, rtab_hbm,
           out_ref, box_ref, coef_ref, meas_ref, amp, seg, ctab, rtab, flat, tabs, rowt, base, pick, roww, colw, pbuf, eb0, eb1, acc, ysc,
           pay, recv, lhs, hs, ms, hpay, hid, left, leftt, gbuf, wst, pre, sbuf, pack,
           got_a, mine_b, got_b, mine_c, got_c, lsem, tsem, osem, ssem, rsem, asem, bsem, csem):
    band = lax.axis_index("band")
    me = lax.axis_index("row")
    core = lax.rem(me, 2)
    chip = me // 2
    row0 = me * ROWS

    def loads(i):
        cols = lanes(i, CHUNK)
        return [pltpu.make_async_copy(seg_hbm.at[:, cols], seg.at[:, cols], lsem.at[0, i]),
                pltpu.make_async_copy(amp_hbm.at[:, cols], amp.at[:, cols], lsem.at[1, i]),
                pltpu.make_async_copy(ctab_hbm.at[band, :, cols], ctab.at[:, cols], lsem.at[2, i])]

    def start_loads(i, carry):
        for copy in loads(i):
            copy.start()
        return carry
    small = [pltpu.make_async_copy(box_hbm, box_ref, osem.at[0]),
             pltpu.make_async_copy(coef_hbm, coef_ref, osem.at[1]),
             pltpu.make_async_copy(meas_hbm, meas_ref, osem.at[2])]
    small[0].start()
    small[1].start()
    lax.fori_loop(0, CHUNKS, start_loads, 0)
    small[2].start()
    table_copy = pltpu.make_async_copy(rtab_hbm.at[band], rtab, tsem)
    table_copy.start()

    barrier = pltpu.get_barrier_semaphore()

    def greet(where):
        pl.semaphore_signal(barrier, inc=1, device_id=where, device_id_type=MESH)
    each(PEERS, lambda o: greet((band, lax.rem(me + o, PEERS))))
    for o in range(1, YS):
        for c in range(2):
            greet((lax.rem(band + o, YS), chip * 2 + c))

    wave_setup(row0, freq_ref, pamp_ref, roww, colw)
    def send(j, source, target):
        def one(o):
            peer = lax.rem(me + o, PEERS)
            remote(source.at[j, peer], target.at[j, me], ssem.at[j, peer], rsem.at[j, me], (band, peer)).start()
        each(PEERS, one)

    def await_all(j, source, target):
        def one(o):
            peer = lax.rem(me + o, PEERS)
            remote(source.at[j, peer], target.at[j, peer], ssem.at[j, peer], rsem.at[j, peer], (band, peer)).wait()
        each(PEERS, one)

    for j in range(2):
        acc[...] = jnp.zeros_like(acc)
        eb1[...] = jnp.zeros_like(eb1)

        def forward(i, carry):
            if j == 0:
                for copy in loads(i):
                    copy.wait()

                @pl.when(i == 0)
                def _():
                    small[0].wait()
                    small[1].wait()
                    segment_setup(row0, box_ref, coef_ref, seg, flat, tabs, rowt, base, pick)
            before = jnp.maximum(2 * i - 1, 0)
            fields(j, 2 * i, eb0, amp, seg, rowt, base, roww, colw, pbuf)
            acc[...] += lax.dot_general(ctab[:, lanes(before, SUB)], eb1[...], NT, preferred_element_type=F32)
            fields(j, 2 * i + 1, eb1, amp, seg, rowt, base, roww, colw, pbuf)
            acc[...] += lax.dot_general(ctab[:, lanes(2 * i, SUB)], eb0[...], NT, preferred_element_type=F32)
            return carry
        lax.fori_loop(0, CHUNKS, forward, 0)
        acc[...] += lax.dot_general(ctab[:, NC - SUB : NC], eb1[...], NT, preferred_element_type=F32)
        column_sums(acc, pay.at[j], ysc)
        if j == 0:
            pl.semaphore_wait(barrier, PEERS - 1 + 2 * (YS - 1))
        send(j, pay, recv)
        recv[j, me] = pay[j, me]

    small[2].wait()
    for b in range(2):
        for v in range(OWN):
            source = jnp.where(me < PEERS // 2, v, OWN - 1 - v)
            for k in range(PROBES):
                at = b * 64 + 8 * v + 2 * k
                ms[0, at : at + 2, :] = meas_ref[b, source, k, :, :HALF]
                ms[1, at : at + 2, :] = meas_ref[b, source, k, :, HALF:]
    flip = (iota((128, 128), 0) + iota((128, 128), 1) == 127).astype(F32)
    ms[1] = jnp.dot(ms[1], flip, precision=lax.Precision.HIGHEST, preferred_element_type=F32)
    table_copy.wait()
    for j in range(2):
        await_all(j, pay, recv)
        focal_part(j, normf, recv.at[j], hpay.at[j], lhs, hs, ms, rtab)
        def one(o):
            peer = lax.rem(me + o, PEERS)
            remote(hpay.at[j, peer], hid.at[j, me], ssem.at[2 + j, peer], rsem.at[2 + j, me], (band, peer)).start()
        each(PEERS, one)
        hid[j, me] = hpay[j, me]

    for j in range(2):
        def done(o):
            peer = lax.rem(me + o, PEERS)
            remote(hpay.at[j, peer], hid.at[j, peer], ssem.at[2 + j, peer], rsem.at[2 + j, peer],
                   (band, peer)).wait()
        each(PEERS, done)
        hidden_left(j, hid.at[j], left, leftt)

    def back(i, carry):
        backward(i, leftt, ctab, gbuf, roww, colw, pbuf, wst)
        return carry
    lax.fori_loop(0, NC // BCHUNK, back, 0)

    segment_sums(tabs, wst, pick, pre, sbuf, pack)

    near = band * 2 + core

    def near_copy(o, slot):
        peer = lax.rem(near + o, 2 * YS)
        to = peer // 2
        at = near if slot == "mine" else peer
        return remote(pack.at[to], got_a.at[at], asem.at[0, peer], asem.at[1, at],
                      (to, chip * 2 + lax.rem(peer, 2)))
    each(2 * YS, lambda o: near_copy(o, "mine").start())
    got_a[near] = pack[band]
    each(2 * YS, lambda o: near_copy(o, "peer").wait())
    total = got_a[0]
    for k in range(1, 2 * YS):
        total = total + got_a[k]
    mine_b[...] = total

    def far_copy(o, slot):
        peer = lax.rem(chip + o, CHIPS)
        at = chip if slot == "mine" else peer
        return remote(mine_b, got_b.at[at], bsem.at[0, peer], bsem.at[1, at], (band, peer * 2 + core))
    each(CHIPS, lambda o: far_copy(o, "mine").start())
    got_b[chip] = mine_b[...]
    each(CHIPS, lambda o: far_copy(o, "peer").wait())
    total = got_b[0]
    for k in range(1, CHIPS):
        total = total + got_b[k]
    mine_c[...] = total * scale

    def share_copy(o, slot):
        peer = lax.rem(band + o, YS)
        at = band if slot == "mine" else peer
        return remote(mine_c, got_c.at[at], csem.at[0, peer], csem.at[1, at], (peer, me))
    each(YS, lambda o: share_copy(o, "mine").start())
    got_c[band] = mine_c[...]
    each(YS, lambda o: share_copy(o, "peer").wait())
    for q in range(3):
        for k in range(10):
            p, r = divmod(q * 10 + k, 8)
            width = min(128, SEG - 128 * k)
            out_ref[q : q + 1, 128 * k : 128 * k + width] = got_c[p, r : r + 1, :width]


VM = pl.BlockSpec(memory_space=pltpu.VMEM)
SM = pl.BlockSpec(memory_space=pltpu.SMEM)
HBM = pl.BlockSpec(memory_space=pl.ANY)
LIMIT = 60 * 1024 * 1024


def solution(mesh):
    ctable = jnp.asarray(column_table())
    rtable = jnp.asarray(row_table())
    root = math.sqrt(NR * NC)

    def body(amplitude, seg_map, seg_box, seg_coeffs, probe_freq, probe_amp, measured):
        dma = pltpu.SemaphoreType.DMA
        return pl.pallas_call(
            functools.partial(kernel, 1.0 / root, 2.0 / root / (BANDS * PROBES)),
            in_specs=[HBM, HBM, HBM, HBM, SM, SM, HBM, HBM, HBM],
            out_specs=VM,
            out_shape=jax.ShapeDtypeStruct((3, SEG), F32),
            scratch_shapes=[
                pltpu.VMEM((4, SEG), jnp.int32),
                pltpu.VMEM((3, SEG), F32),
                pltpu.VMEM((2, OWN, PROBES, 2, M), F32),
                pltpu.VMEM((ROWS, NC), BF16),
                pltpu.VMEM((ROWS, NC), jnp.int32),
                pltpu.VMEM((4 * HALF, NC), BF16),
                pltpu.VMEM((4 * HALF, NR), BF16),
                pltpu.VMEM((8, 1280), F32),
                pltpu.VMEM((SROWS, 8, 128), F32),
                pltpu.VMEM((3, ROWS, 128), F32),
                pltpu.VMEM((ROWS, 128), jnp.int32),
                pltpu.VMEM((128, 128), BF16),
                pltpu.VMEM((4, ROWS, 128), F32),
                pltpu.VMEM((4, TILES, 128), F32),
                pltpu.VMEM((2, ROWS, NC), F32),
                pltpu.VMEM((256, SUB), BF16),
                pltpu.VMEM((256, SUB), BF16),
                pltpu.VMEM((4 * HALF, 256), F32),
                pltpu.VMEM((2, 2, HALF, 256), F32),
                pltpu.VMEM((2, PEERS, 16, 256), BF16),
                pltpu.VMEM((2, PEERS, 16, 256), BF16),
                pltpu.VMEM((2, 32, NR), F32),
                pltpu.VMEM((2, 32, NR), F32),
                pltpu.VMEM((2, 128, HALF), F32),
                pltpu.VMEM((2, PEERS, 16, 256), BF16),
                pltpu.VMEM((2, PEERS, 16, 256), BF16),
                pltpu.VMEM((4 * HALF, 256), F32),
                pltpu.VMEM((512, 4 * HALF), BF16),
                pltpu.VMEM((BCHUNK // 256, 512, 256), F32),
                pltpu.VMEM((128, NC), BF16),
                pltpu.VMEM((4, TILES * 32, 128), F32),
                pltpu.VMEM((SROWS, 8, 128), F32),
                pltpu.VMEM((4, 8, 128), F32),
                pltpu.VMEM((2 * YS, 8, 128), F32),
                pltpu.VMEM((8, 128), F32),
                pltpu.VMEM((CHIPS, 8, 128), F32),
                pltpu.VMEM((8, 128), F32),
                pltpu.VMEM((YS, 8, 128), F32),
                dma((3, CHUNKS)),
                dma,
                dma((3,)),
                dma((4, PEERS)),
                dma((4, PEERS)),
                dma((2, 2 * YS)),
                dma((2, CHIPS)),
                dma((2, YS)),
            ],
            compiler_params=pltpu.CompilerParams(collective_id=0, has_side_effects=True, vmem_limit_bytes=LIMIT),
            name="gradient",
        )(amplitude, seg_map, seg_box, seg_coeffs, probe_freq, probe_amp, measured, ctable, rtable)

    in_specs = (P("row", None), P("row", None), P(), P(), P(), P(), P("band", "row", None, None, None))
    return jax.shard_map(body, mesh=mesh, in_specs=in_specs, out_specs=P(), check_vma=False)
```

```python
import functools
import math

import jax
import jax.numpy as jnp
import ml_dtypes
import numpy as np
from jax import lax
from jax.experimental import pallas as pl
from jax.experimental.pallas import tpu as pltpu
from jax.sharding import PartitionSpec as P

NC = 8192
NR = 2048
M = 256
BANDS = 8
PROBES = 4
SEG = 1200
SROWS = 16
PER_ROW = SEG // SROWS
HALF = M // 2
ROWS = 64
PEERS = 32
OWN = 8
SPREAD = 0.2
SAMPLING = 0.5
MESH = pl.DeviceIdType.MESH
F32 = jnp.float32
BF16 = jnp.bfloat16
SUB = 1024
CHUNK = 2048
CHUNKS = NC // CHUNK
BCHUNK = 1024
TILES = NC // 128
CHIPS = 16
YS = 4
NT = (((1,), (1,)), ((), ()))


def series(fn, top, count):
    cheb = np.polynomial.chebyshev.Chebyshev.interpolate(
        lambda s: fn(np.sqrt(s)), count - 1, domain=[0.0, top * top]
    )
    return [float(v) for v in cheb.convert(kind=np.polynomial.Polynomial).coef]


def sinc(x):
    return np.sinc(x / np.pi)


SIN_PHASE = series(sinc, 3.02, 6)
COS_PHASE = series(np.cos, 3.02, 7)
SIN_WAVE = series(sinc, 0.81, 4)
COS_WAVE = series(np.cos, 0.81, 4)
SIN_TURN = series(lambda x: 2 * np.pi * np.sinc(2 * x), 0.5, 8)
COS_TURN = series(lambda x: np.cos(2 * np.pi * x), 0.5, 8)


def poly(coefs, s):
    total = jnp.full_like(s, coefs[-1])
    for value in coefs[-2::-1]:
        total = total * s + value
    return total


def turn_sincos(turns):
    part = turns - jnp.floor(turns + 0.5)
    square = part * part
    return part * poly(SIN_TURN, square), poly(COS_TURN, square)


def half_tables(coords, order):
    focal = (np.arange(HALF, dtype=np.float32) - np.float32(M / 2) + np.float32(0.5)) * np.float32(SAMPLING)
    base = (np.float32(2.0 * math.pi) * focal)[:, None] * coords[None, :]
    out = []
    for band in range(BANDS):
        ratio = np.float32(1.0) + np.float32(SPREAD) * (
            (np.float32(band) + np.float32(0.5)) / np.float32(BANDS) - np.float32(0.5)
        )
        angle = (base / ratio).astype(np.float64)
        out.append(np.stack([np.cos(angle), np.sin(angle)]).astype(np.float32).astype(ml_dtypes.bfloat16))
    return np.stack(out)


def column_table():
    coords = (np.arange(NC, dtype=np.float32) + np.float32(0.5)) / np.float32(NC) - np.float32(0.5)
    return half_tables(coords, 0).reshape(4, 4 * HALF, NC)


def row_table():
    coords = (np.arange(NR, dtype=np.float32) + np.float32(0.5)) / np.float32(NC) - np.float32(NR / (2.0 * NC))
    return half_tables(coords, 0).reshape(4, 4 * HALF, NR)


def lane_sign(first, second):
    lane = lax.broadcasted_iota(jnp.int32, (1, 128), 1)
    return jnp.where(lane < 64, F32(first), F32(second))


def iota(shape, dim):
    return lax.broadcasted_iota(jnp.int32, shape, dim)


def wave_setup(row0, freq_ref, amp_ref, roww, colw):
    rows = (iota((ROWS, 128), 0) + row0).astype(F32)
    place = (rows + 0.5) / NC - NR / (2.0 * NC)
    cols = (iota((TILES, 128), 0) * 128 + iota((TILES, 128), 1)).astype(F32)
    across = (cols + 0.5) / NC - 0.5
    for j in range(2):
        s, c = turn_sincos(place * freq_ref[j, 1].astype(F32))
        roww[2 * j] = s * amp_ref[j]
        roww[2 * j + 1] = c * amp_ref[j]
        s, c = turn_sincos(across * freq_ref[j, 0].astype(F32))
        colw[2 * j] = s
        colw[2 * j + 1] = c


def wave_sincos(j, rows, tile, roww, colw):
    col_sin = colw[2 * j, pl.ds(tile, 1), :]
    col_cos = colw[2 * j + 1, pl.ds(tile, 1), :]
    wave = roww[2 * j + 1, rows, :] * col_sin + roww[2 * j, rows, :] * col_cos
    square = wave * wave
    return wave * poly(SIN_WAVE, square), poly(COS_WAVE, square)


def lanes(index, width):
    return pl.ds(pl.multiple_of(index * width, width), width)


def segment_setup(row0, box_ref, coef_ref, seg, flat, tabs, rowt, base, pick):
    flat[...] = jnp.zeros_like(flat)
    flat[0:4, 0:SEG] = box_ref[...].astype(F32)
    flat[4:7, 0:SEG] = coef_ref[...]
    lane = iota((8, 128), 1)
    for t in range(SROWS):
        first, off = divmod(PER_ROW * t, 128)
        one = flat[:, 128 * first : 128 * first + 128]
        if off:
            two = flat[:, 128 * first + 128 : 128 * first + 256]
            one = jnp.where(lane < 128 - off, pltpu.roll(one, 128 - off, 1), pltpu.roll(two, 128 - off, 1))
        tabs[t] = one
    column = seg[:, 0:1]
    trow = jnp.zeros((ROWS, 1), jnp.int32)
    for m in range(1, SROWS):
        trow = trow + (column >= PER_ROW * m).astype(jnp.int32)
    trow = jnp.broadcast_to(trow, (ROWS, 128))
    base[...] = trow * PER_ROW
    rows = (iota((ROWS, 128), 0) + row0).astype(F32)
    alpha, beta, middle, down_all = [jnp.zeros((ROWS, 128), F32) for _ in range(4)]
    for t in range(SROWS):
        r0, r1, c0, c1 = [tabs[t, q : q + 1, :] for q in range(4)]
        piston, tip, tilt = [tabs[t, q : q + 1, :] for q in range(4, 7)]
        here = trow == t
        down = (rows - 0.5 * (r0 + r1)) / (0.5 * (r1 - r0 + 1.0))
        alpha = jnp.where(here, piston + tilt * down, alpha)
        beta = jnp.where(here, tip / (0.5 * (c1 - c0 + 1.0)), beta)
        middle = jnp.where(here, 0.5 * (c0 + c1), middle)
        down_all = jnp.where(here, down, down_all)
    rowt[0] = alpha
    rowt[1] = beta
    rowt[2] = middle
    lane = iota((ROWS, 128), 1)
    down_all = jnp.broadcast_to(down_all[:, 0:1], (ROWS, 128))
    high = down_all.astype(BF16).astype(F32)
    which = jnp.where(lane < 16, 1.0, jnp.where(lane < 32, high, jnp.where(lane < 48, down_all - high, 0.0)))
    chosen = jnp.where(lax.rem(lane, 16) == trow, which, 0.0)
    pick[...] = jnp.concatenate([chosen, chosen], axis=0).T.astype(BF16)


def fields(j, chunk, ebuf, amp, seg, rowt, base, roww, colw, pbuf):
    for lt in range(SUB // 128):
        tile = chunk * (SUB // 128) + lt
        wide = lanes(tile, 128)
        cols = slice(128 * lt, 128 * lt + 128)
        cf = (iota((32, 128), 1) + tile * 128).astype(F32)
        for rh in range(2):
            rows = slice(32 * rh, 32 * rh + 32)
            if j == 0:
                idx = seg[rows, wide] - base[rows, :]
                a = jnp.take_along_axis(rowt[0, rows, :], idx, axis=1)
                b = jnp.take_along_axis(rowt[1, rows, :], idx, axis=1)
                m = jnp.take_along_axis(rowt[2, rows, :], idx, axis=1)
                phase = a + b * (cf - m)
                square = phase * phase
                mag = amp[rows, wide].astype(F32)
                pr = mag * poly(COS_PHASE, square)
                pi = mag * (phase * poly(SIN_PHASE, square))
                pbuf[0, rows, wide] = pr
                pbuf[1, rows, wide] = pi
            else:
                pr = pbuf[0, rows, wide]
                pi = pbuf[1, rows, wide]
            sw, cw = wave_sincos(j, rows, tile, roww, colw)
            for t, f in ((0, cw), (1, sw)):
                at = 128 * t + 32 * rh
                ebuf[at : at + 32, cols] = (pr * f).astype(BF16)
                ebuf[at + 64 : at + 96, cols] = (pi * f).astype(BF16)


def column_sums(acc, pay, ysc):
    plus = lane_sign(1.0, -1.0)
    for b in range(2):
        parts = []
        for t in range(2):
            cols = slice(128 * t, 128 * t + 128)
            c = acc[256 * b : 256 * b + 128, cols]
            s = plus * pltpu.roll(acc[256 * b + 128 : 256 * b + 256, cols], 64, 1)
            parts.append((c + s, c - s))
        for side in range(2):
            even = parts[0][side]
            odd = plus * pltpu.roll(parts[1][side], 64, 1)
            ysc[side, b, :, 0:128] = even - odd
            ysc[side, b, :, 128:256] = even + odd
    for d in range(PEERS // 2):
        for side in range(2):
            to = d if side == 0 else PEERS - 1 - d
            pay[to] = jnp.concatenate(
                [ysc[side, b, OWN * d : OWN * d + OWN, :] for b in range(2)], axis=0
            ).astype(BF16)


def focal_part(j, normf, recv, hpay, lhs, hs, ms, table):
    low = iota((16, 128), 1) < 64

    def gather(s4, carry):
        for k in range(4):
            s = s4 * 4 + k
            cols = lanes(s, 128)
            for q in range(2):
                one = recv[2 * s, :, 128 * q : 128 * q + 128].astype(F32)
                two = recv[2 * s + 1, :, 128 * q : 128 * q + 128].astype(F32)
                re = jnp.where(low, one, pltpu.roll(two, 64, 1))
                im = jnp.where(low, pltpu.roll(one, 64, 1), two)
                for b in range(2):
                    lhs[b, 16 * q : 16 * q + 8, cols] = re[8 * b : 8 * b + 8]
                    lhs[b, 16 * q + 8 : 16 * q + 16, cols] = im[8 * b : 8 * b + 8]
        return carry
    lax.fori_loop(0, PEERS // 8, gather, 0)

    for b in range(2):
        here = table[256 * b : 256 * b + 256, :]
        parts = lax.dot_general(lhs[b].astype(BF16), here, NT, preferred_element_type=F32)
        rows = []
        for q in range(2):
            re, im = parts[16 * q : 16 * q + 8], parts[16 * q + 8 : 16 * q + 16]
            pieces = []
            for o, (c, s) in enumerate(((re[:, :HALF], im[:, HALF:]), (im[:, :HALF], -re[:, HALF:]))):
                want = pl.ds(b * 64 + 4 * j + 2 * q + o, 8, stride=8)
                one = (c + s) * normf - ms[0, want, :]
                two = (c - s) * normf - ms[1, want, :]
                pieces.append((one + two, one - two))
            (re_e, re_o), (im_e, im_o) = pieces
            rows.append(jnp.concatenate([re_e, -im_o], axis=1))
            rows.append(jnp.concatenate([im_e, re_o], axis=1))
        left = jnp.concatenate(rows, axis=0).astype(BF16)
        hs[b] = jnp.dot(left, here, preferred_element_type=F32)

    low8 = iota((8, 128), 1) < 64

    def spread(s4, carry):
        for k in range(4):
            s = s4 * 4 + k
            cols = lanes(s, 128)
            for q in range(2):
                first, second = [], []
                for b in range(2):
                    re = hs[b, 16 * q : 16 * q + 8, cols]
                    im = hs[b, 16 * q + 8 : 16 * q + 16, cols]
                    first.append(jnp.where(low8, re, pltpu.roll(im, 64, 1)))
                    second.append(jnp.where(low8, pltpu.roll(re, 64, 1), im))
                hpay[2 * s, :, 128 * q : 128 * q + 128] = jnp.concatenate(first, axis=0).astype(BF16)
                hpay[2 * s + 1, :, 128 * q : 128 * q + 128] = jnp.concatenate(second, axis=0).astype(BF16)
        return carry
    lax.fori_loop(0, PEERS // 8, spread, 0)


def hidden_left(j, hid, left, leftt):
    minus = lane_sign(-1.0, 1.0)
    for d in range(PEERS // 2):
        here = hid[d].astype(F32)
        there = hid[PEERS - 1 - d].astype(F32)
        even, odd = here + there, here - there
        e = [even[:, 128 * t : 128 * t + 128] for t in range(2)]
        o = [odd[:, 128 * t : 128 * t + 128] for t in range(2)]
        for t in range(2):
            cols = slice(128 * t, 128 * t + 128)
            es = e[0] + e[1] if t == 0 else e[0] - e[1]
            os = o[0] + o[1] if t == 0 else o[0] - o[1]
            os = minus * pltpu.roll(os, 64, 1)
            for b in range(2):
                left[256 * b + 8 * d : 256 * b + 8 * d + 8, cols] = es[8 * b : 8 * b + 8]
                left[256 * b + 128 + 8 * d : 256 * b + 136 + 8 * d, cols] = os[8 * b : 8 * b + 8]
    leftt[256 * j : 256 * j + 256, :] = left[...].T.astype(BF16)


def weights(lt, piece, gbuf, roww, colw, pbuf, wst):
    for lh in range(2):
        tile = piece * 2 + lh
        wide = lanes(tile, 128)
        gc = slice(128 * lh, 128 * lh + 128)
        for rh in range(2):
            rows = slice(32 * rh, 32 * rh + 32)
            zr, zi = 0.0, 0.0
            for j in range(2):
                sw, cw = wave_sincos(j, rows, tile, roww, colw)
                at = [256 * j + 64 * n + 32 * rh for n in range(4)]
                g = [gbuf[lt, x : x + 32, gc] for x in at]
                zr = zr + (cw * g[0] + sw * g[3])
                zi = zi + (cw * g[1] - sw * g[2])
            w = pbuf[0, rows, wide] * zi - pbuf[1, rows, wide] * zr
            high = w.astype(BF16)
            wst[32 * rh : 32 * rh + 32, wide] = high
            wst[64 + 32 * rh : 96 + 32 * rh, wide] = (w - high.astype(F32)).astype(BF16)


def backward(chunk, leftt, table, gbuf, roww, colw, pbuf, wst):
    count = BCHUNK // 256
    for lt in range(count + 1):
        piece = chunk * count + lt
        if lt < count:
            gbuf[lt] = jnp.dot(leftt[...], table[:, lanes(piece, 256)], preferred_element_type=F32)
        if lt > 0:
            weights(lt - 1, piece - 1, gbuf, roww, colw, pbuf, wst)


def segment_sums(tabs, wst, pick, ulow, pre0, pre1, sbuf, pack):
    row, col = iota((256, 512), 0), iota((256, 512), 1)
    at = lax.rem(row, 128)
    to = jnp.where(col < 256, lax.rem(col, 128), 127)
    weight = jnp.where(lax.rem(col, 256) < 128, 1.0, at.astype(F32))
    tri = jnp.where(at <= to, weight, 0.0).astype(BF16)

    c0 = jnp.concatenate([tabs[t, 2:3, :] for t in range(SROWS)], axis=0)
    c1 = jnp.concatenate([tabs[t, 3:4, :] for t in range(SROWS)], axis=0)
    tile0 = jnp.floor(c0 * (1.0 / 128.0))
    tile1 = jnp.floor(c1 * (1.0 / 128.0))
    in0 = c0 - 128.0 * tile0 - 1.0
    idx0 = jnp.maximum(in0, 0.0).astype(jnp.int32)
    idx1 = (c1 - 128.0 * tile1).astype(jnp.int32)
    some = in0 >= 0.0
    middle = 0.5 * (c0 + c1)

    def row_sums(k, carry):
        u = jnp.dot(pick[0:48, :], wst[:, lanes(k, 1024)], preferred_element_type=F32)
        parts = []
        for lt in range(8):
            gc = slice(128 * lt, 128 * lt + 128)
            parts += [u[0:16, gc], u[16:32, gc] + u[32:48, gc]]
        u = jnp.concatenate(parts, axis=0)
        high = u.astype(BF16)
        low = (u - high.astype(F32)).astype(BF16)
        ulow[pl.ds(pl.multiple_of(k * 256, 256), 256), :] = jnp.concatenate([high, low], axis=1)
        return carry
    lax.fori_loop(0, TILES // 8, row_sums, 0, unroll=4)

    def prefix(k, pre):
        rows = pl.ds(pl.multiple_of(k * 256, 256), 256)
        pre[...] = jnp.dot(ulow[rows, :], tri, preferred_element_type=F32)

    def edges(k, pre, sums):
        sums = list(sums)
        for lt in range(8):
            tile = (k * 8 + lt).astype(F32)
            last1, last0 = tile1 == tile, tile0 == tile
            over1, over0 = tile1 > tile, tile0 > tile
            diffs = []
            for half, at in ((0, 0), (1, 0), (0, 16)):
                rows = slice(32 * lt + at, 32 * lt + at + 16)
                a = pre[rows, 128 * half : 128 * half + 128]
                whole = pre[rows, 128 * half + 256 : 128 * half + 384]
                g1 = jnp.take_along_axis(a, idx1, axis=1)
                g0 = jnp.where(some, jnp.take_along_axis(a, idx0, axis=1), 0.0)
                upto1 = jnp.where(last1, g1, jnp.where(over1, whole, 0.0))
                upto0 = jnp.where(last0, g0, jnp.where(over0, whole, 0.0))
                diffs.append(upto1 - upto0)
            sums[0] = sums[0] + diffs[0]
            sums[1] = sums[1] + (diffs[1] + (128.0 * tile - middle) * diffs[0])
            sums[2] = sums[2] + diffs[2]
        return tuple(sums)

    pre1[...] = jnp.zeros_like(pre1)

    def pair(m, sums):
        prefix(2 * m, pre0)
        sums = edges(2 * m - 1, pre1, sums)
        prefix(2 * m + 1, pre1)
        return edges(2 * m, pre0, sums)
    zero = jnp.zeros((SROWS, 128), F32)
    sums = lax.fori_loop(0, TILES // 16, pair, (zero, zero, zero))
    s0, s1, s2 = edges(jnp.int32(TILES // 8 - 1), pre1, sums)
    keep = iota((SROWS, 128), 1) < PER_ROW
    s1 = s1 / (0.5 * (c1 - c0 + 1.0))
    s0, s1, s2 = [jnp.where(keep, v, 0.0) for v in (s0, s1, s2)]
    sbuf[...] = jnp.zeros_like(sbuf)
    for t in range(SROWS):
        sbuf[t, 0:1, :] = s0[t : t + 1]
        sbuf[t, 1:2, :] = s1[t : t + 1]
        sbuf[t, 2:3, :] = s2[t : t + 1]

    packed = [jnp.zeros((8, 128), F32) for _ in range(10)]
    lane = iota((8, 128), 1)
    for t in range(SROWS):
        first, off = divmod(PER_ROW * t, 128)
        turned = pltpu.roll(sbuf[t], off, 1) if off else sbuf[t]
        packed[first] = packed[first] + jnp.where(lane >= off, turned, 0.0)
        if off + PER_ROW > 128:
            packed[first + 1] = packed[first + 1] + jnp.where(lane < off, turned, 0.0)
    for q in range(3):
        for k in range(10):
            p, r = divmod(q * 10 + k, 8)
            pack[p, r : r + 1, :] = packed[k][q : q + 1, :]
    pack[3, 6:8, :] = jnp.zeros((2, 128), F32)


def remote(src, dst, ssem, rsem, where):
    return pltpu.make_async_remote_copy(src_ref=src, dst_ref=dst, send_sem=ssem, recv_sem=rsem,
                                        device_id=where, device_id_type=MESH)


def each(count, fn):
    def step(o, carry):
        fn(o)
        return carry
    lax.fori_loop(1, count, step, 0)


def kernel(normf, scale, amp_hbm, seg_hbm, box_hbm, coef_hbm, freq_ref, pamp_ref, meas_hbm, ctab_hbm, rtab_hbm,
           out_ref, box_ref, coef_ref, meas_ref, amp, seg, ctab, rtab, flat, tabs, rowt, base, pick, roww, colw, pbuf, eb0, eb1, acc, ysc,
           pay, recv, lhs, hs, ms, hpay, hid, left, leftt, gbuf, wst, ulow, pre0, pre1, sbuf, pack,
           got_a, mine_b, got_b, mine_c, got_c, lsem, tsem, osem, ssem, rsem, asem, bsem, csem):
    band = lax.axis_index("band")
    me = lax.axis_index("row")
    core = lax.rem(me, 2)
    chip = me // 2
    row0 = me * ROWS

    def loads(i):
        cols = lanes(i, CHUNK)
        return [pltpu.make_async_copy(seg_hbm.at[:, cols], seg.at[:, cols], lsem.at[0, i]),
                pltpu.make_async_copy(amp_hbm.at[:, cols], amp.at[:, cols], lsem.at[1, i]),
                pltpu.make_async_copy(ctab_hbm.at[band, :, cols], ctab.at[:, cols], lsem.at[2, i])]

    def start_loads(i, carry):
        for copy in loads(i):
            copy.start()
        return carry
    small = [pltpu.make_async_copy(box_hbm, box_ref, osem.at[0]),
             pltpu.make_async_copy(coef_hbm, coef_ref, osem.at[1]),
             pltpu.make_async_copy(meas_hbm, meas_ref, osem.at[2])]
    small[0].start()
    small[1].start()
    lax.fori_loop(0, CHUNKS, start_loads, 0)
    small[2].start()
    table_copy = pltpu.make_async_copy(rtab_hbm.at[band], rtab, tsem)
    table_copy.start()

    barrier = pltpu.get_barrier_semaphore()

    def greet(where):
        pl.semaphore_signal(barrier, inc=1, device_id=where, device_id_type=MESH)
    each(PEERS, lambda o: greet((band, lax.rem(me + o, PEERS))))
    for o in range(1, YS):
        for c in range(2):
            greet((lax.rem(band + o, YS), chip * 2 + c))

    wave_setup(row0, freq_ref, pamp_ref, roww, colw)
    def send(j, source, target):
        def one(o):
            peer = lax.rem(me + o, PEERS)
            remote(source.at[j, peer], target.at[j, me], ssem.at[j, peer], rsem.at[j, me], (band, peer)).start()
        each(PEERS, one)

    def await_all(j, source, target):
        def one(o):
            peer = lax.rem(me + o, PEERS)
            remote(source.at[j, peer], target.at[j, peer], ssem.at[j, peer], rsem.at[j, peer], (band, peer)).wait()
        each(PEERS, one)

    for j in range(2):
        acc[...] = jnp.zeros_like(acc)
        eb1[...] = jnp.zeros_like(eb1)

        def forward(i, carry):
            if j == 0:
                for copy in loads(i):
                    copy.wait()

                @pl.when(i == 0)
                def _():
                    small[0].wait()
                    small[1].wait()
                    segment_setup(row0, box_ref, coef_ref, seg, flat, tabs, rowt, base, pick)
            before = jnp.maximum(2 * i - 1, 0)
            fields(j, 2 * i, eb0, amp, seg, rowt, base, roww, colw, pbuf)
            acc[...] += lax.dot_general(ctab[:, lanes(before, SUB)], eb1[...], NT, preferred_element_type=F32)
            fields(j, 2 * i + 1, eb1, amp, seg, rowt, base, roww, colw, pbuf)
            acc[...] += lax.dot_general(ctab[:, lanes(2 * i, SUB)], eb0[...], NT, preferred_element_type=F32)
            return carry
        lax.fori_loop(0, CHUNKS, forward, 0)
        acc[...] += lax.dot_general(ctab[:, NC - SUB : NC], eb1[...], NT, preferred_element_type=F32)
        column_sums(acc, pay.at[j], ysc)
        if j == 0:
            pl.semaphore_wait(barrier, PEERS - 1 + 2 * (YS - 1))
        send(j, pay, recv)
        recv[j, me] = pay[j, me]

    small[2].wait()
    for b in range(2):
        for v in range(OWN):
            source = jnp.where(me < PEERS // 2, v, OWN - 1 - v)
            for k in range(PROBES):
                at = b * 64 + 8 * v + 2 * k
                ms[0, at : at + 2, :] = meas_ref[b, source, k, :, :HALF]
                ms[1, at : at + 2, :] = meas_ref[b, source, k, :, HALF:]
    flip = (iota((128, 128), 0) + iota((128, 128), 1) == 127).astype(F32)
    ms[1] = jnp.dot(ms[1], flip, precision=lax.Precision.HIGHEST, preferred_element_type=F32)
    table_copy.wait()
    for j in range(2):
        await_all(j, pay, recv)
        focal_part(j, normf, recv.at[j], hpay.at[j], lhs, hs, ms, rtab)
        def one(o):
            peer = lax.rem(me + o, PEERS)
            remote(hpay.at[j, peer], hid.at[j, me], ssem.at[2 + j, peer], rsem.at[2 + j, me], (band, peer)).start()
        each(PEERS, one)
        hid[j, me] = hpay[j, me]

    for j in range(2):
        def done(o):
            peer = lax.rem(me + o, PEERS)
            remote(hpay.at[j, peer], hid.at[j, peer], ssem.at[2 + j, peer], rsem.at[2 + j, peer],
                   (band, peer)).wait()
        each(PEERS, done)
        hidden_left(j, hid.at[j], left, leftt)

    def back(i, carry):
        backward(i, leftt, ctab, gbuf, roww, colw, pbuf, wst)
        return carry
    lax.fori_loop(0, NC // BCHUNK, back, 0)

    segment_sums(tabs, wst, pick, ulow, pre0, pre1, sbuf, pack)

    near = band * 2 + core

    def near_copy(o, slot):
        peer = lax.rem(near + o, 2 * YS)
        to = peer // 2
        at = near if slot == "mine" else peer
        return remote(pack.at[to], got_a.at[at], asem.at[0, peer], asem.at[1, at],
                      (to, chip * 2 + lax.rem(peer, 2)))
    each(2 * YS, lambda o: near_copy(o, "mine").start())
    got_a[near] = pack[band]
    each(2 * YS, lambda o: near_copy(o, "peer").wait())
    total = got_a[0]
    for k in range(1, 2 * YS):
        total = total + got_a[k]
    mine_b[...] = total

    def far_copy(o, slot):
        peer = lax.rem(chip + o, CHIPS)
        at = chip if slot == "mine" else peer
        return remote(mine_b, got_b.at[at], bsem.at[0, peer], bsem.at[1, at], (band, peer * 2 + core))
    each(CHIPS, lambda o: far_copy(o, "mine").start())
    got_b[chip] = mine_b[...]
    each(CHIPS, lambda o: far_copy(o, "peer").wait())
    total = got_b[0]
    for k in range(1, CHIPS):
        total = total + got_b[k]
    mine_c[...] = total * scale

    def share_copy(o, slot):
        peer = lax.rem(band + o, YS)
        at = band if slot == "mine" else peer
        return remote(mine_c, got_c.at[at], csem.at[0, peer], csem.at[1, at], (peer, me))
    each(YS, lambda o: share_copy(o, "mine").start())
    got_c[band] = mine_c[...]
    each(YS, lambda o: share_copy(o, "peer").wait())
    for q in range(3):
        for k in range(10):
            p, r = divmod(q * 10 + k, 8)
            width = min(128, SEG - 128 * k)
            out_ref[q : q + 1, 128 * k : 128 * k + width] = got_c[p, r : r + 1, :width]


VM = pl.BlockSpec(memory_space=pltpu.VMEM)
SM = pl.BlockSpec(memory_space=pltpu.SMEM)
HBM = pl.BlockSpec(memory_space=pl.ANY)
LIMIT = 60 * 1024 * 1024


def solution(mesh):
    ctable = jnp.asarray(column_table())
    rtable = jnp.asarray(row_table())
    root = math.sqrt(NR * NC)

    def body(amplitude, seg_map, seg_box, seg_coeffs, probe_freq, probe_amp, measured):
        dma = pltpu.SemaphoreType.DMA
        return pl.pallas_call(
            functools.partial(kernel, 1.0 / root, 2.0 / root / (BANDS * PROBES)),
            in_specs=[HBM, HBM, HBM, HBM, SM, SM, HBM, HBM, HBM],
            out_specs=VM,
            out_shape=jax.ShapeDtypeStruct((3, SEG), F32),
            scratch_shapes=[
                pltpu.VMEM((4, SEG), jnp.int32),
                pltpu.VMEM((3, SEG), F32),
                pltpu.VMEM((2, OWN, PROBES, 2, M), F32),
                pltpu.VMEM((ROWS, NC), BF16),
                pltpu.VMEM((ROWS, NC), jnp.int32),
                pltpu.VMEM((4 * HALF, NC), BF16),
                pltpu.VMEM((4 * HALF, NR), BF16),
                pltpu.VMEM((8, 1280), F32),
                pltpu.VMEM((SROWS, 8, 128), F32),
                pltpu.VMEM((3, ROWS, 128), F32),
                pltpu.VMEM((ROWS, 128), jnp.int32),
                pltpu.VMEM((128, 128), BF16),
                pltpu.VMEM((4, ROWS, 128), F32),
                pltpu.VMEM((4, TILES, 128), F32),
                pltpu.VMEM((2, ROWS, NC), F32),
                pltpu.VMEM((256, SUB), BF16),
                pltpu.VMEM((256, SUB), BF16),
                pltpu.VMEM((4 * HALF, 256), F32),
                pltpu.VMEM((2, 2, HALF, 256), F32),
                pltpu.VMEM((2, PEERS, 16, 256), BF16),
                pltpu.VMEM((2, PEERS, 16, 256), BF16),
                pltpu.VMEM((2, 32, NR), F32),
                pltpu.VMEM((2, 32, NR), F32),
                pltpu.VMEM((2, 128, HALF), F32),
                pltpu.VMEM((2, PEERS, 16, 256), BF16),
                pltpu.VMEM((2, PEERS, 16, 256), BF16),
                pltpu.VMEM((4 * HALF, 256), F32),
                pltpu.VMEM((512, 4 * HALF), BF16),
                pltpu.VMEM((BCHUNK // 256, 512, 256), F32),
                pltpu.VMEM((128, NC), BF16),
                pltpu.VMEM((TILES * 32, 256), BF16),
                pltpu.VMEM((256, 512), F32),
                pltpu.VMEM((256, 512), F32),
                pltpu.VMEM((SROWS, 8, 128), F32),
                pltpu.VMEM((4, 8, 128), F32),
                pltpu.VMEM((2 * YS, 8, 128), F32),
                pltpu.VMEM((8, 128), F32),
                pltpu.VMEM((CHIPS, 8, 128), F32),
                pltpu.VMEM((8, 128), F32),
                pltpu.VMEM((YS, 8, 128), F32),
                dma((3, CHUNKS)),
                dma,
                dma((3,)),
                dma((4, PEERS)),
                dma((4, PEERS)),
                dma((2, 2 * YS)),
                dma((2, CHIPS)),
                dma((2, YS)),
            ],
            compiler_params=pltpu.CompilerParams(collective_id=0, has_side_effects=True, vmem_limit_bytes=LIMIT),
            name="gradient",
        )(amplitude, seg_map, seg_box, seg_coeffs, probe_freq, probe_amp, measured, ctable, rtable)

    in_specs = (P("row", None), P("row", None), P(), P(), P(), P(), P("band", "row", None, None, None))
    return jax.shard_map(body, mesh=mesh, in_specs=in_specs, out_specs=P(), check_vma=False)
```

```python
import functools
import math

import jax
import jax.numpy as jnp
import ml_dtypes
import numpy as np
from jax import lax
from jax.experimental import pallas as pl
from jax.experimental.pallas import tpu as pltpu
from jax.sharding import PartitionSpec as P

NC = 8192
NR = 2048
M = 256
BANDS = 8
PROBES = 4
SEG = 1200
SROWS = 16
PER_ROW = SEG // SROWS
HALF = M // 2
ROWS = 64
PEERS = 32
OWN = 8
SPREAD = 0.2
SAMPLING = 0.5
MESH = pl.DeviceIdType.MESH
F32 = jnp.float32
BF16 = jnp.bfloat16
SUB = 512
CHUNK = 1024
FOLD = NC // 2
CHUNKS = FOLD // CHUNK
BCHUNK = 1024
TILES = NC // 128
CHIPS = 16
YS = 4
NT = (((1,), (1,)), ((), ()))


def series(fn, top, count):
    cheb = np.polynomial.chebyshev.Chebyshev.interpolate(
        lambda s: fn(np.sqrt(s)), count - 1, domain=[0.0, top * top]
    )
    return [float(v) for v in cheb.convert(kind=np.polynomial.Polynomial).coef]


def sinc(x):
    return np.sinc(x / np.pi)


SIN_PHASE = series(sinc, 3.02, 6)
COS_PHASE = series(np.cos, 3.02, 7)
SIN_WAVE = series(sinc, 0.81, 4)
COS_WAVE = series(np.cos, 0.81, 4)
SIN_TURN = series(lambda x: 2 * np.pi * np.sinc(2 * x), 0.5, 8)
COS_TURN = series(lambda x: np.cos(2 * np.pi * x), 0.5, 8)


def poly(coefs, s):
    total = jnp.full_like(s, coefs[-1])
    for value in coefs[-2::-1]:
        total = total * s + value
    return total


def turn_sincos(turns):
    part = turns - jnp.floor(turns + 0.5)
    square = part * part
    return part * poly(SIN_TURN, square), poly(COS_TURN, square)


def half_tables(coords, order):
    focal = (np.arange(HALF, dtype=np.float32) - np.float32(M / 2) + np.float32(0.5)) * np.float32(SAMPLING)
    base = (np.float32(2.0 * math.pi) * focal)[:, None] * coords[None, :]
    out = []
    for band in range(BANDS):
        ratio = np.float32(1.0) + np.float32(SPREAD) * (
            (np.float32(band) + np.float32(0.5)) / np.float32(BANDS) - np.float32(0.5)
        )
        angle = (base / ratio).astype(np.float64)
        out.append(np.stack([np.cos(angle), np.sin(angle)]).astype(np.float32).astype(ml_dtypes.bfloat16))
    return np.stack(out)


def column_table():
    coords = (np.arange(NC, dtype=np.float32) + np.float32(0.5)) / np.float32(NC) - np.float32(0.5)
    tables = half_tables(coords, 0)[..., :FOLD].reshape(4, 2, 2, HALF, FOLD)
    return tables.transpose(0, 2, 1, 3, 4).reshape(4, 4 * HALF, FOLD)


def row_table():
    coords = (np.arange(NR, dtype=np.float32) + np.float32(0.5)) / np.float32(NC) - np.float32(NR / (2.0 * NC))
    return half_tables(coords, 0).reshape(4, 4 * HALF, NR)


def lane_sign(first, second):
    lane = lax.broadcasted_iota(jnp.int32, (1, 128), 1)
    return jnp.where(lane < 64, F32(first), F32(second))


def iota(shape, dim):
    return lax.broadcasted_iota(jnp.int32, shape, dim)


def wave_setup(row0, freq_ref, amp_ref, roww, colw):
    rows = (iota((ROWS, 128), 0) + row0).astype(F32)
    place = (rows + 0.5) / NC - NR / (2.0 * NC)
    cols = (iota((TILES, 128), 0) * 128 + iota((TILES, 128), 1)).astype(F32)
    across = (cols + 0.5) / NC - 0.5
    for j in range(2):
        s, c = turn_sincos(place * freq_ref[j, 1].astype(F32))
        roww[2 * j] = s * amp_ref[j]
        roww[2 * j + 1] = c * amp_ref[j]
        s, c = turn_sincos(across * freq_ref[j, 0].astype(F32))
        colw[2 * j] = s
        colw[2 * j + 1] = c


def wave_sincos(j, rows, tile, roww, colw):
    one = roww[2 * j + 1, rows, :] * colw[2 * j, pl.ds(tile, 1), :]
    two = roww[2 * j, rows, :] * colw[2 * j + 1, pl.ds(tile, 1), :]
    out = []
    for wave in (two + one, two - one):
        square = wave * wave
        out.append((wave * poly(SIN_WAVE, square), poly(COS_WAVE, square)))
    return out


def lanes(index, width):
    return pl.ds(pl.multiple_of(index * width, width), width)


def segment_setup(row0, box_ref, coef_ref, seg, flat, tabs, rowt, base, pick):
    flat[...] = jnp.zeros_like(flat)
    flat[0:4, 0:SEG] = box_ref[...].astype(F32)
    flat[4:7, 0:SEG] = coef_ref[...]
    lane = iota((8, 128), 1)
    for t in range(SROWS):
        first, off = divmod(PER_ROW * t, 128)
        one = flat[:, 128 * first : 128 * first + 128]
        if off:
            two = flat[:, 128 * first + 128 : 128 * first + 256]
            one = jnp.where(lane < 128 - off, pltpu.roll(one, 128 - off, 1), pltpu.roll(two, 128 - off, 1))
        tabs[t] = one
    column = seg[:, 0:1]
    trow = jnp.zeros((ROWS, 1), jnp.int32)
    for m in range(1, SROWS):
        trow = trow + (column >= PER_ROW * m).astype(jnp.int32)
    trow = jnp.broadcast_to(trow, (ROWS, 128))
    base[...] = trow * PER_ROW
    rows = (iota((ROWS, 128), 0) + row0).astype(F32)
    alpha, beta, middle, down_all = [jnp.zeros((ROWS, 128), F32) for _ in range(4)]
    for t in range(SROWS):
        r0, r1, c0, c1 = [tabs[t, q : q + 1, :] for q in range(4)]
        piston, tip, tilt = [tabs[t, q : q + 1, :] for q in range(4, 7)]
        here = trow == t
        down = (rows - 0.5 * (r0 + r1)) / (0.5 * (r1 - r0 + 1.0))
        alpha = jnp.where(here, piston + tilt * down, alpha)
        beta = jnp.where(here, tip / (0.5 * (c1 - c0 + 1.0)), beta)
        middle = jnp.where(here, 0.5 * (c0 + c1), middle)
        down_all = jnp.where(here, down, down_all)
    rowt[0] = alpha
    rowt[1] = beta
    rowt[2] = middle
    lane = iota((ROWS, 128), 1)
    down_all = jnp.broadcast_to(down_all[:, 0:1], (ROWS, 128))
    high = down_all.astype(BF16).astype(F32)
    which = jnp.where(lane < 16, 1.0, jnp.where(lane < 32, high, jnp.where(lane < 48, down_all - high, 0.0)))
    chosen = jnp.where(lax.rem(lane, 16) == trow, which, 0.0)
    pick[...] = jnp.concatenate([chosen, chosen], axis=0).T.astype(BF16)


def fields(j, chunk, ebuf, amp, seg, rowt, base, roww, colw, pbuf):
    lane = iota((32, 128), 1)
    for lt in range(SUB // 128):
        tile = chunk * (SUB // 128) + lt
        cols = slice(128 * lt, 128 * lt + 128)
        for rh in range(2):
            rows = slice(32 * rh, 32 * rh + 32)
            both = []
            for side in range(2):
                at = tile if side == 0 else TILES - 1 - tile
                wide = lanes(at, 128)
                if j == 0:
                    cf = (lane + at * 128).astype(F32)
                    idx = seg[rows, wide] - base[rows, :]
                    a = jnp.take_along_axis(rowt[0, rows, :], idx, axis=1)
                    b = jnp.take_along_axis(rowt[1, rows, :], idx, axis=1)
                    m = jnp.take_along_axis(rowt[2, rows, :], idx, axis=1)
                    phase = a + b * (cf - m)
                    mag = amp[rows, wide].astype(F32)
                    if side == 1:
                        phase = jnp.take_along_axis(phase, 127 - lane, axis=1)
                        mag = jnp.take_along_axis(mag, 127 - lane, axis=1)
                    square = phase * phase
                    pr = mag * poly(COS_PHASE, square)
                    pi = mag * (phase * poly(SIN_PHASE, square))
                    pbuf[0, rows, wide] = pr
                    pbuf[1, rows, wide] = pi
                else:
                    pr = pbuf[0, rows, wide]
                    pi = pbuf[1, rows, wide]
                both.append((pr, pi))
            waves = wave_sincos(j, rows, tile, roww, colw)
            for t in range(2):
                f, g = waves[0][1 - t], waves[1][1 - t]
                for o in range(2):
                    one, two = both[0][o] * f, both[1][o] * g
                    at = 128 * t + 64 * o + 32 * rh
                    ebuf[at : at + 32, cols] = (one + two).astype(BF16)
                    ebuf[256 + at : 288 + at, cols] = (one - two).astype(BF16)


def add_dots(acc, ctab, index, ebuf):
    for part in range(2):
        rows = slice(256 * part, 256 * part + 256)
        acc[rows, :] += lax.dot_general(ctab[rows, lanes(index, SUB)], ebuf[rows, :], NT,
                                        preferred_element_type=F32)


def column_sums(acc, pay, ysc):
    plus = lane_sign(1.0, -1.0)
    for b in range(2):
        parts = []
        for t in range(2):
            cols = slice(128 * t, 128 * t + 128)
            c = acc[128 * b : 128 * b + 128, cols]
            s = plus * pltpu.roll(acc[256 + 128 * b : 384 + 128 * b, cols], 64, 1)
            parts.append((c + s, c - s))
        for side in range(2):
            even = parts[0][side]
            odd = plus * pltpu.roll(parts[1][side], 64, 1)
            ysc[side, b, :, 0:128] = even - odd
            ysc[side, b, :, 128:256] = even + odd
    for d in range(PEERS // 2):
        for side in range(2):
            to = d if side == 0 else PEERS - 1 - d
            pay[to] = jnp.concatenate(
                [ysc[side, b, OWN * d : OWN * d + OWN, :] for b in range(2)], axis=0
            ).astype(BF16)


def focal_part(j, normf, recv, hpay, lhs, hs, ms, table):
    low = iota((16, 128), 1) < 64

    def gather(s4, carry):
        for k in range(4):
            s = s4 * 4 + k
            cols = lanes(s, 128)
            for q in range(2):
                one = recv[2 * s, :, 128 * q : 128 * q + 128].astype(F32)
                two = recv[2 * s + 1, :, 128 * q : 128 * q + 128].astype(F32)
                re = jnp.where(low, one, pltpu.roll(two, 64, 1))
                im = jnp.where(low, pltpu.roll(one, 64, 1), two)
                for b in range(2):
                    lhs[b, 16 * q : 16 * q + 8, cols] = re[8 * b : 8 * b + 8]
                    lhs[b, 16 * q + 8 : 16 * q + 16, cols] = im[8 * b : 8 * b + 8]
        return carry
    lax.fori_loop(0, PEERS // 8, gather, 0)

    for b in range(2):
        here = table[256 * b : 256 * b + 256, :]
        parts = lax.dot_general(lhs[b].astype(BF16), here, NT, preferred_element_type=F32)
        rows = []
        for q in range(2):
            re, im = parts[16 * q : 16 * q + 8], parts[16 * q + 8 : 16 * q + 16]
            pieces = []
            for o, (c, s) in enumerate(((re[:, :HALF], im[:, HALF:]), (im[:, :HALF], -re[:, HALF:]))):
                want = pl.ds(b * 64 + 4 * j + 2 * q + o, 8, stride=8)
                one = (c + s) * normf - ms[0, want, :]
                two = (c - s) * normf - ms[1, want, :]
                pieces.append((one + two, one - two))
            (re_e, re_o), (im_e, im_o) = pieces
            rows.append(jnp.concatenate([re_e, -im_o], axis=1))
            rows.append(jnp.concatenate([im_e, re_o], axis=1))
        left = jnp.concatenate(rows, axis=0).astype(BF16)
        hs[b] = jnp.dot(left, here, preferred_element_type=F32)

    low8 = iota((8, 128), 1) < 64

    def spread(s4, carry):
        for k in range(4):
            s = s4 * 4 + k
            cols = lanes(s, 128)
            for q in range(2):
                first, second = [], []
                for b in range(2):
                    re = hs[b, 16 * q : 16 * q + 8, cols]
                    im = hs[b, 16 * q + 8 : 16 * q + 16, cols]
                    first.append(jnp.where(low8, re, pltpu.roll(im, 64, 1)))
                    second.append(jnp.where(low8, pltpu.roll(re, 64, 1), im))
                hpay[2 * s, :, 128 * q : 128 * q + 128] = jnp.concatenate(first, axis=0).astype(BF16)
                hpay[2 * s + 1, :, 128 * q : 128 * q + 128] = jnp.concatenate(second, axis=0).astype(BF16)
        return carry
    lax.fori_loop(0, PEERS // 8, spread, 0)


def hidden_left(j, hid, left, leftt):
    minus = lane_sign(-1.0, 1.0)
    for d in range(PEERS // 2):
        here = hid[d].astype(F32)
        there = hid[PEERS - 1 - d].astype(F32)
        even, odd = here + there, here - there
        e = [even[:, 128 * t : 128 * t + 128] for t in range(2)]
        o = [odd[:, 128 * t : 128 * t + 128] for t in range(2)]
        for t in range(2):
            cols = slice(128 * t, 128 * t + 128)
            es = e[0] + e[1] if t == 0 else e[0] - e[1]
            os = o[0] + o[1] if t == 0 else o[0] - o[1]
            os = minus * pltpu.roll(os, 64, 1)
            for b in range(2):
                left[128 * b + 8 * d : 128 * b + 8 * d + 8, cols] = es[8 * b : 8 * b + 8]
                left[256 + 128 * b + 8 * d : 264 + 128 * b + 8 * d, cols] = os[8 * b : 8 * b + 8]
    leftt[256 * j : 256 * j + 256, :] = left[...].T.astype(BF16)


def weights(lt, piece, gbuf, roww, colw, pbuf, wst):
    for lh in range(2):
        tile = piece * 2 + lh
        gc = slice(128 * lh, 128 * lh + 128)
        for rh in range(2):
            rows = slice(32 * rh, 32 * rh + 32)
            zr, zi = [0.0, 0.0], [0.0, 0.0]
            for j in range(2):
                waves = wave_sincos(j, rows, tile, roww, colw)
                at = [256 * j + 64 * n + 32 * rh for n in range(4)]
                even = [gbuf[lt, 0, x : x + 32, gc] for x in at]
                odd = [gbuf[lt, 1, x : x + 32, gc] for x in at]
                for side in range(2):
                    g = [e + o if side == 0 else e - o for e, o in zip(even, odd)]
                    sw, cw = waves[side]
                    zr[side] = zr[side] + (cw * g[0] + sw * g[3])
                    zi[side] = zi[side] + (cw * g[1] - sw * g[2])
            for side in range(2):
                wide = lanes(tile if side == 0 else TILES - 1 - tile, 128)
                w = pbuf[0, rows, wide] * zi[side] - pbuf[1, rows, wide] * zr[side]
                high = w.astype(BF16)
                wst[32 * rh : 32 * rh + 32, wide] = high
                wst[64 + 32 * rh : 96 + 32 * rh, wide] = (w - high.astype(F32)).astype(BF16)


def backward(chunk, leftt, table, gbuf, roww, colw, pbuf, wst):
    count = BCHUNK // 256
    for lt in range(count + 1):
        piece = chunk * count + lt
        if lt < count:
            for part in range(2):
                ks = slice(256 * part, 256 * part + 256)
                gbuf[lt, part] = jnp.dot(leftt[:, ks], table[ks, lanes(piece, 256)], preferred_element_type=F32)
        if lt > 0:
            weights(lt - 1, piece - 1, gbuf, roww, colw, pbuf, wst)


def prefix_weights(at, col):
    to = jnp.where(col < 256, lax.rem(col, 128), 127)
    weight = jnp.where(lax.rem(col, 256) < 128, 1.0, at.astype(F32))
    return jnp.where(at <= to, weight, 0.0).astype(BF16)


def segment_sums(tabs, wst, pick, ulow, tris, pre0, pre1, sbuf, pack):
    row, col = iota((256, 512), 0), iota((256, 512), 1)
    at = lax.rem(row, 128)
    for side in range(2):
        tris[side] = prefix_weights(at if side == 0 else 127 - at, col)
    c0 = jnp.concatenate([tabs[t, 2:3, :] for t in range(SROWS)], axis=0)
    c1 = jnp.concatenate([tabs[t, 3:4, :] for t in range(SROWS)], axis=0)
    tile0 = jnp.floor(c0 * (1.0 / 128.0))
    tile1 = jnp.floor(c1 * (1.0 / 128.0))
    in0 = c0 - 128.0 * tile0 - 1.0
    idx0 = jnp.maximum(in0, 0.0).astype(jnp.int32)
    idx1 = (c1 - 128.0 * tile1).astype(jnp.int32)
    some = in0 >= 0.0
    middle = 0.5 * (c0 + c1)

    def row_sums(k, carry):
        u = jnp.dot(pick[0:48, :], wst[:, lanes(k, 1024)], preferred_element_type=F32)
        parts = []
        for lt in range(8):
            gc = slice(128 * lt, 128 * lt + 128)
            parts += [u[0:16, gc], u[16:32, gc] + u[32:48, gc]]
        u = jnp.concatenate(parts, axis=0)
        high = u.astype(BF16)
        low = (u - high.astype(F32)).astype(BF16)
        ulow[pl.ds(pl.multiple_of(k * 256, 256), 256), :] = jnp.concatenate([high, low], axis=1)
        return carry
    lax.fori_loop(0, TILES // 8, row_sums, 0, unroll=4)

    def prefix(k, pre):
        rows = pl.ds(pl.multiple_of(k * 256, 256), 256)
        pre[...] = jnp.dot(ulow[rows, :], tris[k // (TILES // 16)], preferred_element_type=F32)

    def edges(k, pre, sums):
        sums = list(sums)
        for lt in range(8):
            tile = (k * 8 + lt).astype(F32)
            last1, last0 = tile1 == tile, tile0 == tile
            over1, over0 = tile1 > tile, tile0 > tile
            diffs = []
            for half, at in ((0, 0), (1, 0), (0, 16)):
                rows = slice(32 * lt + at, 32 * lt + at + 16)
                a = pre[rows, 128 * half : 128 * half + 128]
                whole = pre[rows, 128 * half + 256 : 128 * half + 384]
                g1 = jnp.take_along_axis(a, idx1, axis=1)
                g0 = jnp.where(some, jnp.take_along_axis(a, idx0, axis=1), 0.0)
                upto1 = jnp.where(last1, g1, jnp.where(over1, whole, 0.0))
                upto0 = jnp.where(last0, g0, jnp.where(over0, whole, 0.0))
                diffs.append(upto1 - upto0)
            sums[0] = sums[0] + diffs[0]
            sums[1] = sums[1] + (diffs[1] + (128.0 * tile - middle) * diffs[0])
            sums[2] = sums[2] + diffs[2]
        return tuple(sums)

    pre1[...] = jnp.zeros_like(pre1)

    def pair(m, sums):
        prefix(2 * m, pre0)
        sums = edges(2 * m - 1, pre1, sums)
        prefix(2 * m + 1, pre1)
        return edges(2 * m, pre0, sums)
    zero = jnp.zeros((SROWS, 128), F32)
    sums = lax.fori_loop(0, TILES // 16, pair, (zero, zero, zero))
    s0, s1, s2 = edges(jnp.int32(TILES // 8 - 1), pre1, sums)
    keep = iota((SROWS, 128), 1) < PER_ROW
    s1 = s1 / (0.5 * (c1 - c0 + 1.0))
    s0, s1, s2 = [jnp.where(keep, v, 0.0) for v in (s0, s1, s2)]
    sbuf[...] = jnp.zeros_like(sbuf)
    for t in range(SROWS):
        sbuf[t, 0:1, :] = s0[t : t + 1]
        sbuf[t, 1:2, :] = s1[t : t + 1]
        sbuf[t, 2:3, :] = s2[t : t + 1]

    packed = [jnp.zeros((8, 128), F32) for _ in range(10)]
    lane = iota((8, 128), 1)
    for t in range(SROWS):
        first, off = divmod(PER_ROW * t, 128)
        turned = pltpu.roll(sbuf[t], off, 1) if off else sbuf[t]
        packed[first] = packed[first] + jnp.where(lane >= off, turned, 0.0)
        if off + PER_ROW > 128:
            packed[first + 1] = packed[first + 1] + jnp.where(lane < off, turned, 0.0)
    for q in range(3):
        for k in range(10):
            p, r = divmod(q * 10 + k, 8)
            pack[p, r : r + 1, :] = packed[k][q : q + 1, :]
    pack[3, 6:8, :] = jnp.zeros((2, 128), F32)


def remote(src, dst, ssem, rsem, where):
    return pltpu.make_async_remote_copy(src_ref=src, dst_ref=dst, send_sem=ssem, recv_sem=rsem,
                                        device_id=where, device_id_type=MESH)


def each(count, fn):
    def step(o, carry):
        fn(o)
        return carry
    lax.fori_loop(1, count, step, 0)


def kernel(normf, scale, amp_hbm, seg_hbm, box_hbm, coef_hbm, freq_ref, pamp_ref, meas_hbm, ctab_hbm, rtab_hbm,
           out_ref, box_ref, coef_ref, meas_ref, amp, seg, ctab, rtab, flat, tabs, rowt, base, pick, roww, colw, pbuf, eb0, eb1, acc, ysc,
           pay, recv, lhs, hs, ms, hpay, hid, left, leftt, gbuf, wst, ulow, tris, pre0, pre1, sbuf, pack,
           got_a, mine_b, got_b, mine_c, got_c, lsem, tsem, osem, ssem, rsem, asem, bsem, csem):
    band = lax.axis_index("band")
    me = lax.axis_index("row")
    core = lax.rem(me, 2)
    chip = me // 2
    row0 = me * ROWS

    def loads(i):
        cols, mirror = lanes(i, CHUNK), lanes(2 * CHUNKS - 1 - i, CHUNK)
        return [pltpu.make_async_copy(seg_hbm.at[:, cols], seg.at[:, cols], lsem.at[0, i]),
                pltpu.make_async_copy(seg_hbm.at[:, mirror], seg.at[:, mirror], lsem.at[1, i]),
                pltpu.make_async_copy(amp_hbm.at[:, cols], amp.at[:, cols], lsem.at[2, i]),
                pltpu.make_async_copy(amp_hbm.at[:, mirror], amp.at[:, mirror], lsem.at[3, i]),
                pltpu.make_async_copy(ctab_hbm.at[band, :, cols], ctab.at[:, cols], lsem.at[4, i])]

    def start_loads(i, carry):
        for copy in loads(i):
            copy.start()
        return carry
    small = [pltpu.make_async_copy(box_hbm, box_ref, osem.at[0]),
             pltpu.make_async_copy(coef_hbm, coef_ref, osem.at[1]),
             pltpu.make_async_copy(meas_hbm, meas_ref, osem.at[2])]
    small[0].start()
    small[1].start()
    lax.fori_loop(0, CHUNKS, start_loads, 0)
    small[2].start()
    table_copy = pltpu.make_async_copy(rtab_hbm.at[band], rtab, tsem)
    table_copy.start()

    barrier = pltpu.get_barrier_semaphore()

    def greet(where):
        pl.semaphore_signal(barrier, inc=1, device_id=where, device_id_type=MESH)
    each(PEERS, lambda o: greet((band, lax.rem(me + o, PEERS))))
    for o in range(1, YS):
        for c in range(2):
            greet((lax.rem(band + o, YS), chip * 2 + c))

    wave_setup(row0, freq_ref, pamp_ref, roww, colw)
    def send(j, source, target):
        def one(o):
            peer = lax.rem(me + o, PEERS)
            remote(source.at[j, peer], target.at[j, me], ssem.at[j, peer], rsem.at[j, me], (band, peer)).start()
        each(PEERS, one)

    def await_all(j, source, target):
        def one(o):
            peer = lax.rem(me + o, PEERS)
            remote(source.at[j, peer], target.at[j, peer], ssem.at[j, peer], rsem.at[j, peer], (band, peer)).wait()
        each(PEERS, one)

    for j in range(2):
        acc[...] = jnp.zeros_like(acc)
        eb1[...] = jnp.zeros_like(eb1)

        def forward(i, carry):
            if j == 0:
                for copy in loads(i):
                    copy.wait()

                @pl.when(i == 0)
                def _():
                    small[0].wait()
                    small[1].wait()
                    segment_setup(row0, box_ref, coef_ref, seg, flat, tabs, rowt, base, pick)
            before = jnp.maximum(2 * i - 1, 0)
            fields(j, 2 * i, eb0, amp, seg, rowt, base, roww, colw, pbuf)
            add_dots(acc, ctab, before, eb1)
            fields(j, 2 * i + 1, eb1, amp, seg, rowt, base, roww, colw, pbuf)
            add_dots(acc, ctab, 2 * i, eb0)
            return carry
        lax.fori_loop(0, CHUNKS, forward, 0)
        add_dots(acc, ctab, FOLD // SUB - 1, eb1)
        column_sums(acc, pay.at[j], ysc)
        if j == 0:
            pl.semaphore_wait(barrier, PEERS - 1 + 2 * (YS - 1))
        send(j, pay, recv)
        recv[j, me] = pay[j, me]

    small[2].wait()
    for b in range(2):
        for v in range(OWN):
            source = jnp.where(me < PEERS // 2, v, OWN - 1 - v)
            for k in range(PROBES):
                at = b * 64 + 8 * v + 2 * k
                ms[0, at : at + 2, :] = meas_ref[b, source, k, :, :HALF]
                ms[1, at : at + 2, :] = meas_ref[b, source, k, :, HALF:]
    flip = (iota((128, 128), 0) + iota((128, 128), 1) == 127).astype(F32)
    ms[1] = jnp.dot(ms[1], flip, precision=lax.Precision.HIGHEST, preferred_element_type=F32)
    table_copy.wait()
    for j in range(2):
        await_all(j, pay, recv)
        focal_part(j, normf, recv.at[j], hpay.at[j], lhs, hs, ms, rtab)
        def one(o):
            peer = lax.rem(me + o, PEERS)
            remote(hpay.at[j, peer], hid.at[j, me], ssem.at[2 + j, peer], rsem.at[2 + j, me], (band, peer)).start()
        each(PEERS, one)
        hid[j, me] = hpay[j, me]

    for j in range(2):
        def done(o):
            peer = lax.rem(me + o, PEERS)
            remote(hpay.at[j, peer], hid.at[j, peer], ssem.at[2 + j, peer], rsem.at[2 + j, peer],
                   (band, peer)).wait()
        each(PEERS, done)
        hidden_left(j, hid.at[j], left, leftt)

    def back(i, carry):
        backward(i, leftt, ctab, gbuf, roww, colw, pbuf, wst)
        return carry
    lax.fori_loop(0, FOLD // BCHUNK, back, 0)

    segment_sums(tabs, wst, pick, ulow, tris, pre0, pre1, sbuf, pack)

    near = band * 2 + core

    def near_copy(o, slot):
        peer = lax.rem(near + o, 2 * YS)
        to = peer // 2
        at = near if slot == "mine" else peer
        return remote(pack.at[to], got_a.at[at], asem.at[0, peer], asem.at[1, at],
                      (to, chip * 2 + lax.rem(peer, 2)))
    each(2 * YS, lambda o: near_copy(o, "mine").start())
    got_a[near] = pack[band]
    each(2 * YS, lambda o: near_copy(o, "peer").wait())
    total = got_a[0]
    for k in range(1, 2 * YS):
        total = total + got_a[k]
    mine_b[...] = total

    def far_copy(o, slot):
        peer = lax.rem(chip + o, CHIPS)
        at = chip if slot == "mine" else peer
        return remote(mine_b, got_b.at[at], bsem.at[0, peer], bsem.at[1, at], (band, peer * 2 + core))
    each(CHIPS, lambda o: far_copy(o, "mine").start())
    got_b[chip] = mine_b[...]
    each(CHIPS, lambda o: far_copy(o, "peer").wait())
    total = got_b[0]
    for k in range(1, CHIPS):
        total = total + got_b[k]
    mine_c[...] = total * scale

    def share_copy(o, slot):
        peer = lax.rem(band + o, YS)
        at = band if slot == "mine" else peer
        return remote(mine_c, got_c.at[at], csem.at[0, peer], csem.at[1, at], (peer, me))
    each(YS, lambda o: share_copy(o, "mine").start())
    got_c[band] = mine_c[...]
    each(YS, lambda o: share_copy(o, "peer").wait())
    for q in range(3):
        for k in range(10):
            p, r = divmod(q * 10 + k, 8)
            width = min(128, SEG - 128 * k)
            out_ref[q : q + 1, 128 * k : 128 * k + width] = got_c[p, r : r + 1, :width]


VM = pl.BlockSpec(memory_space=pltpu.VMEM)
SM = pl.BlockSpec(memory_space=pltpu.SMEM)
HBM = pl.BlockSpec(memory_space=pl.ANY)
LIMIT = 60 * 1024 * 1024


def solution(mesh):
    ctable = jnp.asarray(column_table())
    rtable = jnp.asarray(row_table())
    root = math.sqrt(NR * NC)

    def body(amplitude, seg_map, seg_box, seg_coeffs, probe_freq, probe_amp, measured):
        dma = pltpu.SemaphoreType.DMA
        return pl.pallas_call(
            functools.partial(kernel, 1.0 / root, 2.0 / root / (BANDS * PROBES)),
            in_specs=[HBM, HBM, HBM, HBM, SM, SM, HBM, HBM, HBM],
            out_specs=VM,
            out_shape=jax.ShapeDtypeStruct((3, SEG), F32),
            scratch_shapes=[
                pltpu.VMEM((4, SEG), jnp.int32),
                pltpu.VMEM((3, SEG), F32),
                pltpu.VMEM((2, OWN, PROBES, 2, M), F32),
                pltpu.VMEM((ROWS, NC), BF16),
                pltpu.VMEM((ROWS, NC), jnp.int32),
                pltpu.VMEM((4 * HALF, FOLD), BF16),
                pltpu.VMEM((4 * HALF, NR), BF16),
                pltpu.VMEM((8, 1280), F32),
                pltpu.VMEM((SROWS, 8, 128), F32),
                pltpu.VMEM((3, ROWS, 128), F32),
                pltpu.VMEM((ROWS, 128), jnp.int32),
                pltpu.VMEM((128, 128), BF16),
                pltpu.VMEM((4, ROWS, 128), F32),
                pltpu.VMEM((4, TILES, 128), F32),
                pltpu.VMEM((2, ROWS, NC), F32),
                pltpu.VMEM((512, SUB), BF16),
                pltpu.VMEM((512, SUB), BF16),
                pltpu.VMEM((4 * HALF, 256), F32),
                pltpu.VMEM((2, 2, HALF, 256), F32),
                pltpu.VMEM((2, PEERS, 16, 256), BF16),
                pltpu.VMEM((2, PEERS, 16, 256), BF16),
                pltpu.VMEM((2, 32, NR), F32),
                pltpu.VMEM((2, 32, NR), F32),
                pltpu.VMEM((2, 128, HALF), F32),
                pltpu.VMEM((2, PEERS, 16, 256), BF16),
                pltpu.VMEM((2, PEERS, 16, 256), BF16),
                pltpu.VMEM((4 * HALF, 256), F32),
                pltpu.VMEM((512, 4 * HALF), BF16),
                pltpu.VMEM((BCHUNK // 256, 2, 512, 256), F32),
                pltpu.VMEM((128, NC), BF16),
                pltpu.VMEM((TILES * 32, 256), BF16),
                pltpu.VMEM((2, 256, 512), BF16),
                pltpu.VMEM((256, 512), F32),
                pltpu.VMEM((256, 512), F32),
                pltpu.VMEM((SROWS, 8, 128), F32),
                pltpu.VMEM((4, 8, 128), F32),
                pltpu.VMEM((2 * YS, 8, 128), F32),
                pltpu.VMEM((8, 128), F32),
                pltpu.VMEM((CHIPS, 8, 128), F32),
                pltpu.VMEM((8, 128), F32),
                pltpu.VMEM((YS, 8, 128), F32),
                dma((5, CHUNKS)),
                dma,
                dma((3,)),
                dma((4, PEERS)),
                dma((4, PEERS)),
                dma((2, 2 * YS)),
                dma((2, CHIPS)),
                dma((2, YS)),
            ],
            compiler_params=pltpu.CompilerParams(collective_id=0, has_side_effects=True, vmem_limit_bytes=LIMIT),
            name="gradient",
        )(amplitude, seg_map, seg_box, seg_coeffs, probe_freq, probe_amp, measured, ctable, rtable)

    in_specs = (P("row", None), P("row", None), P(), P(), P(), P(), P("band", "row", None, None, None))
    return jax.shard_map(body, mesh=mesh, in_specs=in_specs, out_specs=P(), check_vma=False)
```

```python
import functools
import math

import jax
import jax.numpy as jnp
import ml_dtypes
import numpy as np
from jax import lax
from jax.experimental import pallas as pl
from jax.experimental.pallas import tpu as pltpu
from jax.sharding import PartitionSpec as P

NC = 8192
NR = 2048
M = 256
BANDS = 8
PROBES = 4
SEG = 1200
SROWS = 16
PER_ROW = SEG // SROWS
HALF = M // 2
ROWS = 64
PEERS = 32
OWN = 8
SPREAD = 0.2
SAMPLING = 0.5
MESH = pl.DeviceIdType.MESH
F32 = jnp.float32
BF16 = jnp.bfloat16
STEP = 64
SUB = 512
CHUNK = 1024
FOLD = NC // 2
CHUNKS = FOLD // CHUNK
BCHUNK = 1024
TILES = NC // 128
CHIPS = 16
YS = 4
NT = (((1,), (1,)), ((), ()))


def series(fn, top, count):
    cheb = np.polynomial.chebyshev.Chebyshev.interpolate(
        lambda s: fn(np.sqrt(s)), count - 1, domain=[0.0, top * top]
    )
    return [float(v) for v in cheb.convert(kind=np.polynomial.Polynomial).coef]


def sinc(x):
    return np.sinc(x / np.pi)


SIN_PHASE = series(sinc, 3.02, 6)
COS_PHASE = series(np.cos, 3.02, 7)
SIN_WAVE = series(sinc, 0.81, 4)
COS_WAVE = series(np.cos, 0.81, 4)
SIN_TURN = series(lambda x: 2 * np.pi * np.sinc(2 * x), 0.5, 8)
COS_TURN = series(lambda x: np.cos(2 * np.pi * x), 0.5, 8)


def poly(coefs, s):
    total = jnp.full_like(s, coefs[-1])
    for value in coefs[-2::-1]:
        total = total * s + value
    return total


def turn_sincos(turns):
    part = turns - jnp.floor(turns + 0.5)
    square = part * part
    return part * poly(SIN_TURN, square), poly(COS_TURN, square)


def half_tables(coords, order):
    focal = (np.arange(HALF, dtype=np.float32) - np.float32(M / 2) + np.float32(0.5)) * np.float32(SAMPLING)
    base = (np.float32(2.0 * math.pi) * focal)[:, None] * coords[None, :]
    out = []
    for band in range(BANDS):
        ratio = np.float32(1.0) + np.float32(SPREAD) * (
            (np.float32(band) + np.float32(0.5)) / np.float32(BANDS) - np.float32(0.5)
        )
        angle = (base / ratio).astype(np.float64)
        out.append(np.stack([np.cos(angle), np.sin(angle)]).astype(np.float32).astype(ml_dtypes.bfloat16))
    return np.stack(out)


def column_table():
    coords = (np.arange(NC, dtype=np.float32) + np.float32(0.5)) / np.float32(NC) - np.float32(0.5)
    tables = half_tables(coords, 0)[..., :FOLD].reshape(4, 2, 2, HALF, FOLD)
    return tables.transpose(0, 2, 1, 3, 4).reshape(4, 4 * HALF, FOLD)


def row_table():
    coords = (np.arange(NR, dtype=np.float32) + np.float32(0.5)) / np.float32(NC) - np.float32(NR / (2.0 * NC))
    return half_tables(coords, 0).reshape(4, 4 * HALF, NR)


def lane_sign(first, second):
    lane = lax.broadcasted_iota(jnp.int32, (1, 128), 1)
    return jnp.where(lane < 64, F32(first), F32(second))


def iota(shape, dim):
    return lax.broadcasted_iota(jnp.int32, shape, dim)


def wave_setup(row0, freq_ref, amp_ref, roww, colw):
    rows = (iota((ROWS, 128), 0) + row0).astype(F32)
    place = (rows + 0.5) / NC - NR / (2.0 * NC)
    cols = (iota((TILES, 128), 0) * 128 + iota((TILES, 128), 1)).astype(F32)
    across = (cols + 0.5) / NC - 0.5
    for j in range(2):
        s, c = turn_sincos(place * freq_ref[j, 1].astype(F32))
        roww[2 * j] = s * amp_ref[j]
        roww[2 * j + 1] = c * amp_ref[j]
        s, c = turn_sincos(across * freq_ref[j, 0].astype(F32))
        colw[2 * j] = s
        colw[2 * j + 1] = c


def wave_sincos(j, rows, tile, roww, colw):
    one = roww[2 * j + 1, rows, :] * colw[2 * j, pl.ds(tile, 1), :]
    two = roww[2 * j, rows, :] * colw[2 * j + 1, pl.ds(tile, 1), :]
    out = []
    for wave in (two + one, two - one):
        square = wave * wave
        out.append((wave * poly(SIN_WAVE, square), poly(COS_WAVE, square)))
    return out


def lanes(index, width):
    return pl.ds(pl.multiple_of(index * width, width), width)


def segment_setup(row0, box_ref, coef_ref, seg, flat, tabs, rowt, base, pick):
    flat[...] = jnp.zeros_like(flat)
    flat[0:4, 0:SEG] = box_ref[...].astype(F32)
    flat[4:7, 0:SEG] = coef_ref[...]
    lane = iota((8, 128), 1)
    for t in range(SROWS):
        first, off = divmod(PER_ROW * t, 128)
        one = flat[:, 128 * first : 128 * first + 128]
        if off:
            two = flat[:, 128 * first + 128 : 128 * first + 256]
            one = jnp.where(lane < 128 - off, pltpu.roll(one, 128 - off, 1), pltpu.roll(two, 128 - off, 1))
        tabs[t] = one
    column = seg[:, 0:1]
    trow = jnp.zeros((ROWS, 1), jnp.int32)
    for m in range(1, SROWS):
        trow = trow + (column >= PER_ROW * m).astype(jnp.int32)
    trow = jnp.broadcast_to(trow, (ROWS, 128))
    base[...] = trow * PER_ROW
    rows = (iota((ROWS, 128), 0) + row0).astype(F32)
    alpha, beta, middle, down_all = [jnp.zeros((ROWS, 128), F32) for _ in range(4)]
    for t in range(SROWS):
        r0, r1, c0, c1 = [tabs[t, q : q + 1, :] for q in range(4)]
        piston, tip, tilt = [tabs[t, q : q + 1, :] for q in range(4, 7)]
        here = trow == t
        down = (rows - 0.5 * (r0 + r1)) / (0.5 * (r1 - r0 + 1.0))
        alpha = jnp.where(here, piston + tilt * down, alpha)
        beta = jnp.where(here, tip / (0.5 * (c1 - c0 + 1.0)), beta)
        middle = jnp.where(here, 0.5 * (c0 + c1), middle)
        down_all = jnp.where(here, down, down_all)
    rowt[0] = alpha
    rowt[1] = beta
    rowt[2] = middle
    lane = iota((ROWS, 128), 1)
    down_all = jnp.broadcast_to(down_all[:, 0:1], (ROWS, 128))
    high = down_all.astype(BF16).astype(F32)
    which = jnp.where(lane < 16, 1.0, jnp.where(lane < 32, high, jnp.where(lane < 48, down_all - high, 0.0)))
    chosen = jnp.where(lax.rem(lane, 16) == trow, which, 0.0)
    pick[...] = jnp.concatenate([chosen, chosen], axis=0).T.astype(BF16)


def fields(j, chunk, ebuf, amp, seg, rowt, base, roww, colw, pbuf, wbuf):
    lane = iota((STEP, 128), 1)
    for lt in range(SUB // 128):
        tile = chunk * (SUB // 128) + lt
        cols = slice(128 * lt, 128 * lt + 128)
        for rh in range(ROWS // STEP):
            rows = slice(STEP * rh, STEP * rh + STEP)
            both = []
            for side in range(2):
                at = tile if side == 0 else TILES - 1 - tile
                wide = lanes(at, 128)
                if j == 0:
                    cf = (lane + at * 128).astype(F32)
                    idx = seg[rows, wide] - base[rows, :]
                    a = jnp.take_along_axis(rowt[0, rows, :], idx, axis=1)
                    b = jnp.take_along_axis(rowt[1, rows, :], idx, axis=1)
                    m = jnp.take_along_axis(rowt[2, rows, :], idx, axis=1)
                    phase = a + b * (cf - m)
                    mag = amp[rows, wide].astype(F32)
                    if side == 1:
                        phase = jnp.take_along_axis(phase, 127 - lane, axis=1)
                        mag = jnp.take_along_axis(mag, 127 - lane, axis=1)
                    square = phase * phase
                    pr = mag * poly(COS_PHASE, square)
                    pi = mag * (phase * poly(SIN_PHASE, square))
                    pbuf[0, rows, wide] = pr
                    pbuf[1, rows, wide] = pi
                else:
                    pr = pbuf[0, rows, wide]
                    pi = pbuf[1, rows, wide]
                both.append((pr, pi))
            waves = wave_sincos(j, rows, tile, roww, colw)
            for side in range(2):
                wide = lanes(tile if side == 0 else TILES - 1 - tile, 128)
                wbuf[2 * j, rows, wide] = waves[side][0]
                wbuf[2 * j + 1, rows, wide] = waves[side][1]
            for t in range(2):
                f, g = waves[0][1 - t], waves[1][1 - t]
                for o in range(2):
                    one, two = both[0][o] * f, both[1][o] * g
                    at = 128 * t + 64 * o + STEP * rh
                    ebuf[at : at + STEP, cols] = (one + two).astype(BF16)
                    ebuf[256 + at : 256 + at + STEP, cols] = (one - two).astype(BF16)


def add_dots(acc, ctab, index, ebuf):
    for part in range(2):
        rows = slice(256 * part, 256 * part + 256)
        acc[rows, :] += lax.dot_general(ctab[rows, lanes(index, SUB)], ebuf[rows, :], NT,
                                        preferred_element_type=F32)


def column_sums(acc, pay, ysc):
    plus = lane_sign(1.0, -1.0)
    for b in range(2):
        parts = []
        for t in range(2):
            cols = slice(128 * t, 128 * t + 128)
            c = acc[128 * b : 128 * b + 128, cols]
            s = plus * pltpu.roll(acc[256 + 128 * b : 384 + 128 * b, cols], 64, 1)
            parts.append((c + s, c - s))
        for side in range(2):
            even = parts[0][side]
            odd = plus * pltpu.roll(parts[1][side], 64, 1)
            ysc[side, b, :, 0:128] = even - odd
            ysc[side, b, :, 128:256] = even + odd
    for d in range(PEERS // 2):
        for side in range(2):
            to = d if side == 0 else PEERS - 1 - d
            pay[to] = jnp.concatenate(
                [ysc[side, b, OWN * d : OWN * d + OWN, :] for b in range(2)], axis=0
            ).astype(BF16)


def focal_part(j, normf, recv, hpay, lhs, hs, ms, table):
    low = iota((16, 128), 1) < 64

    def gather(s4, carry):
        for k in range(4):
            s = s4 * 4 + k
            cols = lanes(s, 128)
            for q in range(2):
                one = recv[2 * s, :, 128 * q : 128 * q + 128].astype(F32)
                two = recv[2 * s + 1, :, 128 * q : 128 * q + 128].astype(F32)
                re = jnp.where(low, one, pltpu.roll(two, 64, 1))
                im = jnp.where(low, pltpu.roll(one, 64, 1), two)
                for b in range(2):
                    lhs[b, 16 * q : 16 * q + 8, cols] = re[8 * b : 8 * b + 8]
                    lhs[b, 16 * q + 8 : 16 * q + 16, cols] = im[8 * b : 8 * b + 8]
        return carry
    lax.fori_loop(0, PEERS // 8, gather, 0)

    for b in range(2):
        here = table[256 * b : 256 * b + 256, :]
        parts = lax.dot_general(lhs[b].astype(BF16), here, NT, preferred_element_type=F32)
        rows = []
        for q in range(2):
            re, im = parts[16 * q : 16 * q + 8], parts[16 * q + 8 : 16 * q + 16]
            pieces = []
            for o, (c, s) in enumerate(((re[:, :HALF], im[:, HALF:]), (im[:, :HALF], -re[:, HALF:]))):
                want = pl.ds(b * 64 + 4 * j + 2 * q + o, 8, stride=8)
                one = (c + s) * normf - ms[0, want, :]
                two = (c - s) * normf - ms[1, want, :]
                pieces.append((one + two, one - two))
            (re_e, re_o), (im_e, im_o) = pieces
            rows.append(jnp.concatenate([re_e, -im_o], axis=1))
            rows.append(jnp.concatenate([im_e, re_o], axis=1))
        left = jnp.concatenate(rows, axis=0).astype(BF16)
        hs[b] = jnp.dot(left, here, preferred_element_type=F32)

    low8 = iota((8, 128), 1) < 64

    def spread(s4, carry):
        for k in range(4):
            s = s4 * 4 + k
            cols = lanes(s, 128)
            for q in range(2):
                first, second = [], []
                for b in range(2):
                    re = hs[b, 16 * q : 16 * q + 8, cols]
                    im = hs[b, 16 * q + 8 : 16 * q + 16, cols]
                    first.append(jnp.where(low8, re, pltpu.roll(im, 64, 1)))
                    second.append(jnp.where(low8, pltpu.roll(re, 64, 1), im))
                hpay[2 * s, :, 128 * q : 128 * q + 128] = jnp.concatenate(first, axis=0).astype(BF16)
                hpay[2 * s + 1, :, 128 * q : 128 * q + 128] = jnp.concatenate(second, axis=0).astype(BF16)
        return carry
    lax.fori_loop(0, PEERS // 8, spread, 0)


def hidden_left(j, hid, left, leftt):
    minus = lane_sign(-1.0, 1.0)
    for d in range(PEERS // 2):
        here = hid[d].astype(F32)
        there = hid[PEERS - 1 - d].astype(F32)
        even, odd = here + there, here - there
        e = [even[:, 128 * t : 128 * t + 128] for t in range(2)]
        o = [odd[:, 128 * t : 128 * t + 128] for t in range(2)]
        for t in range(2):
            cols = slice(128 * t, 128 * t + 128)
            es = e[0] + e[1] if t == 0 else e[0] - e[1]
            os = o[0] + o[1] if t == 0 else o[0] - o[1]
            os = minus * pltpu.roll(os, 64, 1)
            for b in range(2):
                left[128 * b + 8 * d : 128 * b + 8 * d + 8, cols] = es[8 * b : 8 * b + 8]
                left[256 + 128 * b + 8 * d : 264 + 128 * b + 8 * d, cols] = os[8 * b : 8 * b + 8]
    leftt[256 * j : 256 * j + 256, :] = left[...].T.astype(BF16)


def weights(lt, piece, gbuf, wbuf, pbuf, wst):
    for lh in range(2):
        tile = piece * 2 + lh
        gc = slice(128 * lh, 128 * lh + 128)
        for rh in range(2):
            rows = slice(32 * rh, 32 * rh + 32)
            zr, zi = [0.0, 0.0], [0.0, 0.0]
            for j in range(2):
                at = [256 * j + 64 * n + 32 * rh for n in range(4)]
                even = [gbuf[lt, 0, x : x + 32, gc] for x in at]
                odd = [gbuf[lt, 1, x : x + 32, gc] for x in at]
                for side in range(2):
                    g = [e + o if side == 0 else e - o for e, o in zip(even, odd)]
                    wide = lanes(tile if side == 0 else TILES - 1 - tile, 128)
                    sw, cw = wbuf[2 * j, rows, wide], wbuf[2 * j + 1, rows, wide]
                    zr[side] = zr[side] + (cw * g[0] + sw * g[3])
                    zi[side] = zi[side] + (cw * g[1] - sw * g[2])
            for side in range(2):
                wide = lanes(tile if side == 0 else TILES - 1 - tile, 128)
                w = pbuf[0, rows, wide] * zi[side] - pbuf[1, rows, wide] * zr[side]
                high = w.astype(BF16)
                wst[32 * rh : 32 * rh + 32, wide] = high
                wst[64 + 32 * rh : 96 + 32 * rh, wide] = (w - high.astype(F32)).astype(BF16)


def backward(chunk, leftt, table, gbuf, wbuf, pbuf, wst):
    count = BCHUNK // 256
    for lt in range(count + 1):
        piece = chunk * count + lt
        if lt < count:
            for part in range(2):
                ks = slice(256 * part, 256 * part + 256)
                gbuf[lt, part] = jnp.dot(leftt[:, ks], table[ks, lanes(piece, 256)], preferred_element_type=F32)
        if lt > 0:
            weights(lt - 1, piece - 1, gbuf, wbuf, pbuf, wst)


def prefix_weights(tris):
    row, lane = iota((128, 128), 0), iota((128, 128), 1)
    for side in range(2):
        at = row if side == 0 else 127 - row
        weight = at.astype(F32)
        some = at <= lane
        one = jnp.where(some, 1.0, 0.0).astype(BF16)
        two = jnp.where(some, weight, 0.0).astype(BF16)
        three = jnp.ones((128, 128), BF16)
        four = weight.astype(BF16)
        for half in range(2):
            for q, part in enumerate((one, two, three, four)):
                tris[side, 128 * half : 128 * half + 128, 128 * q : 128 * q + 128] = part


def segment_sums(tabs, wst, pick, ulow, tris, pre0, pre1, sbuf, pack):
    c0 = jnp.concatenate([tabs[t, 2:3, :] for t in range(SROWS)], axis=0)
    c1 = jnp.concatenate([tabs[t, 3:4, :] for t in range(SROWS)], axis=0)
    tile1 = jnp.floor(c1 * (1.0 / 128.0))
    idx1 = (c1 - 128.0 * tile1).astype(jnp.int32)
    first = iota((SROWS, 128), 1) == 0

    def less_previous(ends):
        return ends - jnp.where(first, 0.0, pltpu.roll(ends, 1, 1))

    middle = 0.5 * (c0 + c1)

    def row_sums(k, carry):
        u = jnp.dot(pick[0:48, :], wst[:, lanes(k, 1024)], preferred_element_type=F32)
        parts = []
        for lt in range(8):
            gc = slice(128 * lt, 128 * lt + 128)
            parts += [u[0:16, gc], u[16:32, gc] + u[32:48, gc]]
        u = jnp.concatenate(parts, axis=0)
        high = u.astype(BF16)
        low = (u - high.astype(F32)).astype(BF16)
        ulow[pl.ds(pl.multiple_of(k * 256, 256), 256), :] = jnp.concatenate([high, low], axis=1)
        return carry
    lax.fori_loop(0, TILES // 8, row_sums, 0, unroll=4)

    def prefix(k, pre):
        rows = pl.ds(pl.multiple_of(k * 256, 256), 256)
        pre[...] = jnp.dot(ulow[rows, :], tris[k // (TILES // 16)], preferred_element_type=F32)

    def edges(k, pre, sums):
        sums = list(sums)
        for lt in range(8):
            tile = (k * 8 + lt).astype(F32)
            last1, over1 = tile1 == tile, tile1 > tile
            upto = []
            for half, at in ((0, 0), (1, 0), (0, 16)):
                rows = slice(32 * lt + at, 32 * lt + at + 16)
                a = pre[rows, 128 * half : 128 * half + 128]
                whole = pre[rows, 128 * half + 256 : 128 * half + 384]
                g1 = jnp.take_along_axis(a, idx1, axis=1)
                upto.append(jnp.where(last1, g1, jnp.where(over1, whole, 0.0)))
            diff = less_previous(upto[0])
            sums[0] = sums[0] + diff
            sums[1] = sums[1] + (128.0 * tile - middle) * diff
            sums[2] = sums[2] + upto[1]
            sums[3] = sums[3] + upto[2]
        return tuple(sums)

    def pair(m, sums):
        prefix(2 * m, pre0)
        sums = edges(2 * m - 1, pre1, sums)
        prefix(2 * m + 1, pre1)
        return edges(2 * m, pre0, sums)
    zero = jnp.zeros((SROWS, 128), F32)
    sums = lax.fori_loop(0, TILES // 16, pair, (zero, zero, zero, zero))
    s0, s1, s1_inside, s2 = edges(jnp.int32(TILES // 8 - 1), pre1, sums)
    s1, s2 = s1 + less_previous(s1_inside), less_previous(s2)
    keep = iota((SROWS, 128), 1) < PER_ROW
    s1 = s1 / (0.5 * (c1 - c0 + 1.0))
    s0, s1, s2 = [jnp.where(keep, v, 0.0) for v in (s0, s1, s2)]
    sbuf[...] = jnp.zeros_like(sbuf)
    for t in range(SROWS):
        sbuf[t, 0:1, :] = s0[t : t + 1]
        sbuf[t, 1:2, :] = s1[t : t + 1]
        sbuf[t, 2:3, :] = s2[t : t + 1]

    packed = [jnp.zeros((8, 128), F32) for _ in range(10)]
    lane = iota((8, 128), 1)
    for t in range(SROWS):
        first, off = divmod(PER_ROW * t, 128)
        turned = pltpu.roll(sbuf[t], off, 1) if off else sbuf[t]
        packed[first] = packed[first] + jnp.where(lane >= off, turned, 0.0)
        if off + PER_ROW > 128:
            packed[first + 1] = packed[first + 1] + jnp.where(lane < off, turned, 0.0)
    for q in range(3):
        for k in range(10):
            p, r = divmod(q * 10 + k, 8)
            pack[p, r : r + 1, :] = packed[k][q : q + 1, :]
    pack[3, 6:8, :] = jnp.zeros((2, 128), F32)


def remote(src, dst, ssem, rsem, where):
    return pltpu.make_async_remote_copy(src_ref=src, dst_ref=dst, send_sem=ssem, recv_sem=rsem,
                                        device_id=where, device_id_type=MESH)


def each(count, fn):
    def step(o, carry):
        fn(o)
        return carry
    lax.fori_loop(1, count, step, 0)


def kernel(normf, amp_hbm, seg_hbm, box_hbm, coef_hbm, freq_ref, pamp_ref, meas_hbm, ctab_hbm, rtab_hbm,
           out_ref, box_ref, coef_ref, meas_ref, amp, seg, ctab, rtab, flat, tabs, rowt, base, pick, roww, colw, pbuf, wbuf, eb0, eb1, acc, ysc,
           pay, recv, lhs, hs, ms, hpay, hid, left, leftt, gbuf, wst, ulow, tris, pre0, pre1, sbuf, pack,
           got_a, mine_b, got_b, mine_c, got_c, lsem, tsem, osem, ssem, rsem, asem, bsem, csem):
    band = lax.axis_index("band")
    me = lax.axis_index("row")
    core = lax.rem(me, 2)
    chip = me // 2
    row0 = me * ROWS

    def loads(i):
        cols, mirror = lanes(i, CHUNK), lanes(2 * CHUNKS - 1 - i, CHUNK)
        return [pltpu.make_async_copy(seg_hbm.at[:, cols], seg.at[:, cols], lsem.at[0, i]),
                pltpu.make_async_copy(seg_hbm.at[:, mirror], seg.at[:, mirror], lsem.at[1, i]),
                pltpu.make_async_copy(amp_hbm.at[:, cols], amp.at[:, cols], lsem.at[2, i]),
                pltpu.make_async_copy(amp_hbm.at[:, mirror], amp.at[:, mirror], lsem.at[3, i]),
                pltpu.make_async_copy(ctab_hbm.at[band, :, cols], ctab.at[:, cols], lsem.at[4, i])]

    def start_loads(i, carry):
        for copy in loads(i):
            copy.start()
        return carry
    small = [pltpu.make_async_copy(box_hbm, box_ref, osem.at[0]),
             pltpu.make_async_copy(coef_hbm, coef_ref, osem.at[1]),
             pltpu.make_async_copy(meas_hbm, meas_ref, osem.at[2])]
    small[0].start()
    small[1].start()
    lax.fori_loop(0, CHUNKS, start_loads, 0)
    small[2].start()
    table_copy = pltpu.make_async_copy(rtab_hbm.at[band], rtab, tsem)
    table_copy.start()

    barrier = pltpu.get_barrier_semaphore()

    def greet(where):
        pl.semaphore_signal(barrier, inc=1, device_id=where, device_id_type=MESH)
    each(PEERS, lambda o: greet((band, lax.rem(me + o, PEERS))))
    for o in range(1, YS):
        for c in range(2):
            greet((lax.rem(band + o, YS), chip * 2 + c))

    wave_setup(row0, freq_ref, pamp_ref, roww, colw)
    def send(j, source, target):
        def one(o):
            peer = lax.rem(me + o, PEERS)
            remote(source.at[j, peer], target.at[j, me], ssem.at[j, peer], rsem.at[j, me], (band, peer)).start()
        each(PEERS, one)

    def await_all(j, source, target):
        def one(o):
            peer = lax.rem(me + o, PEERS)
            remote(source.at[j, peer], target.at[j, peer], ssem.at[j, peer], rsem.at[j, peer], (band, peer)).wait()
        each(PEERS, one)

    for j in range(2):
        acc[...] = jnp.zeros_like(acc)
        eb1[...] = jnp.zeros_like(eb1)

        def forward(i, carry):
            if j == 0:
                for copy in loads(i):
                    copy.wait()

                @pl.when(i == 0)
                def _():
                    small[0].wait()
                    small[1].wait()
                    segment_setup(row0, box_ref, coef_ref, seg, flat, tabs, rowt, base, pick)
            before = jnp.maximum(2 * i - 1, 0)
            fields(j, 2 * i, eb0, amp, seg, rowt, base, roww, colw, pbuf, wbuf)
            add_dots(acc, ctab, before, eb1)
            fields(j, 2 * i + 1, eb1, amp, seg, rowt, base, roww, colw, pbuf, wbuf)
            add_dots(acc, ctab, 2 * i, eb0)
            return carry
        lax.fori_loop(0, CHUNKS, forward, 0)
        add_dots(acc, ctab, FOLD // SUB - 1, eb1)
        column_sums(acc, pay.at[j], ysc)
        if j == 0:
            pl.semaphore_wait(barrier, PEERS - 1 + 2 * (YS - 1))
        send(j, pay, recv)
        recv[j, me] = pay[j, me]

    small[2].wait()
    for b in range(2):
        for v in range(OWN):
            source = jnp.where(me < PEERS // 2, v, OWN - 1 - v)
            for k in range(PROBES):
                at = b * 64 + 8 * v + 2 * k
                ms[0, at : at + 2, :] = meas_ref[b, source, k, :, :HALF]
                ms[1, at : at + 2, :] = meas_ref[b, source, k, :, HALF:]
    flip = (iota((128, 128), 0) + iota((128, 128), 1) == 127).astype(F32)
    ms[1] = jnp.dot(ms[1], flip, precision=lax.Precision.HIGHEST, preferred_element_type=F32)
    table_copy.wait()
    for j in range(2):
        await_all(j, pay, recv)
        focal_part(j, normf, recv.at[j], hpay.at[j], lhs, hs, ms, rtab)
        def one(o):
            peer = lax.rem(me + o, PEERS)
            remote(hpay.at[j, peer], hid.at[j, me], ssem.at[2 + j, peer], rsem.at[2 + j, me], (band, peer)).start()
        each(PEERS, one)
        hid[j, me] = hpay[j, me]

    prefix_weights(tris)
    pre1[...] = jnp.zeros_like(pre1)
    for j in range(2):
        def done(o):
            peer = lax.rem(me + o, PEERS)
            remote(hpay.at[j, peer], hid.at[j, peer], ssem.at[2 + j, peer], rsem.at[2 + j, peer],
                   (band, peer)).wait()
        each(PEERS, done)
        hidden_left(j, hid.at[j], left, leftt)

    def back(i, carry):
        backward(i, leftt, ctab, gbuf, wbuf, pbuf, wst)
        return carry
    lax.fori_loop(0, FOLD // BCHUNK, back, 0)

    segment_sums(tabs, wst, pick, ulow, tris, pre0, pre1, sbuf, pack)

    near = band * 2 + core

    def near_copy(o, slot):
        peer = lax.rem(near + o, 2 * YS)
        to = peer // 2
        at = near if slot == "mine" else peer
        return remote(pack.at[to], got_a.at[at], asem.at[0, peer], asem.at[1, at],
                      (to, chip * 2 + lax.rem(peer, 2)))
    each(2 * YS, lambda o: near_copy(o, "mine").start())
    got_a[near] = pack[band]
    each(2 * YS, lambda o: near_copy(o, "peer").wait())
    total = got_a[0]
    for k in range(1, 2 * YS):
        total = total + got_a[k]
    mine_b[...] = total

    def far_copy(o, slot):
        peer = lax.rem(chip + o, CHIPS)
        at = chip if slot == "mine" else peer
        return remote(mine_b, got_b.at[at], bsem.at[0, peer], bsem.at[1, at], (band, peer * 2 + core))
    each(CHIPS, lambda o: far_copy(o, "mine").start())
    got_b[chip] = mine_b[...]
    each(CHIPS, lambda o: far_copy(o, "peer").wait())
    total = got_b[0]
    for k in range(1, CHIPS):
        total = total + got_b[k]
    mine_c[...] = total

    def share_copy(o, slot):
        peer = lax.rem(band + o, YS)
        at = band if slot == "mine" else peer
        return remote(mine_c, got_c.at[at], csem.at[0, peer], csem.at[1, at], (peer, me))
    each(YS, lambda o: share_copy(o, "mine").start())
    got_c[band] = mine_c[...]
    each(YS, lambda o: share_copy(o, "peer").wait())
    for q in range(3):
        for k in range(10):
            p, r = divmod(q * 10 + k, 8)
            width = min(128, SEG - 128 * k)
            out_ref[q : q + 1, 128 * k : 128 * k + width] = got_c[p, r : r + 1, :width]


VM = pl.BlockSpec(memory_space=pltpu.VMEM)
SM = pl.BlockSpec(memory_space=pltpu.SMEM)
HBM = pl.BlockSpec(memory_space=pl.ANY)
LIMIT = 60 * 1024 * 1024


def solution(mesh):
    ctable = jnp.asarray(column_table())
    rtable = jnp.asarray(row_table())
    root = math.sqrt(NR * NC)

    def body(amplitude, seg_map, seg_box, seg_coeffs, probe_freq, probe_amp, measured):
        dma = pltpu.SemaphoreType.DMA
        sums = pl.pallas_call(
            functools.partial(kernel, 1.0 / root),
            in_specs=[HBM, HBM, HBM, HBM, SM, SM, HBM, HBM, HBM],
            out_specs=VM,
            out_shape=jax.ShapeDtypeStruct((3, SEG), F32),
            scratch_shapes=[
                pltpu.VMEM((4, SEG), jnp.int32),
                pltpu.VMEM((3, SEG), F32),
                pltpu.VMEM((2, OWN, PROBES, 2, M), F32),
                pltpu.VMEM((ROWS, NC), BF16),
                pltpu.VMEM((ROWS, NC), jnp.int32),
                pltpu.VMEM((4 * HALF, FOLD), BF16),
                pltpu.VMEM((4 * HALF, NR), BF16),
                pltpu.VMEM((8, 1280), F32),
                pltpu.VMEM((SROWS, 8, 128), F32),
                pltpu.VMEM((3, ROWS, 128), F32),
                pltpu.VMEM((ROWS, 128), jnp.int32),
                pltpu.VMEM((128, 128), BF16),
                pltpu.VMEM((4, ROWS, 128), F32),
                pltpu.VMEM((4, TILES, 128), F32),
                pltpu.VMEM((2, ROWS, NC), F32),
                pltpu.VMEM((4, ROWS, NC), F32),
                pltpu.VMEM((512, SUB), BF16),
                pltpu.VMEM((512, SUB), BF16),
                pltpu.VMEM((4 * HALF, 256), F32),
                pltpu.VMEM((2, 2, HALF, 256), F32),
                pltpu.VMEM((2, PEERS, 16, 256), BF16),
                pltpu.VMEM((2, PEERS, 16, 256), BF16),
                pltpu.VMEM((2, 32, NR), F32),
                pltpu.VMEM((2, 32, NR), F32),
                pltpu.VMEM((2, 128, HALF), F32),
                pltpu.VMEM((2, PEERS, 16, 256), BF16),
                pltpu.VMEM((2, PEERS, 16, 256), BF16),
                pltpu.VMEM((4 * HALF, 256), F32),
                pltpu.VMEM((512, 4 * HALF), BF16),
                pltpu.VMEM((BCHUNK // 256, 2, 512, 256), F32),
                pltpu.VMEM((128, NC), BF16),
                pltpu.VMEM((TILES * 32, 256), BF16),
                pltpu.VMEM((2, 256, 512), BF16),
                pltpu.VMEM((256, 512), F32),
                pltpu.VMEM((256, 512), F32),
                pltpu.VMEM((SROWS, 8, 128), F32),
                pltpu.VMEM((4, 8, 128), F32),
                pltpu.VMEM((2 * YS, 8, 128), F32),
                pltpu.VMEM((8, 128), F32),
                pltpu.VMEM((CHIPS, 8, 128), F32),
                pltpu.VMEM((8, 128), F32),
                pltpu.VMEM((YS, 8, 128), F32),
                dma((5, CHUNKS)),
                dma,
                dma((3,)),
                dma((4, PEERS)),
                dma((4, PEERS)),
                dma((2, 2 * YS)),
                dma((2, CHIPS)),
                dma((2, YS)),
            ],
            compiler_params=pltpu.CompilerParams(collective_id=0, has_side_effects=True, vmem_limit_bytes=LIMIT),
            name="gradient",
        )(amplitude, seg_map, seg_box, seg_coeffs, probe_freq, probe_amp, measured, ctable, rtable)
        return sums * (2.0 / root / (BANDS * PROBES))

    in_specs = (P("row", None), P("row", None), P(), P(), P(), P(), P("band", "row", None, None, None))
    return jax.shard_map(body, mesh=mesh, in_specs=in_specs, out_specs=P(), check_vma=False)
```

```python
import functools
import math

import jax
import jax.numpy as jnp
import ml_dtypes
import numpy as np
from jax import lax
from jax.experimental import pallas as pl
from jax.experimental.pallas import tpu as pltpu
from jax.sharding import PartitionSpec as P

NC = 8192
NR = 2048
M = 256
BANDS = 8
PROBES = 4
SEG = 1200
SROWS = 16
PER_ROW = SEG // SROWS
HALF = M // 2
ROWS = 64
PEERS = 32
OWN = 8
SPREAD = 0.2
SAMPLING = 0.5
MESH = pl.DeviceIdType.MESH
F32 = jnp.float32
BF16 = jnp.bfloat16
STEP = 64
SUB = 512
CHUNK = 1024
FOLD = NC // 2
CHUNKS = FOLD // CHUNK
BCHUNK = 1024
TILES = NC // 128
CHIPS = 16
YS = 4
NT = (((1,), (1,)), ((), ()))


def series(fn, top, count):
    cheb = np.polynomial.chebyshev.Chebyshev.interpolate(
        lambda s: fn(np.sqrt(s)), count - 1, domain=[0.0, top * top]
    )
    return [float(v) for v in cheb.convert(kind=np.polynomial.Polynomial).coef]


def sinc(x):
    return np.sinc(x / np.pi)


SIN_PHASE = series(sinc, 3.02, 6)
COS_PHASE = series(np.cos, 3.02, 7)
SIN_WAVE = series(sinc, 0.81, 4)
COS_WAVE = series(np.cos, 0.81, 4)
SIN_TURN = series(lambda x: 2 * np.pi * np.sinc(2 * x), 0.5, 8)
COS_TURN = series(lambda x: np.cos(2 * np.pi * x), 0.5, 8)


def poly(coefs, s):
    total = jnp.full_like(s, coefs[-1])
    for value in coefs[-2::-1]:
        total = total * s + value
    return total


def turn_sincos(turns):
    part = turns - jnp.floor(turns + 0.5)
    square = part * part
    return part * poly(SIN_TURN, square), poly(COS_TURN, square)


def half_tables(coords, order):
    focal = (np.arange(HALF, dtype=np.float32) - np.float32(M / 2) + np.float32(0.5)) * np.float32(SAMPLING)
    base = (np.float32(2.0 * math.pi) * focal)[:, None] * coords[None, :]
    out = []
    for band in range(BANDS):
        ratio = np.float32(1.0) + np.float32(SPREAD) * (
            (np.float32(band) + np.float32(0.5)) / np.float32(BANDS) - np.float32(0.5)
        )
        angle = (base / ratio).astype(np.float64)
        out.append(np.stack([np.cos(angle), np.sin(angle)]).astype(np.float32).astype(ml_dtypes.bfloat16))
    return np.stack(out)


def column_table():
    coords = (np.arange(NC, dtype=np.float32) + np.float32(0.5)) / np.float32(NC) - np.float32(0.5)
    tables = half_tables(coords, 0)[..., :FOLD].reshape(4, 2, 2, HALF, FOLD)
    return tables.transpose(0, 2, 1, 3, 4).reshape(4, 4 * HALF, FOLD)


def row_table():
    coords = (np.arange(NR, dtype=np.float32) + np.float32(0.5)) / np.float32(NC) - np.float32(NR / (2.0 * NC))
    return half_tables(coords, 0).reshape(4, 4 * HALF, NR)


def lane_sign(first, second):
    lane = lax.broadcasted_iota(jnp.int32, (1, 128), 1)
    return jnp.where(lane < 64, F32(first), F32(second))


def iota(shape, dim):
    return lax.broadcasted_iota(jnp.int32, shape, dim)


def wave_setup(row0, freq_ref, amp_ref, roww, colw):
    rows = (iota((ROWS, 128), 0) + row0).astype(F32)
    place = (rows + 0.5) / NC - NR / (2.0 * NC)
    cols = (iota((TILES, 128), 0) * 128 + iota((TILES, 128), 1)).astype(F32)
    across = (cols + 0.5) / NC - 0.5
    for j in range(2):
        s, c = turn_sincos(place * freq_ref[j, 1].astype(F32))
        roww[2 * j] = s * amp_ref[j]
        roww[2 * j + 1] = c * amp_ref[j]
        s, c = turn_sincos(across * freq_ref[j, 0].astype(F32))
        colw[2 * j] = s
        colw[2 * j + 1] = c


def wave_sincos(j, rows, tile, roww, colw):
    one = roww[2 * j + 1, rows, :] * colw[2 * j, pl.ds(tile, 1), :]
    two = roww[2 * j, rows, :] * colw[2 * j + 1, pl.ds(tile, 1), :]
    out = []
    for wave in (two + one, two - one):
        square = wave * wave
        out.append((wave * poly(SIN_WAVE, square), poly(COS_WAVE, square)))
    return out


def lanes(index, width):
    return pl.ds(pl.multiple_of(index * width, width), width)


def segment_setup(row0, box_ref, coef_ref, seg, flat, tabs, rowt, base, pick):
    flat[...] = jnp.zeros_like(flat)
    flat[0:4, 0:SEG] = box_ref[...].astype(F32)
    flat[4:7, 0:SEG] = coef_ref[...]
    lane = iota((8, 128), 1)
    for t in range(SROWS):
        first, off = divmod(PER_ROW * t, 128)
        one = flat[:, 128 * first : 128 * first + 128]
        if off:
            two = flat[:, 128 * first + 128 : 128 * first + 256]
            one = jnp.where(lane < 128 - off, pltpu.roll(one, 128 - off, 1), pltpu.roll(two, 128 - off, 1))
        tabs[t] = one
    column = seg[:, 0:1]
    trow = jnp.zeros((ROWS, 1), jnp.int32)
    for m in range(1, SROWS):
        trow = trow + (column >= PER_ROW * m).astype(jnp.int32)
    trow = jnp.broadcast_to(trow, (ROWS, 128))
    base[...] = trow * PER_ROW
    rows = (iota((ROWS, 128), 0) + row0).astype(F32)
    alpha, beta, middle, down_all = [jnp.zeros((ROWS, 128), F32) for _ in range(4)]
    for t in range(SROWS):
        r0, r1, c0, c1 = [tabs[t, q : q + 1, :] for q in range(4)]
        piston, tip, tilt = [tabs[t, q : q + 1, :] for q in range(4, 7)]
        here = trow == t
        down = (rows - 0.5 * (r0 + r1)) / (0.5 * (r1 - r0 + 1.0))
        alpha = jnp.where(here, piston + tilt * down, alpha)
        beta = jnp.where(here, tip / (0.5 * (c1 - c0 + 1.0)), beta)
        middle = jnp.where(here, 0.5 * (c0 + c1), middle)
        down_all = jnp.where(here, down, down_all)
    rowt[0] = alpha
    rowt[1] = beta
    rowt[2] = middle
    lane = iota((ROWS, 128), 1)
    down_all = jnp.broadcast_to(down_all[:, 0:1], (ROWS, 128))
    high = down_all.astype(BF16).astype(F32)
    which = jnp.where(lane < 16, 1.0, jnp.where(lane < 32, high, jnp.where(lane < 48, down_all - high, 0.0)))
    chosen = jnp.where(lax.rem(lane, 16) == trow, which, 0.0)
    pick[...] = jnp.concatenate([chosen, chosen], axis=0).T.astype(BF16)


def fields(j, chunk, ebuf, amp, seg, rowt, base, roww, colw, pbuf, wbuf):
    lane = iota((STEP, 128), 1)
    for lt in range(SUB // 128):
        tile = chunk * (SUB // 128) + lt
        cols = slice(128 * lt, 128 * lt + 128)
        for rh in range(ROWS // STEP):
            rows = slice(STEP * rh, STEP * rh + STEP)
            both = []
            for side in range(2):
                at = tile if side == 0 else TILES - 1 - tile
                wide = lanes(at, 128)
                if j == 0:
                    cf = (lane + at * 128).astype(F32)
                    idx = seg[rows, wide] - base[rows, :]
                    a = jnp.take_along_axis(rowt[0, rows, :], idx, axis=1)
                    b = jnp.take_along_axis(rowt[1, rows, :], idx, axis=1)
                    m = jnp.take_along_axis(rowt[2, rows, :], idx, axis=1)
                    phase = a + b * (cf - m)
                    mag = amp[rows, wide].astype(F32)
                    if side == 1:
                        phase = jnp.take_along_axis(phase, 127 - lane, axis=1)
                        mag = jnp.take_along_axis(mag, 127 - lane, axis=1)
                    square = phase * phase
                    pr = mag * poly(COS_PHASE, square)
                    pi = mag * (phase * poly(SIN_PHASE, square))
                    pbuf[0, rows, wide] = pr
                    pbuf[1, rows, wide] = pi
                else:
                    pr = pbuf[0, rows, wide]
                    pi = pbuf[1, rows, wide]
                both.append((pr, pi))
            waves = wave_sincos(j, rows, tile, roww, colw)
            for side in range(2):
                wide = lanes(tile if side == 0 else TILES - 1 - tile, 128)
                wbuf[2 * j, rows, wide] = waves[side][0]
                wbuf[2 * j + 1, rows, wide] = waves[side][1]
            for t in range(2):
                f, g = waves[0][1 - t], waves[1][1 - t]
                for o in range(2):
                    one, two = both[0][o] * f, both[1][o] * g
                    at = 128 * t + 64 * o + STEP * rh
                    ebuf[at : at + STEP, cols] = (one + two).astype(BF16)
                    ebuf[256 + at : 256 + at + STEP, cols] = (one - two).astype(BF16)


def add_dots(acc, ctab, index, ebuf):
    for part in range(2):
        rows = slice(256 * part, 256 * part + 256)
        acc[rows, :] += lax.dot_general(ctab[rows, lanes(index, SUB)], ebuf[rows, :], NT,
                                        preferred_element_type=F32)


def column_sums(acc, pay, ysc):
    plus = lane_sign(1.0, -1.0)
    for b in range(2):
        parts = []
        for t in range(2):
            cols = slice(128 * t, 128 * t + 128)
            c = acc[128 * b : 128 * b + 128, cols]
            s = plus * pltpu.roll(acc[256 + 128 * b : 384 + 128 * b, cols], 64, 1)
            parts.append((c + s, c - s))
        for side in range(2):
            even = parts[0][side]
            odd = plus * pltpu.roll(parts[1][side], 64, 1)
            ysc[side, b, :, 0:128] = even - odd
            ysc[side, b, :, 128:256] = even + odd
    for d in range(PEERS // 2):
        for side in range(2):
            to = d if side == 0 else PEERS - 1 - d
            pay[to] = jnp.concatenate(
                [ysc[side, b, OWN * d : OWN * d + OWN, :] for b in range(2)], axis=0
            ).astype(BF16)


def focal_part(j, normf, recv, hpay, lhs, hs, ms, table):
    low = iota((16, 128), 1) < 64

    def gather(s4, carry):
        for k in range(4):
            s = s4 * 4 + k
            cols = lanes(s, 128)
            for q in range(2):
                one = recv[2 * s, :, 128 * q : 128 * q + 128].astype(F32)
                two = recv[2 * s + 1, :, 128 * q : 128 * q + 128].astype(F32)
                re = jnp.where(low, one, pltpu.roll(two, 64, 1))
                im = jnp.where(low, pltpu.roll(one, 64, 1), two)
                for b in range(2):
                    lhs[b, 16 * q : 16 * q + 8, cols] = re[8 * b : 8 * b + 8]
                    lhs[b, 16 * q + 8 : 16 * q + 16, cols] = im[8 * b : 8 * b + 8]
        return carry
    lax.fori_loop(0, PEERS // 8, gather, 0)

    for b in range(2):
        here = table[256 * b : 256 * b + 256, :]
        parts = lax.dot_general(lhs[b].astype(BF16), here, NT, preferred_element_type=F32)
        rows = []
        for q in range(2):
            re, im = parts[16 * q : 16 * q + 8], parts[16 * q + 8 : 16 * q + 16]
            pieces = []
            for o, (c, s) in enumerate(((re[:, :HALF], im[:, HALF:]), (im[:, :HALF], -re[:, HALF:]))):
                want = pl.ds(b * 64 + 4 * j + 2 * q + o, 8, stride=8)
                one = (c + s) * normf - ms[0, want, :]
                two = (c - s) * normf - ms[1, want, :]
                pieces.append((one + two, one - two))
            (re_e, re_o), (im_e, im_o) = pieces
            rows.append(jnp.concatenate([re_e, -im_o], axis=1))
            rows.append(jnp.concatenate([im_e, re_o], axis=1))
        left = jnp.concatenate(rows, axis=0).astype(BF16)
        hs[b] = jnp.dot(left, here, preferred_element_type=F32)

    low8 = iota((8, 128), 1) < 64

    def spread(s4, carry):
        for k in range(4):
            s = s4 * 4 + k
            cols = lanes(s, 128)
            for q in range(2):
                first, second = [], []
                for b in range(2):
                    re = hs[b, 16 * q : 16 * q + 8, cols]
                    im = hs[b, 16 * q + 8 : 16 * q + 16, cols]
                    first.append(jnp.where(low8, re, pltpu.roll(im, 64, 1)))
                    second.append(jnp.where(low8, pltpu.roll(re, 64, 1), im))
                hpay[2 * s, :, 128 * q : 128 * q + 128] = jnp.concatenate(first, axis=0).astype(BF16)
                hpay[2 * s + 1, :, 128 * q : 128 * q + 128] = jnp.concatenate(second, axis=0).astype(BF16)
        return carry
    lax.fori_loop(0, PEERS // 8, spread, 0)


def hidden_left(j, hid, left, leftt):
    minus = lane_sign(-1.0, 1.0)
    for d in range(PEERS // 2):
        here = hid[d].astype(F32)
        there = hid[PEERS - 1 - d].astype(F32)
        even, odd = here + there, here - there
        e = [even[:, 128 * t : 128 * t + 128] for t in range(2)]
        o = [odd[:, 128 * t : 128 * t + 128] for t in range(2)]
        for t in range(2):
            cols = slice(128 * t, 128 * t + 128)
            es = e[0] + e[1] if t == 0 else e[0] - e[1]
            os = o[0] + o[1] if t == 0 else o[0] - o[1]
            os = minus * pltpu.roll(os, 64, 1)
            for b in range(2):
                left[128 * b + 8 * d : 128 * b + 8 * d + 8, cols] = es[8 * b : 8 * b + 8]
                left[256 + 128 * b + 8 * d : 264 + 128 * b + 8 * d, cols] = os[8 * b : 8 * b + 8]
    leftt[256 * j : 256 * j + 256, :] = left[...].T.astype(BF16)


def weights(lt, piece, gbuf, wbuf, pbuf, wst):
    for lh in range(2):
        tile = piece * 2 + lh
        gc = slice(128 * lh, 128 * lh + 128)
        for rh in range(2):
            rows = slice(32 * rh, 32 * rh + 32)
            zr, zi = [0.0, 0.0], [0.0, 0.0]
            for j in range(2):
                at = [256 * j + 64 * n + 32 * rh for n in range(4)]
                even = [gbuf[lt, 0, x : x + 32, gc] for x in at]
                odd = [gbuf[lt, 1, x : x + 32, gc] for x in at]
                for side in range(2):
                    g = [e + o if side == 0 else e - o for e, o in zip(even, odd)]
                    wide = lanes(tile if side == 0 else TILES - 1 - tile, 128)
                    sw, cw = wbuf[2 * j, rows, wide], wbuf[2 * j + 1, rows, wide]
                    zr[side] = zr[side] + (cw * g[0] + sw * g[3])
                    zi[side] = zi[side] + (cw * g[1] - sw * g[2])
            for side in range(2):
                wide = lanes(tile if side == 0 else TILES - 1 - tile, 128)
                w = pbuf[0, rows, wide] * zi[side] - pbuf[1, rows, wide] * zr[side]
                high = w.astype(BF16)
                wst[32 * rh : 32 * rh + 32, wide] = high
                wst[64 + 32 * rh : 96 + 32 * rh, wide] = (w - high.astype(F32)).astype(BF16)


def backward(chunk, leftt, table, gbuf, wbuf, pbuf, wst):
    count = BCHUNK // 256
    for lt in range(count + 1):
        piece = chunk * count + lt
        if lt < count:
            for part in range(2):
                ks = slice(256 * part, 256 * part + 256)
                gbuf[lt, part] = jnp.dot(leftt[:, ks], table[ks, lanes(piece, 256)], preferred_element_type=F32)
        if lt > 0:
            weights(lt - 1, piece - 1, gbuf, wbuf, pbuf, wst)


def prefix_weights(tris):
    row, lane = iota((128, 128), 0), iota((128, 128), 1)
    for side in range(2):
        at = row if side == 0 else 127 - row
        weight = at.astype(F32)
        some = at <= lane
        one = jnp.where(some, 1.0, 0.0).astype(BF16)
        two = jnp.where(some, weight, 0.0).astype(BF16)
        three = jnp.ones((128, 128), BF16)
        four = weight.astype(BF16)
        for half in range(2):
            for q, part in enumerate((one, two, three, four)):
                tris[side, 128 * half : 128 * half + 128, 128 * q : 128 * q + 128] = part


def segment_sums(tabs, wst, pick, ulow, tris, pre0, pre1, sbuf, pack):
    c0 = jnp.concatenate([tabs[t, 2:3, :] for t in range(SROWS)], axis=0)
    c1 = jnp.concatenate([tabs[t, 3:4, :] for t in range(SROWS)], axis=0)
    tile1 = jnp.floor(c1 * (1.0 / 128.0))
    idx1 = (c1 - 128.0 * tile1).astype(jnp.int32)
    first = iota((SROWS, 128), 1) == 0

    def less_previous(ends):
        return ends - jnp.where(first, 0.0, pltpu.roll(ends, 1, 1))

    middle = 0.5 * (c0 + c1)

    def row_sums(k, carry):
        u = jnp.dot(pick[0:48, :], wst[:, lanes(k, 1024)], preferred_element_type=F32)
        parts = []
        for lt in range(8):
            gc = slice(128 * lt, 128 * lt + 128)
            parts += [u[0:16, gc], u[16:32, gc] + u[32:48, gc]]
        u = jnp.concatenate(parts, axis=0)
        high = u.astype(BF16)
        low = (u - high.astype(F32)).astype(BF16)
        ulow[pl.ds(pl.multiple_of(k * 256, 256), 256), :] = jnp.concatenate([high, low], axis=1)
        return carry
    lax.fori_loop(0, TILES // 8, row_sums, 0, unroll=4)

    def prefix(k, pre):
        rows = pl.ds(pl.multiple_of(k * 256, 256), 256)
        pre[...] = jnp.dot(ulow[rows, :], tris[k // (TILES // 16)], preferred_element_type=F32)

    def edges(k, pre, sums):
        sums = list(sums)
        for lt in range(8):
            tile = (k * 8 + lt).astype(F32)
            last1, over1 = tile1 == tile, tile1 > tile
            upto = []
            for half, at in ((0, 0), (1, 0), (0, 16)):
                rows = slice(32 * lt + at, 32 * lt + at + 16)
                a = pre[rows, 128 * half : 128 * half + 128]
                whole = pre[rows, 128 * half + 256 : 128 * half + 384]
                g1 = jnp.take_along_axis(a, idx1, axis=1)
                upto.append(jnp.where(last1, g1, jnp.where(over1, whole, 0.0)))
            diff = less_previous(upto[0])
            sums[0] = sums[0] + diff
            sums[1] = sums[1] + (128.0 * tile - middle) * diff
            sums[2] = sums[2] + upto[1]
            sums[3] = sums[3] + upto[2]
        return tuple(sums)

    def pair(m, sums):
        prefix(2 * m, pre0)
        sums = edges(2 * m - 1, pre1, sums)
        prefix(2 * m + 1, pre1)
        return edges(2 * m, pre0, sums)
    zero = jnp.zeros((SROWS, 128), F32)
    sums = lax.fori_loop(0, TILES // 16, pair, (zero, zero, zero, zero))
    s0, s1, s1_inside, s2 = edges(jnp.int32(TILES // 8 - 1), pre1, sums)
    s1, s2 = s1 + less_previous(s1_inside), less_previous(s2)
    keep = iota((SROWS, 128), 1) < PER_ROW
    s1 = s1 / (0.5 * (c1 - c0 + 1.0))
    s0, s1, s2 = [jnp.where(keep, v, 0.0) for v in (s0, s1, s2)]
    sbuf[...] = jnp.zeros_like(sbuf)
    for t in range(SROWS):
        sbuf[t, 0:1, :] = s0[t : t + 1]
        sbuf[t, 1:2, :] = s1[t : t + 1]
        sbuf[t, 2:3, :] = s2[t : t + 1]

    packed = [jnp.zeros((8, 128), F32) for _ in range(10)]
    lane = iota((8, 128), 1)
    for t in range(SROWS):
        first, off = divmod(PER_ROW * t, 128)
        turned = pltpu.roll(sbuf[t], off, 1) if off else sbuf[t]
        packed[first] = packed[first] + jnp.where(lane >= off, turned, 0.0)
        if off + PER_ROW > 128:
            packed[first + 1] = packed[first + 1] + jnp.where(lane < off, turned, 0.0)
    for q in range(3):
        for k in range(10):
            p, r = divmod(q * 10 + k, 8)
            pack[p, r : r + 1, :] = packed[k][q : q + 1, :]
    pack[3, 6:8, :] = jnp.zeros((2, 128), F32)


def remote(src, dst, ssem, rsem, where):
    return pltpu.make_async_remote_copy(src_ref=src, dst_ref=dst, send_sem=ssem, recv_sem=rsem,
                                        device_id=where, device_id_type=MESH)


def each(count, fn):
    def step(o, carry):
        fn(o)
        return carry
    lax.fori_loop(1, count, step, 0, unroll=count < PEERS)


def kernel(normf, amp_hbm, seg_hbm, box_hbm, coef_hbm, freq_ref, pamp_ref, meas_hbm, ctab_hbm, rtab_hbm,
           out_ref, box_ref, coef_ref, meas_ref, amp, seg, ctab, rtab, flat, tabs, rowt, base, pick, roww, colw, pbuf, wbuf, eb0, eb1, acc, ysc,
           pay, recv, lhs, hs, ms, hpay, hid, left, leftt, gbuf, wst, ulow, tris, pre0, pre1, sbuf, pack,
           got_a, mine_b, got_b, mine_c, got_c, lsem, tsem, osem, ssem, rsem, asem, bsem, csem):
    band = lax.axis_index("band")
    me = lax.axis_index("row")
    core = lax.rem(me, 2)
    chip = me // 2
    row0 = me * ROWS

    def loads(i):
        cols, mirror = lanes(i, CHUNK), lanes(2 * CHUNKS - 1 - i, CHUNK)
        return [pltpu.make_async_copy(seg_hbm.at[:, cols], seg.at[:, cols], lsem.at[0, i]),
                pltpu.make_async_copy(seg_hbm.at[:, mirror], seg.at[:, mirror], lsem.at[1, i]),
                pltpu.make_async_copy(amp_hbm.at[:, cols], amp.at[:, cols], lsem.at[2, i]),
                pltpu.make_async_copy(amp_hbm.at[:, mirror], amp.at[:, mirror], lsem.at[3, i]),
                pltpu.make_async_copy(ctab_hbm.at[band, :, cols], ctab.at[:, cols], lsem.at[4, i])]

    def start_loads(i, carry):
        for copy in loads(i):
            copy.start()
        return carry
    small = [pltpu.make_async_copy(box_hbm, box_ref, osem.at[0]),
             pltpu.make_async_copy(coef_hbm, coef_ref, osem.at[1]),
             pltpu.make_async_copy(meas_hbm, meas_ref, osem.at[2])]
    small[0].start()
    small[1].start()
    lax.fori_loop(0, CHUNKS, start_loads, 0)
    small[2].start()
    table_copy = pltpu.make_async_copy(rtab_hbm.at[band], rtab, tsem)
    table_copy.start()

    barrier = pltpu.get_barrier_semaphore()

    def greet(where):
        pl.semaphore_signal(barrier, inc=1, device_id=where, device_id_type=MESH)
    each(PEERS, lambda o: greet((band, lax.rem(me + o, PEERS))))
    for o in range(1, YS):
        for c in range(2):
            greet((lax.rem(band + o, YS), chip * 2 + c))

    wave_setup(row0, freq_ref, pamp_ref, roww, colw)
    def send(j, source, target):
        def one(o):
            peer = lax.rem(me + o, PEERS)
            remote(source.at[j, peer], target.at[j, me], ssem.at[j, peer], rsem.at[j, me], (band, peer)).start()
        each(PEERS, one)

    def await_all(j, source, target):
        def one(o):
            peer = lax.rem(me + o, PEERS)
            remote(source.at[j, peer], target.at[j, peer], ssem.at[j, peer], rsem.at[j, peer], (band, peer)).wait()
        each(PEERS, one)

    for j in range(2):
        acc[...] = jnp.zeros_like(acc)
        eb1[...] = jnp.zeros_like(eb1)

        def forward(i, carry):
            if j == 0:
                for copy in loads(i):
                    copy.wait()

                @pl.when(i == 0)
                def _():
                    small[0].wait()
                    small[1].wait()
                    segment_setup(row0, box_ref, coef_ref, seg, flat, tabs, rowt, base, pick)
            before = jnp.maximum(2 * i - 1, 0)
            fields(j, 2 * i, eb0, amp, seg, rowt, base, roww, colw, pbuf, wbuf)
            add_dots(acc, ctab, before, eb1)
            fields(j, 2 * i + 1, eb1, amp, seg, rowt, base, roww, colw, pbuf, wbuf)
            add_dots(acc, ctab, 2 * i, eb0)
            return carry
        lax.fori_loop(0, CHUNKS, forward, 0)
        add_dots(acc, ctab, FOLD // SUB - 1, eb1)
        column_sums(acc, pay.at[j], ysc)
        if j == 0:
            pl.semaphore_wait(barrier, PEERS - 1 + 2 * (YS - 1))
        send(j, pay, recv)
        recv[j, me] = pay[j, me]

    small[2].wait()
    for b in range(2):
        for v in range(OWN):
            source = jnp.where(me < PEERS // 2, v, OWN - 1 - v)
            for k in range(PROBES):
                at = b * 64 + 8 * v + 2 * k
                ms[0, at : at + 2, :] = meas_ref[b, source, k, :, :HALF]
                ms[1, at : at + 2, :] = meas_ref[b, source, k, :, HALF:]
    flip = (iota((128, 128), 0) + iota((128, 128), 1) == 127).astype(F32)
    ms[1] = jnp.dot(ms[1], flip, precision=lax.Precision.HIGHEST, preferred_element_type=F32)
    table_copy.wait()
    for j in range(2):
        await_all(j, pay, recv)
        focal_part(j, normf, recv.at[j], hpay.at[j], lhs, hs, ms, rtab)
        def one(o):
            peer = lax.rem(me + o, PEERS)
            remote(hpay.at[j, peer], hid.at[j, me], ssem.at[2 + j, peer], rsem.at[2 + j, me], (band, peer)).start()
        each(PEERS, one)
        hid[j, me] = hpay[j, me]

    prefix_weights(tris)
    pre1[...] = jnp.zeros_like(pre1)
    for j in range(2):
        def done(o):
            peer = lax.rem(me + o, PEERS)
            remote(hpay.at[j, peer], hid.at[j, peer], ssem.at[2 + j, peer], rsem.at[2 + j, peer],
                   (band, peer)).wait()
        each(PEERS, done)
        hidden_left(j, hid.at[j], left, leftt)

    def back(i, carry):
        backward(i, leftt, ctab, gbuf, wbuf, pbuf, wst)
        return carry
    lax.fori_loop(0, FOLD // BCHUNK, back, 0)

    segment_sums(tabs, wst, pick, ulow, tris, pre0, pre1, sbuf, pack)

    near = band * 2 + core

    def near_copy(o, slot):
        peer = lax.rem(near + o, 2 * YS)
        to = peer // 2
        at = near if slot == "mine" else peer
        return remote(pack.at[to], got_a.at[at], asem.at[0, peer], asem.at[1, at],
                      (to, chip * 2 + lax.rem(peer, 2)))
    each(2 * YS, lambda o: near_copy(o, "mine").start())
    got_a[near] = pack[band]
    each(2 * YS, lambda o: near_copy(o, "peer").wait())
    total = got_a[0]
    for k in range(1, 2 * YS):
        total = total + got_a[k]
    mine_b[...] = total

    def far_copy(o, slot):
        peer = lax.rem(chip + o, CHIPS)
        at = chip if slot == "mine" else peer
        return remote(mine_b, got_b.at[at], bsem.at[0, peer], bsem.at[1, at], (band, peer * 2 + core))
    each(CHIPS, lambda o: far_copy(o, "mine").start())
    got_b[chip] = mine_b[...]
    each(CHIPS, lambda o: far_copy(o, "peer").wait())
    total = got_b[0]
    for k in range(1, CHIPS):
        total = total + got_b[k]
    mine_c[...] = total

    def share_copy(o, slot):
        peer = lax.rem(band + o, YS)
        at = band if slot == "mine" else peer
        return remote(mine_c, got_c.at[at], csem.at[0, peer], csem.at[1, at], (peer, me))
    each(YS, lambda o: share_copy(o, "mine").start())
    got_c[band] = mine_c[...]
    each(YS, lambda o: share_copy(o, "peer").wait())
    for q in range(3):
        for k in range(10):
            p, r = divmod(q * 10 + k, 8)
            width = min(128, SEG - 128 * k)
            out_ref[q : q + 1, 128 * k : 128 * k + width] = got_c[p, r : r + 1, :width]


VM = pl.BlockSpec(memory_space=pltpu.VMEM)
SM = pl.BlockSpec(memory_space=pltpu.SMEM)
HBM = pl.BlockSpec(memory_space=pl.ANY)
LIMIT = 60 * 1024 * 1024


def solution(mesh):
    ctable = jnp.asarray(column_table())
    rtable = jnp.asarray(row_table())
    root = math.sqrt(NR * NC)

    def body(amplitude, seg_map, seg_box, seg_coeffs, probe_freq, probe_amp, measured):
        dma = pltpu.SemaphoreType.DMA
        sums = pl.pallas_call(
            functools.partial(kernel, 1.0 / root),
            in_specs=[HBM, HBM, HBM, HBM, SM, SM, HBM, HBM, HBM],
            out_specs=VM,
            out_shape=jax.ShapeDtypeStruct((3, SEG), F32),
            scratch_shapes=[
                pltpu.VMEM((4, SEG), jnp.int32),
                pltpu.VMEM((3, SEG), F32),
                pltpu.VMEM((2, OWN, PROBES, 2, M), F32),
                pltpu.VMEM((ROWS, NC), BF16),
                pltpu.VMEM((ROWS, NC), jnp.int32),
                pltpu.VMEM((4 * HALF, FOLD), BF16),
                pltpu.VMEM((4 * HALF, NR), BF16),
                pltpu.VMEM((8, 1280), F32),
                pltpu.VMEM((SROWS, 8, 128), F32),
                pltpu.VMEM((3, ROWS, 128), F32),
                pltpu.VMEM((ROWS, 128), jnp.int32),
                pltpu.VMEM((128, 128), BF16),
                pltpu.VMEM((4, ROWS, 128), F32),
                pltpu.VMEM((4, TILES, 128), F32),
                pltpu.VMEM((2, ROWS, NC), F32),
                pltpu.VMEM((4, ROWS, NC), F32),
                pltpu.VMEM((512, SUB), BF16),
                pltpu.VMEM((512, SUB), BF16),
                pltpu.VMEM((4 * HALF, 256), F32),
                pltpu.VMEM((2, 2, HALF, 256), F32),
                pltpu.VMEM((2, PEERS, 16, 256), BF16),
                pltpu.VMEM((2, PEERS, 16, 256), BF16),
                pltpu.VMEM((2, 32, NR), F32),
                pltpu.VMEM((2, 32, NR), F32),
                pltpu.VMEM((2, 128, HALF), F32),
                pltpu.VMEM((2, PEERS, 16, 256), BF16),
                pltpu.VMEM((2, PEERS, 16, 256), BF16),
                pltpu.VMEM((4 * HALF, 256), F32),
                pltpu.VMEM((512, 4 * HALF), BF16),
                pltpu.VMEM((BCHUNK // 256, 2, 512, 256), F32),
                pltpu.VMEM((128, NC), BF16),
                pltpu.VMEM((TILES * 32, 256), BF16),
                pltpu.VMEM((2, 256, 512), BF16),
                pltpu.VMEM((256, 512), F32),
                pltpu.VMEM((256, 512), F32),
                pltpu.VMEM((SROWS, 8, 128), F32),
                pltpu.VMEM((4, 8, 128), F32),
                pltpu.VMEM((2 * YS, 8, 128), F32),
                pltpu.VMEM((8, 128), F32),
                pltpu.VMEM((CHIPS, 8, 128), F32),
                pltpu.VMEM((8, 128), F32),
                pltpu.VMEM((YS, 8, 128), F32),
                dma((5, CHUNKS)),
                dma,
                dma((3,)),
                dma((4, PEERS)),
                dma((4, PEERS)),
                dma((2, 2 * YS)),
                dma((2, CHIPS)),
                dma((2, YS)),
            ],
            compiler_params=pltpu.CompilerParams(collective_id=0, has_side_effects=True, vmem_limit_bytes=LIMIT),
            name="gradient",
        )(amplitude, seg_map, seg_box, seg_coeffs, probe_freq, probe_amp, measured, ctable, rtable)
        return sums * (2.0 / root / (BANDS * PROBES))

    in_specs = (P("row", None), P("row", None), P(), P(), P(), P(), P("band", "row", None, None, None))
    return jax.shard_map(body, mesh=mesh, in_specs=in_specs, out_specs=P(), check_vma=False)
```
